768 devices in a mesh: gx: 8 (over y), gy: 8 (over x, core), gz: 12 (over z).
Axes of the slice: x: 4, y: 8, z: 12, core: 2. Of those that a mesh axis runs over, the one named last changes fastest.
Arguments:
- forcing: float32 [3, 24, 48, 2304], P(None, 'gx', 'gy', 'gz'), may hold values from -6 to 6
- initial_guess: float32 [3, 24, 48, 2304], P(None, 'gx', 'gy', 'gz'), may hold values from -4 to 4
- material: int32 [24, 48, 2304], P('gx', 'gy', 'gz'), may hold values from 0 to 3
- moduli: float32 [2, 4], replicated, may hold values from 0.5 to 4
- support: float32 [24, 48, 2304], P('gx', 'gy', 'gz'), may hold values from 0.05 to 0.5
- offsets: int32 [3], replicated, may hold values from 1 to 2, as said below
- aggregate_class: int32 [8, 16, 768], P('gx', 'gy', 'gz'), may hold values from 0 to 7
- class_blocks: float32 [8, 6, 6], replicated
Outputs:
- displacement: float32 [3, 24, 48, 2304], P(None, 'gx', 'gy', 'gz')
- coarse_correction: float32 [6, 8, 16, 768], P(None, 'gx', 'gy', 'gz')
The draws below stay inside these ranges and needn't reach their ends.
Inputs may be any that keep to these rules, and one draw needn't show every extreme that they name: `offsets`: each entry is 1 or 2, and both values occur.
All inputs are finite; a program needn't handle non-finite values.
Results may differ from the reference program's by a relative error of at most 0.00029.
Values sent between devices are 32-bit elements; how exact they have to be, the bound alone decides.
No kernel may reach another device: no remote copies, remote signals or barrier semaphores. Data moves between devices by JAX's collectives and lax.ppermute only.
A program may use at most 32 MiB of HBM per device.

```python
import math
import jax
import jax.numpy as jnp
from jax import lax

CX = 3
FINE_DEG = 2
COARSE_DEG = 3
MATS = 4
CLASSES = 8
NX = 24
NY = 48
NZ = 2304
NAX = 8
NAY = 16
NAZ = 768


def draw_offsets(key, part):
    key = jax.random.fold_in(key, 11)
    key_third, key_order = jax.random.split(key)
    third = jax.random.randint(key_third, (1,), 1, 3, dtype=jnp.int32)
    values = jnp.concatenate([jnp.array([1, 2], dtype=jnp.int32), third])
    order = jax.random.permutation(key_order, 3)
    return values[order]


def draw_class_blocks(key, part):
    key = jax.random.fold_in(key, 7)
    key_diag, key_couple = jax.random.split(key)
    diagonal = jax.random.uniform(key_diag, (CLASSES, 6), jnp.float32, 2.0, 6.0)
    coupling = jax.random.uniform(key_couple, (CLASSES, 6, 6), jnp.float32, -0.35, 0.35)
    symmetric = 0.5 * (coupling + jnp.swapaxes(coupling, 1, 2))
    identity = jnp.eye(6, dtype=jnp.float32)
    return symmetric * (1.0 - identity) + diagonal[:, :, None] * identity


def set_ends(values, stream_key, least, largest):
    shape = values.shape
    spot = [jax.random.randint(jax.random.fold_in(stream_key, axis), (), 0, shape[axis]) for axis in range(len(shape))]
    values = values.at[tuple(spot)].set(least)
    longest = shape.index(max(shape))
    spot[longest] = (spot[longest] + 1) % shape[longest]
    return values.at[tuple(spot)].set(largest)


def block_scale(own_key, extent, shards, least, largest):
    def one(dim, parts):
        heights = jax.random.uniform(jax.random.fold_in(jax.random.fold_in(own_key, 6), dim), (parts,), jnp.float32, least / len(shards), largest / len(shards))
        return jnp.repeat(jnp.exp(heights), extent[dim] // parts).reshape((-1,) + (1,) * (len(extent) - dim - 1))

    gain = one(*shards[0])
    for cut in shards[1:]:
        gain = gain * one(*cut)
    return gain


def noise(key, extent, deviation, most, cuts=(), held_as=jnp.bfloat16):
    result = deviation * jax.random.normal(key, extent, jnp.float32)
    if cuts:
        result = result * block_scale(key, extent, cuts, -0.22, 0.18)
    return jnp.clip(result, -most, most).astype(held_as)


def setup_inputs(seed: int = 0) -> dict:
    seeds = jax.random.split(jax.random.key(seed), 9)
    return {
        "forcing": noise(seeds[0], (3, NX, NY, NZ), 1.0, 6.0, ((1, 8), (2, 8), (3, 12)), jnp.float32),
        "initial_guess": noise(seeds[1], (3, NX, NY, NZ), 0.5, 4.0, ((1, 8), (2, 8), (3, 12)), jnp.float32),
        "material": set_ends(jax.random.randint(seeds[2], (NX, NY, NZ), 0, MATS), jax.random.fold_in(seeds[2], 1), 0, MATS - 1).astype(jnp.int32),
        "moduli": jnp.clip(jnp.exp(jax.random.uniform(seeds[3], (2, MATS), jnp.float32, math.log(0.5), math.log(4.0))), 0.5, 4.0),
        "support": jnp.clip(jnp.exp(math.log(0.5) - 2.3025851 * jax.random.uniform(seeds[4], (NX, NY, NZ), jnp.float32) ** block_scale(seeds[4], (NX, NY, NZ), ((0, 8), (1, 8), (2, 12)), -0.2, 0.2)), 0.05, 0.5),
        "offsets": draw_offsets(jax.random.fold_in(seeds[8], 71), 0),
        "aggregate_class": set_ends(jax.random.randint(seeds[6], (NAX, NAY, NAZ), 0, CLASSES), jax.random.fold_in(seeds[6], 1), 0, CLASSES - 1).astype(jnp.int32),
        "class_blocks": draw_class_blocks(jax.random.fold_in(seeds[8], 71), 0),
    }


FINE_LOW = 0.25
FINE_HIGH = 2.5
COARSE_LOW = 0.2
COARSE_HIGH = 1.9

def stiffness_tables():
    points = [0.5 - 0.5 / math.sqrt(3.0), 0.5 + 0.5 / math.sqrt(3.0)]
    corner_bits = [(corner // 4, corner // 2 % 2, corner % 2) for corner in range(8)]
    lame_rows = [[0.0 for column in range(24)] for row_idx in range(24)]
    shear_rows = [[0.0 for column in range(24)] for row_idx in range(24)]
    for point_x in points:
        for point_y in points:
            for point_z in points:
                sample = (point_x, point_y, point_z)
                grads = []
                for corner in range(8):
                    bits = corner_bits[corner]
                    factor = [sample[axis_num] if bits[axis_num] else 1.0 - sample[axis_num] for axis_num in range(3)]
                    slopes = [2.0 * bits[axis_num] - 1.0 for axis_num in range(3)]
                    grads.append([slopes[0] * factor[1] * factor[2], factor[0] * slopes[1] * factor[2], factor[0] * factor[1] * slopes[2]])
                for dim_one in range(3):
                    for node_one in range(8):
                        for dim_two in range(3):
                            for node_two in range(8):
                                inner = sum([grads[node_one][axis_num] * grads[node_two][axis_num] for axis_num in range(3)])
                                lame_rows[8 * dim_one + node_one][8 * dim_two + node_two] += 0.125 * grads[node_one][dim_one] * grads[node_two][dim_two]
                                same = inner if dim_one == dim_two else 0.0
                                shear_rows[8 * dim_one + node_one][8 * dim_two + node_two] += 0.125 * (same + grads[node_two][dim_one] * grads[node_one][dim_two])
    coupled = [lame_rows[row_idx] + shear_rows[row_idx] for row_idx in range(24)]
    lame_diag = [[lame_rows[8 * dim_one + node_one][8 * dim_one + node_one] for node_one in range(8)] for dim_one in range(3)]
    shear_diag = [[shear_rows[8 * dim_one + node_one][8 * dim_one + node_one] for node_one in range(8)] for dim_one in range(3)]
    return (jnp.asarray(coupled, dtype=jnp.float32), jnp.asarray(lame_diag, dtype=jnp.float32), jnp.asarray(shear_diag, dtype=jnp.float32))

def element_forces(padded, lame_ext, shear_ext, support, coupled):
    elems_x = padded.shape[1] - 1
    elems_y = padded.shape[2] - 1
    elems_z = padded.shape[3] - 1
    pieces = []
    for corner in range(8):
        move_x, move_y, move_z = (corner // 4, corner // 2 % 2, corner % 2)
        pieces.append(padded[:, move_x:move_x + elems_x, move_y:move_y + elems_y, move_z:move_z + elems_z])
    flat = jnp.stack(pieces, axis=1).reshape(24, -1)
    scaled = jnp.concatenate([flat * lame_ext.reshape(1, -1), flat * shear_ext.reshape(1, -1)], axis=0)
    forces = jnp.dot(coupled, scaled, precision=lax.Precision.HIGHEST, preferred_element_type=jnp.float32)
    forces = forces.reshape(3, 8, elems_x, elems_y, elems_z)
    total = support[None] * padded[:, 1:-1, 1:-1, 1:-1]
    for corner in range(8):
        move_x, move_y, move_z = (corner // 4, corner // 2 % 2, corner % 2)
        total = total + forces[:, corner, 1 - move_x:1 - move_x + elems_x - 1, 1 - move_y:1 - move_y + elems_y - 1, 1 - move_z:1 - move_z + elems_z - 1]
    return total

def diagonal_terms(lame_ext, shear_ext, support, lame_diag, shear_diag):
    nodes_x, nodes_y, nodes_z = support.shape
    total = jnp.broadcast_to(support[None], (3, nodes_x, nodes_y, nodes_z))
    for corner in range(8):
        move_x, move_y, move_z = (corner // 4, corner // 2 % 2, corner % 2)
        lame_slice = lame_ext[1 - move_x:1 - move_x + nodes_x, 1 - move_y:1 - move_y + nodes_y, 1 - move_z:1 - move_z + nodes_z]
        shear_slice = shear_ext[1 - move_x:1 - move_x + nodes_x, 1 - move_y:1 - move_y + nodes_y, 1 - move_z:1 - move_z + nodes_z]
        total = total + lame_diag[:, corner][:, None, None, None] * lame_slice[None] + shear_diag[:, corner][:, None, None, None] * shear_slice[None]
    return total

def invert_blocks(matrices):
    order = matrices.shape[-1]
    identity = jnp.broadcast_to(jnp.eye(order, dtype=matrices.dtype), matrices.shape)
    augmented = jnp.concatenate([matrices, identity], axis=-1)
    for pivot in range(order):
        pivot_row = augmented[:, pivot, :] / augmented[:, pivot, pivot][:, None]
        factors = augmented[:, :, pivot]
        augmented = augmented - factors[:, :, None] * pivot_row[:, None, :]
        augmented = augmented.at[:, pivot, :].set(pivot_row)
    return augmented[:, :, order:]

def restrict_blocks(values):
    size_x, size_y, size_z = (values.shape[1], values.shape[2], values.shape[3])
    grouped = values.reshape(3, size_x // 3, 3, size_y // 3, 3, size_z // 3, 3)
    lever = jnp.arange(3, dtype=values.dtype) - 1.0
    lever_x = lever.reshape(1, 1, 3, 1, 1, 1, 1)
    lever_y = lever.reshape(1, 1, 1, 1, 3, 1, 1)
    lever_z = lever.reshape(1, 1, 1, 1, 1, 1, 3)
    sums = lax.optimization_barrier(jnp.sum(grouped, axis=(2, 4, 6)))
    moment_x = lax.optimization_barrier(jnp.sum(grouped * lever_x, axis=(2, 4, 6)))
    moment_y = lax.optimization_barrier(jnp.sum(grouped * lever_y, axis=(2, 4, 6)))
    moment_z = lax.optimization_barrier(jnp.sum(grouped * lever_z, axis=(2, 4, 6)))
    turn_x = moment_y[2] - moment_z[1]
    turn_y = moment_z[0] - moment_x[2]
    turn_z = moment_x[1] - moment_y[0]
    return jnp.concatenate([sums, jnp.stack([turn_x, turn_y, turn_z])], axis=0)

def prolong_blocks(coarse):
    size_x, size_y, size_z = (coarse.shape[1], coarse.shape[2], coarse.shape[3])
    lever = jnp.arange(3, dtype=coarse.dtype) - 1.0
    lever_x = lever.reshape(3, 1, 1, 1, 1)
    lever_y = lever.reshape(1, 1, 3, 1, 1)
    lever_z = lever.reshape(1, 1, 1, 1, 3)
    spread = coarse[:, :, None, :, None, :, None]
    full = (size_x, 3, size_y, 3, size_z, 3)
    comp_x = spread[0] + spread[4] * lever_z - spread[5] * lever_y
    comp_y = spread[1] + spread[5] * lever_x - spread[3] * lever_z
    comp_z = spread[2] + spread[3] * lever_y - spread[4] * lever_x
    stacked = jnp.stack([jnp.broadcast_to(comp_x, full), jnp.broadcast_to(comp_y, full), jnp.broadcast_to(comp_z, full)])
    return stacked.reshape(3, 3 * size_x, 3 * size_y, 3 * size_z)

def smooth(operator, scale_inverse, current, residual, degree, low_bound, high_bound, keep_residual):
    center = 0.5 * (high_bound + low_bound)
    spread = 0.5 * (high_bound - low_bound)
    center_ratio = center / spread
    weight_now = 1.0 / center_ratio
    update = scale_inverse(residual) / center
    current = current + update
    for repeat in range(1, degree):
        residual = residual - operator(update)
        weight_next = 1.0 / (2.0 * center_ratio - weight_now)
        update = weight_next * weight_now * update + 2.0 * weight_next / spread * scale_inverse(residual)
        current = current + update
        weight_now = weight_next
    if keep_residual:
        residual = residual - operator(update)
    return (current, residual)

def reference(forcing, initial_guess, material, moduli, support, offsets, aggregate_class, class_blocks):
    coupled, lame_diag, shear_diag = stiffness_tables()
    lame_ext = jnp.pad(moduli[0][material], ((1, 0), (1, 0), (1, 0)), mode='wrap')
    shear_ext = jnp.pad(moduli[1][material], ((1, 0), (1, 0), (1, 0)), mode='wrap')
    inverse_diag = 1.0 / diagonal_terms(lame_ext, shear_ext, support, lame_diag, shear_diag)
    slab_count = NX // CX
    starts = jnp.arange(slab_count, dtype=jnp.int32) * CX
    anchor = jnp.zeros((), dtype=jnp.int32)

    def fine_apply(values):
        padded = jnp.pad(values, ((0, 0), (1, 1), (1, 1), (1, 1)), mode='wrap')

        def one_slab(start):
            slab = lax.dynamic_slice(padded, (anchor, start, anchor, anchor), (3, CX + 2, NY + 2, NZ + 2))
            lame_slab = lax.dynamic_slice(lame_ext, (start, anchor, anchor), (CX + 1, NY + 1, NZ + 1))
            shear_slab = lax.dynamic_slice(shear_ext, (start, anchor, anchor), (CX + 1, NY + 1, NZ + 1))
            support_slab = lax.dynamic_slice(support, (start, anchor, anchor), (CX, NY, NZ))
            return element_forces(slab, lame_slab, shear_slab, support_slab, coupled)
        slabs = lax.map(one_slab, starts)
        return jnp.moveaxis(slabs, 0, 1).reshape(3, NX, NY, NZ)

    def fine_scale(values):
        return values * inverse_diag
    blocks = jnp.moveaxis(class_blocks[aggregate_class], (3, 4), (0, 1))
    shifted = class_blocks + 6.0 * jnp.eye(6, dtype=class_blocks.dtype)
    inverse_blocks = jnp.moveaxis(invert_blocks(shifted)[aggregate_class], (3, 4), (0, 1))

    def coarse_apply(values):
        faces = jnp.zeros_like(values)
        for axis_number in (1, 2, 3):
            faces = faces + jnp.roll(values, 1, axis=axis_number) + jnp.roll(values, -1, axis=axis_number)
        return lax.optimization_barrier(jnp.sum(blocks * values[None], axis=1)) + 6.0 * values - faces

    def coarse_scale(values):
        return lax.optimization_barrier(jnp.sum(inverse_blocks * values[None], axis=1))
    residual = forcing - fine_apply(initial_guess)
    current, residual = smooth(fine_apply, fine_scale, initial_guess, residual, FINE_DEG, FINE_LOW, FINE_HIGH, True)
    aligned = jnp.roll(residual, -offsets[0], axis=1)
    aligned = jnp.roll(aligned, -offsets[1], axis=2)
    aligned = jnp.roll(aligned, -offsets[2], axis=3)
    coarse_right = restrict_blocks(aligned)
    correction, unused = smooth(coarse_apply, coarse_scale, jnp.zeros_like(coarse_right), coarse_right, COARSE_DEG, COARSE_LOW, COARSE_HIGH, False)
    expanded = prolong_blocks(correction)
    expanded = jnp.roll(expanded, offsets[0], axis=1)
    expanded = jnp.roll(expanded, offsets[1], axis=2)
    expanded = jnp.roll(expanded, offsets[2], axis=3)
    current = current + expanded
    residual = forcing - fine_apply(current)
    current, residual = smooth(fine_apply, fine_scale, current, residual, FINE_DEG, FINE_LOW, FINE_HIGH, False)
    return (current, correction)
```

```python
import functools

import jax
import jax.numpy as jnp
from jax import lax
from jax.experimental import pallas as pl
from jax.experimental.pallas import tpu as pltpu
from jax.sharding import PartitionSpec as P

FINE_LOW = 0.25
FINE_HIGH = 2.5
COARSE_LOW = 0.2
COARSE_HIGH = 1.9

ROWS = 16
LANES = 256
ROW0 = 5
LANE0 = 16
EDGE = 16
HALO_X = 3
OWN_X, OWN_Y, OWN_Z = 3, 6, 192
FIELDS = 8
SIDE = 8
COARSE_OWN = 64
COARSE_LANES = 70


def chebyshev(low, high, count):
    center = 0.5 * (high + low)
    spread = 0.5 * (high - low)
    ratio = center / spread
    weight = 1.0 / ratio
    steps = []
    for _ in range(1, count):
        following = 1.0 / (2.0 * ratio - weight)
        steps.append((following * weight, 2.0 * following / spread))
        weight = following
    return 1.0 / center, steps


FINE_FIRST, FINE_STEPS = chebyshev(FINE_LOW, FINE_HIGH, 2)
COARSE_FIRST, COARSE_STEPS = chebyshev(COARSE_LOW, COARSE_HIGH, 3)


def turned(value, shift, axis):
    shift = shift % value.shape[axis]
    return value if shift == 0 else pltpu.roll(value, shift, axis)


def following(value, axis):
    return turned(value, -1, axis)


def preceding(value, axis):
    return turned(value, 1, axis)


def plane_modes(value):
    ahead = following(value, 1)
    total, slope = value + ahead, ahead - value
    total_up, slope_up = following(total, 0), following(slope, 0)
    return {
        (0, 0): total + total_up,
        (1, 0): total_up - total,
        (0, 1): slope + slope_up,
        (1, 1): slope_up - slope,
    }


def element_modes(below, above, lame, shear):
    u = []
    for comp in range(3):
        modes = {}
        for key in ((0, 0), (1, 0), (0, 1), (1, 1)):
            first, second = below[comp][key], above[comp][key]
            if key != (0, 0):
                modes[(0,) + key] = first + second
            modes[(1,) + key] = second - first
        u.append(modes)
    x, y, z = u
    third = 1.0 / 3.0
    lame_b, shear_b = lame * third, shear * third
    shear_2 = shear + shear
    last = (lame + (shear_2 + shear_2)) * (1.0 / 9.0)
    f = [{}, {}, {}]
    divergence = lame * (x[1, 0, 0] + y[0, 1, 0] + z[0, 0, 1])
    f[0][1, 0, 0] = divergence + shear_2 * x[1, 0, 0]
    f[1][0, 1, 0] = divergence + shear_2 * y[0, 1, 0]
    f[2][0, 0, 1] = divergence + shear_2 * z[0, 0, 1]
    f[0][0, 1, 0] = f[1][1, 0, 0] = shear * (x[0, 1, 0] + y[1, 0, 0])
    f[0][0, 0, 1] = f[2][1, 0, 0] = shear * (x[0, 0, 1] + z[1, 0, 0])
    f[1][0, 0, 1] = f[2][0, 1, 0] = shear * (y[0, 0, 1] + z[0, 1, 0])
    for one, key_one, two, key_two in (
        (0, (1, 1, 0), 2, (0, 1, 1)),
        (0, (1, 0, 1), 1, (0, 1, 1)),
        (1, (1, 1, 0), 2, (1, 0, 1)),
    ):
        shared = lame_b * (u[one][key_one] + u[two][key_two])
        f[one][key_one] = shared + shear * u[one][key_one]
        f[two][key_two] = shared + shear * u[two][key_two]
    mixed = x[0, 1, 1] + y[1, 0, 1] + z[1, 1, 0]
    f[0][0, 1, 1] = shear_b * (mixed + x[0, 1, 1])
    f[1][1, 0, 1] = shear_b * (mixed + y[1, 0, 1])
    f[2][1, 1, 0] = shear_b * (mixed + z[1, 1, 0])
    for comp in range(3):
        f[comp][1, 1, 1] = last * u[comp][1, 1, 1]
    low, high = [], []
    for comp in range(3):
        down, up = {}, {}
        for key in ((0, 0), (1, 0), (0, 1), (1, 1)):
            slope = f[comp][(1,) + key]
            if key == (0, 0):
                down[key], up[key] = -slope, slope
            else:
                total = f[comp][(0,) + key]
                down[key], up[key] = total - slope, total + slope
        low.append(down)
        high.append(up)
    return low, high


def plane_forces(modes):
    parts = []
    for last in (0, 1):
        total, slope = modes[0, last], modes[1, last]
        parts.append((total - slope) + preceding(total + slope, 0))
    return (parts[0] - parts[1]) + preceding(parts[0] + parts[1], 1)


def stencil(read, elements, first, last, emit):
    below = [plane_modes(read(comp, first)) for comp in range(3)]
    carried = None
    for plane in range(first, last):
        above = [plane_modes(read(comp, plane + 1)) for comp in range(3)]
        low, high = element_modes(below, above, *elements(plane))
        if carried is not None:
            emit(
                plane,
                [
                    plane_forces({key: low[comp][key] + carried[comp][key] for key in low[comp]})
                    for comp in range(3)
                ],
            )
        below, carried = above, high


def tile_row(plane, row, half):
    return ((plane * OWN_Y + row) * 2 + half) * FIELDS


def edges_kernel(guess, forcing, support, material, classes, block, low, high, class_ext):
    def rows(plane):
        for comp in range(3):
            yield comp, guess[comp, plane]
            yield 3 + comp, forcing[comp, plane]
        yield 6, support[plane]
        yield 7, material[plane].astype(jnp.float32)

    block[...] = jnp.zeros_like(block)
    low[...] = jnp.zeros_like(low)
    high[...] = jnp.zeros_like(high)
    class_ext[...] = jnp.zeros_like(class_ext)
    kinds = classes[0].astype(jnp.float32)
    class_ext[0:2, LANE0 : LANE0 + COARSE_OWN] = kinds
    low[0, 0:2, 96:112] = kinds[:, 0:EDGE]
    high[0, 0:2, 96:112] = kinds[:, COARSE_OWN - EDGE :]
    first = 128 - LANE0
    for plane in range(OWN_X):
        for field, value in rows(plane):
            for row in range(OWN_Y):
                line = value[row : row + 1]
                start = tile_row(plane, row, 0) + field
                block[start : start + 1, LANE0:128] = line[:, :first]
                start = tile_row(plane, row, 1) + field
                block[start : start + 1, 0 : OWN_Z - first] = line[:, first:]
                low[plane, field : field + 1, EDGE * row : EDGE * (row + 1)] = line[:, :EDGE]
                high[plane, field : field + 1, EDGE * row : EDGE * (row + 1)] = line[:, -EDGE:]


def widen_kernel(block, low, high, class_ext, wide, class_wide):
    lane = lax.broadcasted_iota(jnp.int32, (8, 128), 1)
    end = LANE0 + OWN_Z - 128
    for plane in range(OWN_X):
        for row in range(OWN_Y):
            start = tile_row(plane, row, 0)
            wide[start : start + 8] = jnp.where(
                lane < LANE0, turned(low[plane], -EDGE * row, 1), block[start : start + 8]
            )
            start = tile_row(plane, row, 1)
            wide[start : start + 8] = jnp.where(
                (lane >= end) & (lane < end + EDGE),
                turned(high[plane], end - EDGE * row, 1),
                block[start : start + 8],
            )
    end = LANE0 + COARSE_OWN
    value = jnp.where(lane < LANE0, turned(low[0], -96, 1), class_ext[...])
    class_wide[...] = jnp.where(
        (lane >= end) & (lane < end + EDGE), turned(high[0], end - 96, 1), value
    )


def pre_kernel(
    moduli, before, own, after, left, right, rest, smoothed, elements, nodes, fields, lame_s, shear_s,
    inverse_s, resid, step_one, step_two,
):
    count = OWN_X + 2 * HALO_X
    for plane in range(count):
        block = (before, own, after)[plane // OWN_X]
        inner = plane % OWN_X
        for field in range(FIELDS):
            if field >= 3 and plane == count - 1 or 3 <= field < 7 and plane == 0:
                continue
            for half in range(2):
                lanes = slice(128 * half, 128 * half + 128)
                start = (plane * 5 * 2 + half) * FIELDS + field
                fields[field, plane, 0:5, lanes] = left[pl.ds(start, 5, stride=16), :]
                fields[field, plane, 11:16, lanes] = right[pl.ds(start, 5, stride=16), :]
                start = tile_row(inner, 0, half) + field
                fields[field, plane, 5:11, lanes] = block[pl.ds(start, 6, stride=16), :]
    carried = None
    for plane in range(count - 1):
        kind = fields[7, plane]
        picked = []
        for which in range(2):
            value = jnp.where(kind < 2.5, moduli[4 * which + 2], moduli[4 * which + 3])
            value = jnp.where(kind < 1.5, moduli[4 * which + 1], value)
            picked.append(jnp.where(kind < 0.5, moduli[4 * which], value) * (1.0 / 16.0))
        lame_s[plane] = picked[0]
        shear_s[plane] = picked[1]
        weight = (picked[0] + 4.0 * picked[1]) * (16.0 / 9.0)
        weight = weight + preceding(weight, 1)
        weight = weight + preceding(weight, 0)
        if carried is not None:
            inverse_s[plane] = 1.0 / (fields[6, plane] + weight + carried)
        carried = weight

    def coefficients(plane):
        return lame_s[plane], shear_s[plane]

    def first_step(plane, forces):
        for comp in range(3):
            value = forces[comp] + fields[6, plane] * fields[comp, plane]
            value = fields[3 + comp, plane] - value
            resid[comp, plane] = value
            step_one[comp, plane] = inverse_s[plane] * value * FINE_FIRST

    def second_step(plane, forces):
        for comp in range(3):
            step = step_one[comp, plane]
            value = resid[comp, plane] - (forces[comp] + fields[6, plane] * step)
            resid[comp, plane] = value
            update = FINE_STEPS[0][0] * step + FINE_STEPS[0][1] * (inverse_s[plane] * value)
            step_two[comp, plane] = update
            if 3 <= plane < 6:
                smoothed[plane - 3, comp] = fields[comp, plane] + step + update

    def last_step(plane, forces):
        for comp in range(3):
            value = forces[comp] + fields[6, plane] * step_two[comp, plane]
            rest[plane - 3, comp] = resid[comp, plane] - value

    stencil(lambda comp, plane: fields[comp, plane], coefficients, 0, 8, first_step)
    stencil(lambda comp, plane: step_one[comp, plane], coefficients, 1, 7, second_step)
    stencil(lambda comp, plane: step_two[comp, plane], coefficients, 2, 6, last_step)
    for plane in range(6):
        elements[0, plane] = lame_s[plane + 1]
        elements[1, plane] = shear_s[plane + 1]
    for plane in range(5):
        nodes[0, plane] = inverse_s[plane + 2]
        nodes[1, plane] = fields[6, plane + 2]


def restrict_kernel(offsets, rest, class_wide, chunk):
    shift_x, shift_y, shift_z = offsets[0], offsets[1], offsets[2]
    planes = [[rest[shift_x + 1 + step, comp] for comp in range(3)] for step in range(3)]
    total = [planes[0][comp] + planes[1][comp] + planes[2][comp] for comp in range(3)]
    moment = [planes[2][comp] - planes[0][comp] for comp in range(3)]
    row = lax.broadcasted_iota(jnp.int32, (ROWS, LANES), 0)
    plain = jnp.zeros((ROWS, LANES), jnp.float32)
    lever = jnp.zeros((ROWS, LANES), jnp.float32)
    for half in range(2):
        place = row - (ROW0 + 3 * half) - shift_y
        inside = (place >= 0) & (place < 3)
        arm = (place - 1).astype(jnp.float32)

        def summed(value):
            return jnp.sum(jnp.where(inside, value, 0.0), axis=0, keepdims=True)

        sums = [summed(total[comp]) for comp in range(3)]
        lines = sums + [
            summed(arm * total[2]),
            summed(-moment[2]),
            summed(moment[1] - arm * total[0]),
        ]
        for comp in range(6):
            plain = jnp.where(row == 8 * half + comp, lines[comp], plain)
        lever = jnp.where(row == 8 * half + 3, -sums[1], lever)
        lever = jnp.where(row == 8 * half + 4, sums[0], lever)
    fine = lax.broadcasted_iota(jnp.int32, (LANES, 128), 0)
    coarse = lax.broadcasted_iota(jnp.int32, (LANES, 128), 1)
    place = fine - 3 * coarse + 2 * shift_z - 10
    inside = (place >= 0) & (place < 3) & (coarse < COARSE_LANES)
    sums_z = jnp.where(inside, 1.0, 0.0)
    arms_z = jnp.where(inside, (place - 1).astype(jnp.float32), 0.0)
    dot = functools.partial(
        jnp.dot, precision=lax.Precision.HIGHEST, preferred_element_type=jnp.float32
    )
    result = dot(plain, sums_z) + dot(lever, arms_z)
    kinds = pltpu.roll(class_wide[...], shift_z + (128 - 14), 1)
    line = lax.broadcasted_iota(jnp.int32, (8, 128), 0)
    lane = lax.broadcasted_iota(jnp.int32, (8, 128), 1)
    low = jnp.where(line == 6, kinds[0:1], result[0:8])
    high = jnp.where(line == 6, kinds[1:2], result[8:16])
    packed = jnp.where(lane < 64, turned(low, -3, 1), turned(high, 61, 1))
    ends = jnp.zeros((1, 128), jnp.float32)
    lane_one = lane[0:1]
    for half in range(2):
        for comp in range(7):
            base = 12 * comp + 6 * half
            source = (low, high)[half][comp : comp + 1]
            ends = jnp.where(
                (lane_one >= base) & (lane_one < base + 3), turned(source, base, 1), ends
            )
            ends = jnp.where(
                (lane_one >= base + 3) & (lane_one < base + 6), turned(source, base - 64, 1), ends
            )
    packed = jnp.where(line == 7, ends, packed)
    for target in range(SIDE * SIDE):
        chunk[target] = packed


def coarse_kernel(
    offsets, place, tables, received, rest, smoothed, elements, nodes, displacement, correction, right,
    matrix, step_a, step_b, error, spread_y, spread_z, work, step, resid,
):
    shift_x, shift_y, shift_z = offsets[0], offsets[1], offsets[2]
    mine_x, mine_y = place[0], place[1]
    lane = lax.broadcasted_iota(jnp.int32, (8, 128), 1)
    middle = (lane >= 3) & (lane < 67)
    for at_x in range(SIDE):
        ends = received[pl.ds(64 * at_x + 7, 8, stride=8), :]
        for comp in range(7):
            main = received[pl.ds(64 * at_x + comp, 8, stride=8), :]
            for half in range(2):
                base = 12 * comp + 6 * half
                value = jnp.where(lane < 3, turned(ends, -base, 1), turned(ends, 64 - base, 1))
                value = jnp.where(middle, turned(main, 67 if half else 3, 1), value)
                right[comp, 8 * half + at_x] = jnp.where(lane < COARSE_LANES, value, 0.0)

    def fill(entry, unused):
        t = [tables[8 * entry + which] for which in range(8)]
        for spot in range(16):
            kind = right[6, spot]
            value = jnp.full((8, 128), t[7])
            for which in range(6, -1, -1):
                value = jnp.where(kind < which + 0.5, t[which], value)
            matrix[entry, spot] = value
        return unused

    lax.fori_loop(0, 72, fill, 0)

    def product(base, values, spot):
        result = []
        for i in range(6):
            total = matrix[base + 6 * i, spot] * values[0]
            for j in range(1, 6):
                total = total + matrix[base + 6 * i + j, spot] * values[j]
            result.append(total)
        return result

    def coarse_step(source, target, first, scale_old, scale_new):
        def body(at_x, unused):
            above = lax.rem(at_x + 1, SIDE)
            below = lax.rem(at_x + SIDE - 1, SIDE)
            for half in range(2):
                spot = 8 * half + at_x
                remains = [right[comp, spot] for comp in range(6)]
                if first:
                    update = [COARSE_FIRST * v for v in product(36, remains, spot)]
                    for comp in range(6):
                        target[comp, spot] = update[comp]
                        error[comp, spot] = update[comp]
                    continue
                old = [source[comp, spot] for comp in range(6)]
                applied = product(0, old, spot)
                for comp in range(6):
                    other = source[comp, 8 * (1 - half) + at_x]
                    faces = source[comp, 8 * half + above] + source[comp, 8 * half + below]
                    faces = faces + other + turned(other, 1 if half == 0 else -1, 0)
                    faces = faces + turned(old[comp], 1, 1) + turned(old[comp], -1, 1)
                    remains[comp] = remains[comp] - (applied[comp] + 6.0 * old[comp] - faces)
                    right[comp, spot] = remains[comp]
                fresh = product(36, remains, spot)
                for comp in range(6):
                    update = scale_old * old[comp] + scale_new * fresh[comp]
                    target[comp, spot] = update
                    error[comp, spot] = error[comp, spot] + update
            return unused

        lax.fori_loop(0, SIDE, body, 0)

    coarse_step(None, step_a, True, 0.0, 0.0)
    coarse_step(step_a, step_b, False, *COARSE_STEPS[0])
    coarse_step(step_b, step_a, False, *COARSE_STEPS[1])

    for half in range(2):
        for comp in range(6):
            line = error[comp, 8 * half + mine_x, pl.ds(mine_y, 1), :]
            line = pltpu.roll(jnp.broadcast_to(line, (8, 128)), 126 - shift_z, 1)
            correction[comp, 0, half : half + 1, :] = line[0:1, :COARSE_OWN]

    row = lax.broadcasted_iota(jnp.int32, (ROWS, 128), 0)
    for near_x in range(3):
        at_x = lax.rem(mine_x - shift_x + near_x + SIDE, SIDE)
        for comp in range(6):
            value = jnp.zeros((ROWS, 128), jnp.float32)
            for near_y in range(4):
                at_y = lax.rem(2 * mine_y - shift_y + near_y + 2 * SIDE, 2 * SIDE)
                spot = 8 * lax.rem(at_y, 2) + at_x
                line = error[comp, spot, pl.ds(lax.div(at_y, 2), 1), :]
                inner = row - ROW0 - shift_y - 3 * (near_y - shift_y)
                value = jnp.where((inner >= 0) & (inner < 3), line, value)
            start = (comp * 3 + near_x) * ROWS
            spread_y[start : start + ROWS] = value
    coarse = lax.broadcasted_iota(jnp.int32, (128, LANES), 0)
    fine = lax.broadcasted_iota(jnp.int32, (128, LANES), 1)
    inner = fine - 3 * coarse + 2 * shift_z - 10
    copies = jnp.where((inner >= 0) & (inner < 3), 1.0, 0.0)
    wide = jnp.dot(
        spread_y[...], copies, precision=lax.Precision.HIGHEST, preferred_element_type=jnp.float32
    )
    for which in range(18):
        spread_z[which] = wide[which * ROWS : (which + 1) * ROWS]

    row = lax.broadcasted_iota(jnp.int32, (ROWS, LANES), 0)
    fine = lax.broadcasted_iota(jnp.int32, (ROWS, LANES), 1)
    arm_y = (lax.rem(row + 4 - shift_y, 3) - 1).astype(jnp.float32)
    arm_z = (lax.rem(fine + 2 * shift_z + 2, 3) - 1).astype(jnp.float32)
    for plane in range(7):
        ahead = plane - 2 - shift_x + 6
        near_x = lax.div(ahead, 3) - 2 + shift_x
        arm_x = (lax.rem(ahead, 3) - 1).astype(jnp.float32)
        e = [spread_z[comp * 3 + near_x] for comp in range(6)]
        work[0, plane] = e[0] + e[4] * arm_z - e[5] * arm_y
        work[1, plane] = e[1] + e[5] * arm_x - e[3] * arm_z
        work[2, plane] = e[2] + e[3] * arm_y - e[4] * arm_x

    def first_step(plane, forces):
        at = plane - 1
        for comp in range(3):
            value = forces[comp] + nodes[1, at] * work[comp, plane]
            value = rest[at, comp] - value
            resid[comp, at] = value
            step[comp, at] = nodes[0, at] * value * FINE_FIRST

    def last_step(plane, forces):
        for comp in range(3):
            old = step[comp, plane]
            value = resid[comp, plane] - (forces[comp] + nodes[1, plane] * old)
            update = FINE_STEPS[0][0] * old + FINE_STEPS[0][1] * (nodes[0, plane] * value)
            value = smoothed[plane - 1, comp] + work[comp, plane + 1] + old + update
            displacement[comp, plane - 1] = value[
                ROW0 : ROW0 + OWN_Y, LANE0 : LANE0 + OWN_Z
            ]

    stencil(
        lambda comp, plane: work[comp, plane],
        lambda plane: (elements[0, plane], elements[1, plane]),
        0,
        6,
        first_step,
    )
    stencil(
        lambda comp, plane: step[comp, plane],
        lambda plane: (elements[0, plane + 1], elements[1, plane + 1]),
        0,
        4,
        last_step,
    )


def invert_blocks(matrices):
    order = matrices.shape[-1]
    identity = jnp.broadcast_to(jnp.eye(order, dtype=matrices.dtype), matrices.shape)
    augmented = jnp.concatenate([matrices, identity], axis=-1)
    for pivot in range(order):
        pivot_row = augmented[:, pivot, :] / augmented[:, pivot, pivot][:, None]
        factors = augmented[:, :, pivot]
        augmented = augmented - factors[:, :, None] * pivot_row[:, None, :]
        augmented = augmented.at[:, pivot, :].set(pivot_row)
    return augmented[:, :, order:]


def passed_along(value, axis, steps):
    count = lax.axis_size(axis)
    pairs = [(source, (source + steps) % count) for source in range(count)]
    return lax.ppermute(value, axis, pairs)


VMEM = pl.BlockSpec(memory_space=pltpu.VMEM)
SMEM = pl.BlockSpec(memory_space=pltpu.SMEM)
INTERPRET = False


def call(kernel, scalars, vectors, shapes, scratch=()):
    return pl.pallas_call(
        kernel,
        out_shape=[jax.ShapeDtypeStruct(shape, jnp.float32) for shape in shapes],
        in_specs=[SMEM] * len(scalars) + [VMEM] * len(vectors),
        out_specs=[VMEM] * len(shapes),
        scratch_shapes=[pltpu.VMEM(shape, jnp.float32) for shape in scratch],
        compiler_params=pltpu.CompilerParams(vmem_limit_bytes=48 * 1024 * 1024),
        interpret=INTERPRET,
    )(*scalars, *vectors)


def pack_edges(initial_guess, forcing, support, material, aggregate_class):
    return call(
        edges_kernel,
        (),
        (initial_guess, forcing, support, material, aggregate_class),
        [(OWN_X * OWN_Y * 2 * FIELDS, 128), (3, 8, 128), (3, 8, 128), (8, 128)],
    )


def widen(block, low, high, class_ext):
    return call(
        widen_kernel,
        (),
        (block, low, high, class_ext),
        [(OWN_X * OWN_Y * 2 * FIELDS, 128), (8, 128)],
    )


def pre_smooth(moduli, before, own, after, left, right):
    plane = (ROWS, LANES)
    return call(
        pre_kernel,
        (moduli.reshape(-1),),
        (before, own, after, left, right),
        [(3, 3) + plane, (3, 3) + plane, (2, 6) + plane, (2, 5) + plane],
        [(8, 9) + plane, (8,) + plane, (8,) + plane, (8,) + plane]
        + [(3, 9) + plane, (3, 9) + plane, (3, 9) + plane],
    )


def restrict(offsets, rest, class_wide):
    return call(restrict_kernel, (offsets,), (rest, class_wide), [(SIDE * SIDE, 8, 128)])[0]


def coarse_and_post(offsets, place, tables, received, rest, smoothed, elements, nodes):
    plane = (ROWS, LANES)
    spots = (16, 8, 128)
    return call(
        coarse_kernel,
        (offsets, place, tables),
        (received, rest, smoothed, elements, nodes),
        [(3, OWN_X, OWN_Y, OWN_Z), (6, 1, 2, COARSE_OWN)],
        [(7,) + spots, (72,) + spots, (6,) + spots, (6,) + spots, (6,) + spots]
        + [(18 * ROWS, 128), (18,) + plane, (3, 7) + plane, (3, 5) + plane, (3, 5) + plane],
    )


def coarse_tables(class_blocks):
    shifted = class_blocks + 6.0 * jnp.eye(6, dtype=jnp.float32)
    both = jnp.stack([class_blocks, invert_blocks(shifted)])
    return jnp.transpose(both.reshape(2, 8, 36), (0, 2, 1)).reshape(-1)


def body(forcing, initial_guess, material, moduli, support, offsets, aggregate_class, class_blocks):
    tables = coarse_tables(class_blocks)
    place = jnp.stack([lax.axis_index("gx"), lax.axis_index("gy")]).astype(jnp.int32)
    block, low, high, class_ext = pack_edges(
        initial_guess, forcing, support, material, aggregate_class
    )
    from_low = passed_along(high, "gz", 1)
    from_high = passed_along(low, "gz", -1)
    own, class_wide = widen(block, from_low, from_high, class_ext)
    before = passed_along(own, "gx", 1)
    after = passed_along(own, "gx", -1)
    planes = jnp.concatenate([before, own, after], axis=0)
    planes = planes.reshape(9, OWN_Y, 2 * FIELDS, 128)
    left = passed_along(planes[:, 1:], "gy", 1).reshape(-1, 128)
    right = passed_along(planes[:, :5], "gy", -1).reshape(-1, 128)
    rest, smoothed, elements, nodes = pre_smooth(moduli, before, own, after, left, right)
    rest_low = passed_along(rest[2:], "gx", 1)
    rest_high = passed_along(rest[:2], "gx", -1)
    rest = jnp.concatenate([rest_low, rest, rest_high], axis=0)
    chunk = restrict(offsets, rest, class_wide)
    received = lax.all_to_all(chunk, ("gx", "gy"), 0, 0, tiled=True).reshape(-1, 128)
    displacement, correction = coarse_and_post(
        offsets, place, tables, received, rest, smoothed, elements, nodes
    )
    return displacement, correction


def solution(mesh):
    placed = (
        P(None, "gx", "gy", "gz"),
        P(None, "gx", "gy", "gz"),
        P("gx", "gy", "gz"),
        P(),
        P("gx", "gy", "gz"),
        P(),
        P("gx", "gy", "gz"),
        P(),
    )
    return jax.shard_map(
        body,
        mesh=mesh,
        in_specs=placed,
        out_specs=(P(None, "gx", "gy", "gz"), P(None, "gx", "gy", "gz")),
        check_vma=False,
    )
```

```python
import functools

import jax
import jax.numpy as jnp
from jax import lax
from jax.experimental import pallas as pl
from jax.experimental.pallas import tpu as pltpu
from jax.sharding import PartitionSpec as P

FINE_LOW = 0.25
FINE_HIGH = 2.5
COARSE_LOW = 0.2
COARSE_HIGH = 1.9

ROWS = 16
LANES = 256
ROW0 = 5
LANE0 = 16
EDGE = 16
SENT = slice(4, 12)
PLANES = 10
OWN_X, OWN_Y, OWN_Z = 3, 6, 192
FIELDS = 8
SIDE = 8
COARSE_OWN = 64
COARSE_LANES = 70


def chebyshev(low, high, count):
    center = 0.5 * (high + low)
    spread = 0.5 * (high - low)
    ratio = center / spread
    weight = 1.0 / ratio
    steps = []
    for _ in range(1, count):
        following = 1.0 / (2.0 * ratio - weight)
        steps.append((following * weight, 2.0 * following / spread))
        weight = following
    return 1.0 / center, steps


FINE_FIRST, FINE_STEPS = chebyshev(FINE_LOW, FINE_HIGH, 2)
COARSE_FIRST, COARSE_STEPS = chebyshev(COARSE_LOW, COARSE_HIGH, 3)


def turned(value, shift, axis):
    shift = shift % value.shape[axis]
    return value if shift == 0 else pltpu.roll(value, shift, axis)


def following(value, axis):
    return turned(value, -1, axis)


def preceding(value, axis):
    return turned(value, 1, axis)


def plane_modes(value):
    ahead = following(value, 1)
    total, slope = value + ahead, ahead - value
    total_up, slope_up = following(total, 0), following(slope, 0)
    return {
        (0, 0): total + total_up,
        (1, 0): total_up - total,
        (0, 1): slope + slope_up,
        (1, 1): slope_up - slope,
    }


def element_modes(below, above, lame, shear):
    u = []
    for comp in range(3):
        modes = {}
        for key in ((0, 0), (1, 0), (0, 1), (1, 1)):
            first, second = below[comp][key], above[comp][key]
            if key != (0, 0):
                modes[(0,) + key] = first + second
            modes[(1,) + key] = second - first
        u.append(modes)
    x, y, z = u
    third = 1.0 / 3.0
    lame_b, shear_b = lame * third, shear * third
    shear_2 = shear + shear
    last = (lame + (shear_2 + shear_2)) * (1.0 / 9.0)
    f = [{}, {}, {}]
    divergence = lame * (x[1, 0, 0] + y[0, 1, 0] + z[0, 0, 1])
    f[0][1, 0, 0] = divergence + shear_2 * x[1, 0, 0]
    f[1][0, 1, 0] = divergence + shear_2 * y[0, 1, 0]
    f[2][0, 0, 1] = divergence + shear_2 * z[0, 0, 1]
    f[0][0, 1, 0] = f[1][1, 0, 0] = shear * (x[0, 1, 0] + y[1, 0, 0])
    f[0][0, 0, 1] = f[2][1, 0, 0] = shear * (x[0, 0, 1] + z[1, 0, 0])
    f[1][0, 0, 1] = f[2][0, 1, 0] = shear * (y[0, 0, 1] + z[0, 1, 0])
    for one, key_one, two, key_two in (
        (0, (1, 1, 0), 2, (0, 1, 1)),
        (0, (1, 0, 1), 1, (0, 1, 1)),
        (1, (1, 1, 0), 2, (1, 0, 1)),
    ):
        shared = lame_b * (u[one][key_one] + u[two][key_two])
        f[one][key_one] = shared + shear * u[one][key_one]
        f[two][key_two] = shared + shear * u[two][key_two]
    mixed = x[0, 1, 1] + y[1, 0, 1] + z[1, 1, 0]
    f[0][0, 1, 1] = shear_b * (mixed + x[0, 1, 1])
    f[1][1, 0, 1] = shear_b * (mixed + y[1, 0, 1])
    f[2][1, 1, 0] = shear_b * (mixed + z[1, 1, 0])
    for comp in range(3):
        f[comp][1, 1, 1] = last * u[comp][1, 1, 1]
    low, high = [], []
    for comp in range(3):
        down, up = {}, {}
        for key in ((0, 0), (1, 0), (0, 1), (1, 1)):
            slope = f[comp][(1,) + key]
            if key == (0, 0):
                down[key], up[key] = -slope, slope
            else:
                total = f[comp][(0,) + key]
                down[key], up[key] = total - slope, total + slope
        low.append(down)
        high.append(up)
    return low, high


def plane_forces(modes):
    parts = []
    for last in (0, 1):
        total, slope = modes[0, last], modes[1, last]
        parts.append((total - slope) + preceding(total + slope, 0))
    return (parts[0] - parts[1]) + preceding(parts[0] + parts[1], 1)


def stencil(read, elements, first, last, emit):
    below = [plane_modes(read(comp, first)) for comp in range(3)]
    carried = None
    for plane in range(first, last):
        above = [plane_modes(read(comp, plane + 1)) for comp in range(3)]
        low, high = element_modes(below, above, *elements(plane))
        if carried is not None:
            emit(
                plane,
                [
                    plane_forces({key: low[comp][key] + carried[comp][key] for key in low[comp]})
                    for comp in range(3)
                ],
            )
        below, carried = above, high


def tile_row(plane, row, half):
    return ((plane * OWN_Y + row) * 2 + half) * FIELDS


def field_planes(guess, forcing, support, material, plane):
    for comp in range(3):
        yield comp, guess[comp, plane]
        yield 3 + comp, forcing[comp, plane]
    yield 6, support[plane]
    yield 7, material[plane].astype(jnp.float32)


def edges_kernel(
    guess_h, forcing_h, support_h, material_h, classes_h, low, high, guess, forcing, support, material,
    classes, done,
):
    pairs = (
        (guess_h, guess),
        (forcing_h, forcing),
        (support_h, support),
        (material_h, material),
        (classes_h, classes),
    )
    copies = [
        pltpu.make_async_copy(source, target, done.at[which])
        for which, (source, target) in enumerate(pairs)
    ]
    for copy in copies:
        copy.start()
    low[...] = jnp.zeros_like(low)
    high[...] = jnp.zeros_like(high)
    for copy in copies:
        copy.wait()
    kinds = classes[0].astype(jnp.float32)
    low[0, 0:2, 96:112] = kinds[:, 0:EDGE]
    high[0, 0:2, 96:112] = kinds[:, COARSE_OWN - EDGE :]
    for plane in range(OWN_X):
        for field, value in field_planes(guess, forcing, support, material, plane):
            for row in range(OWN_Y):
                line = value[row : row + 1]
                low[plane, field : field + 1, EDGE * row : EDGE * (row + 1)] = line[:, :EDGE]
                high[plane, field : field + 1, EDGE * row : EDGE * (row + 1)] = line[:, -EDGE:]


def pack_kernel(guess, forcing, support, material, classes, block, class_ext):
    first = 128 - LANE0
    block[...] = jnp.zeros_like(block)
    class_ext[...] = jnp.zeros_like(class_ext)
    class_ext[0:2, LANE0 : LANE0 + COARSE_OWN] = classes[0].astype(jnp.float32)
    for plane in range(OWN_X):
        for field, value in field_planes(guess, forcing, support, material, plane):
            for row in range(OWN_Y):
                line = value[row : row + 1]
                start = tile_row(plane, row, 0) + field
                block[start : start + 1, LANE0:128] = line[:, :first]
                start = tile_row(plane, row, 1) + field
                block[start : start + 1, 0 : OWN_Z - first] = line[:, first:]


def widen_kernel(block, low, high, class_ext, wide, class_wide):
    lane = lax.broadcasted_iota(jnp.int32, (8, 128), 1)
    end = LANE0 + OWN_Z - 128
    for plane in range(OWN_X):
        for row in range(OWN_Y):
            start = tile_row(plane, row, 0)
            wide[start : start + 8] = jnp.where(
                lane < LANE0, turned(low[plane], -EDGE * row, 1), block[start : start + 8]
            )
            start = tile_row(plane, row, 1)
            wide[start : start + 8] = jnp.where(
                (lane >= end) & (lane < end + EDGE),
                turned(high[plane], end - EDGE * row, 1),
                block[start : start + 8],
            )
    end = LANE0 + COARSE_OWN
    value = jnp.where(lane < LANE0, turned(low[0], -96, 1), class_ext[...])
    class_wide[...] = jnp.where(
        (lane >= end) & (lane < end + EDGE), turned(high[0], end - 96, 1), value
    )


def pre_kernel(
    moduli, scalars, planes, left, right, class_wide, chunk, remains, carry, smoothed, elements, nodes,
    fields, lame_s, shear_s, inverse_s, resid, step_one, step_two, sums_s,
):
    for plane in range(PLANES):
        for field in range(FIELDS):
            for half in range(2):
                lanes = slice(128 * half, 128 * half + 128)
                start = (plane * 5 * 2 + half) * FIELDS + field
                fields[field, plane, 0:5, lanes] = left[pl.ds(start, 5, stride=16), :]
                fields[field, plane, 11:16, lanes] = right[pl.ds(start, 5, stride=16), :]
                start = tile_row(plane, 0, half) + field
                fields[field, plane, 5:11, lanes] = planes[pl.ds(start, 6, stride=16), :]
    carried = None
    for plane in range(PLANES - 1):
        kind = fields[7, plane]
        picked = []
        for which in range(2):
            value = jnp.where(kind < 2.5, moduli[4 * which + 2], moduli[4 * which + 3])
            value = jnp.where(kind < 1.5, moduli[4 * which + 1], value)
            picked.append(jnp.where(kind < 0.5, moduli[4 * which], value) * (1.0 / 16.0))
        lame_s[plane] = picked[0]
        shear_s[plane] = picked[1]
        weight = (picked[0] + 4.0 * picked[1]) * (16.0 / 9.0)
        weight = weight + preceding(weight, 1)
        weight = weight + preceding(weight, 0)
        if carried is not None:
            inverse_s[plane] = 1.0 / (fields[6, plane] + weight + carried)
        carried = weight
    for plane in range(6):
        elements[0, plane] = lame_s[plane]
        elements[1, plane] = shear_s[plane]
    for plane in range(5):
        nodes[0, plane] = inverse_s[plane + 1]
        nodes[1, plane] = fields[6, plane + 1]

    shift_x, shift_y, shift_z = scalars[0], scalars[1], scalars[2]
    base = shift_x - 1

    def coefficients(plane):
        return lame_s[base + plane], shear_s[base + plane]

    def first_step(plane, forces):
        at = base + plane
        support, inverse = fields[6, at], inverse_s[at]
        for comp in range(3):
            value = forces[comp] + support * fields[comp, at]
            value = fields[3 + comp, at] - value
            resid[comp, plane] = value
            step_one[comp, plane] = inverse * value * FINE_FIRST

    def second_step(plane, forces):
        at = base + plane
        support, inverse = fields[6, at], inverse_s[at]
        for comp in range(3):
            step = step_one[comp, plane]
            value = resid[comp, plane] - (forces[comp] + support * step)
            resid[comp, plane] = value
            update = FINE_STEPS[0][0] * step + FINE_STEPS[0][1] * (inverse * value)
            step_two[comp, plane] = update
            sums_s[plane - 2, comp] = fields[comp, at] + step + update

    def last_step(plane, forces):
        support = fields[6, base + plane]
        for comp in range(3):
            value = forces[comp] + support * step_two[comp, plane]
            value = resid[comp, plane] - value
            remains[plane - 3, comp] = value
            carry[plane - 3, comp] = value[SENT]

    stencil(lambda comp, plane: fields[comp, base + plane], coefficients, 0, 8, first_step)
    stencil(lambda comp, plane: step_one[comp, plane], coefficients, 1, 7, second_step)
    stencil(lambda comp, plane: step_two[comp, plane], coefficients, 2, 6, last_step)
    for comp in range(3):
        smoothed[0, comp] = sums_s[0, comp]
        smoothed[1, comp] = sums_s[2 - shift_x, comp]
        smoothed[2, comp] = sums_s[3 - shift_x, comp]
        carry[3, comp] = sums_s[4 - shift_x, comp][SENT]

    total = [remains[0, comp] + remains[1, comp] + remains[2, comp] for comp in range(3)]
    moment = [remains[2, comp] - remains[0, comp] for comp in range(3)]
    row = lax.broadcasted_iota(jnp.int32, (ROWS, LANES), 0)
    plain = jnp.zeros((ROWS, LANES), jnp.float32)
    lever = jnp.zeros((ROWS, LANES), jnp.float32)
    for half in range(2):
        place = row - (ROW0 + 3 * half) - shift_y
        inside = (place >= 0) & (place < 3)
        arm = (place - 1).astype(jnp.float32)

        def summed(value):
            return jnp.sum(jnp.where(inside, value, 0.0), axis=0, keepdims=True)

        sums = [summed(total[comp]) for comp in range(3)]
        lines = sums + [
            summed(arm * total[2]),
            summed(-moment[2]),
            summed(moment[1] - arm * total[0]),
        ]
        for comp in range(6):
            plain = jnp.where(row == 8 * half + comp, lines[comp], plain)
        lever = jnp.where(row == 8 * half + 3, -sums[1], lever)
        lever = jnp.where(row == 8 * half + 4, sums[0], lever)
    fine = lax.broadcasted_iota(jnp.int32, (LANES, 128), 0)
    coarse = lax.broadcasted_iota(jnp.int32, (LANES, 128), 1)
    place = fine - 3 * coarse + 2 * shift_z - 10
    inside = (place >= 0) & (place < 3) & (coarse < COARSE_LANES)
    sums_z = jnp.where(inside, 1.0, 0.0)
    arms_z = jnp.where(inside, (place - 1).astype(jnp.float32), 0.0)
    dot = functools.partial(
        jnp.dot, precision=lax.Precision.HIGHEST, preferred_element_type=jnp.float32
    )
    result = dot(plain, sums_z) + dot(lever, arms_z)
    kinds = pltpu.roll(class_wide[...], shift_z + (128 - 14), 1)
    line = lax.broadcasted_iota(jnp.int32, (8, 128), 0)
    lane = lax.broadcasted_iota(jnp.int32, (8, 128), 1)
    low = jnp.where(line == 6, kinds[0:1], result[0:8])
    high = jnp.where(line == 6, kinds[1:2], result[8:16])
    packed = jnp.where(lane < 64, turned(low, -3, 1), turned(high, 61, 1))
    ends = jnp.zeros((1, 128), jnp.float32)
    lane_one = lane[0:1]
    for half in range(2):
        for comp in range(7):
            base = 12 * comp + 6 * half
            source = (low, high)[half][comp : comp + 1]
            ends = jnp.where(
                (lane_one >= base) & (lane_one < base + 3), turned(source, base, 1), ends
            )
            ends = jnp.where(
                (lane_one >= base + 3) & (lane_one < base + 6), turned(source, base - 64, 1), ends
            )
    packed = jnp.where(line == 7, ends, packed)
    for target in range(SIDE * SIDE):
        chunk[target] = packed


def coarse_kernel(
    scalars, tables, received, rest, low, smoothed, elements, nodes, displacement, correction, right,
    matrix, step_a, step_b, error, spread_y, spread_z, work, step, resid, near,
):
    shift_x, shift_y, shift_z = scalars[0], scalars[1], scalars[2]
    mine_x, mine_y = scalars[3], scalars[4]
    lane = lax.broadcasted_iota(jnp.int32, (8, 128), 1)
    line = lax.broadcasted_iota(jnp.int32, (8, 128), 0)
    even = line < 4
    middle = (lane >= 3) & (lane < 67)
    odd_shift = lax.rem(shift_y, 2)
    turn_even = lax.rem(SIDE + 2 - mine_y, SIDE)
    turn_odd = lax.rem(SIDE + 6 - mine_y - odd_shift, SIDE)
    for at_x in range(SIDE):
        ends = received[pl.ds(64 * at_x + 7, 8, stride=8), :]
        ends = [pltpu.roll(ends, turn_even, 0), pltpu.roll(ends, turn_odd, 0)]
        for comp in range(7):
            main = received[pl.ds(64 * at_x + comp, 8, stride=8), :]
            main = [pltpu.roll(main, turn_even, 0), pltpu.roll(main, turn_odd, 0)]
            parts = []
            for which in range(2):
                half = odd_shift if which == 0 else 1 - odd_shift
                base = 12 * comp + 6 * half
                low_end = pltpu.roll(ends[which], lax.rem(128 - base, 128), 1)
                high_end = pltpu.roll(ends[which], lax.rem(192 - base, 128), 1)
                value = jnp.where(lane < 3, low_end, high_end)
                parts.append(jnp.where(middle, pltpu.roll(main[which], 3 + 64 * half, 1), value))
            value = jnp.where(even, parts[0], parts[1])
            right[comp, at_x] = jnp.where(lane < COARSE_LANES, value, 0.0)

    kinds = [right[6, spot].astype(jnp.int32) for spot in range(SIDE)]
    for entry in range(72):
        values = jnp.broadcast_to(tables[entry : entry + 1], (8, 128))
        for spot in range(SIDE):
            matrix[entry, spot] = jnp.take_along_axis(
                values, kinds[spot], axis=1, mode="promise_in_bounds"
            )

    def product(base, values, spot):
        result = []
        for i in range(6):
            total = matrix[base + 6 * i, spot] * values[0]
            for j in range(1, 6):
                total = total + matrix[base + 6 * i + j, spot] * values[j]
            result.append(total)
        return result

    def coarse_step(source, target, first, scale_old, scale_new):
        def body(spot, unused):
            remains = [right[comp, spot] for comp in range(6)]
            if first:
                update = [COARSE_FIRST * v for v in product(36, remains, spot)]
                for comp in range(6):
                    target[comp, spot] = update[comp]
                    error[comp, spot] = update[comp]
                return unused
            above = lax.rem(spot + 1, SIDE)
            below = lax.rem(spot + SIDE - 1, SIDE)
            old = [source[comp, spot] for comp in range(6)]
            applied = product(0, old, spot)
            for comp in range(6):
                value = old[comp]
                faces = source[comp, above] + source[comp, below]
                faces = faces + turned(value, 4, 0)
                faces = faces + jnp.where(even, turned(value, -3, 0), turned(value, 3, 0))
                faces = faces + turned(value, 1, 1) + turned(value, -1, 1)
                remains[comp] = remains[comp] - (applied[comp] + 6.0 * value - faces)
                right[comp, spot] = remains[comp]
            fresh = product(36, remains, spot)
            for comp in range(6):
                update = scale_old * old[comp] + scale_new * fresh[comp]
                target[comp, spot] = update
                error[comp, spot] = error[comp, spot] + update
            return unused

        lax.fori_loop(0, SIDE, body, 0)

    coarse_step(None, step_a, True, 0.0, 0.0)
    coarse_step(step_a, step_b, False, *COARSE_STEPS[0])
    coarse_step(step_b, step_a, False, *COARSE_STEPS[1])

    def window_row(inner):
        return 4 * lax.rem(inner, 2) + lax.div(inner, 2)

    for half in range(2):
        inner = window_row(half + shift_y + 2)
        for comp in range(6):
            value = error[comp, mine_x, pl.ds(inner, 1), :]
            value = pltpu.roll(jnp.broadcast_to(value, (8, 128)), 126 - shift_z, 1)
            correction[comp, 0, half : half + 1, :] = value[0:1, :COARSE_OWN]

    row = lax.broadcasted_iota(jnp.int32, (ROWS, 128), 0)
    for near_x in range(3):
        at_x = lax.rem(mine_x - shift_x + near_x + SIDE, SIDE)
        for comp in range(6):
            plane = error[comp, at_x]
            value = jnp.zeros((ROWS, 128), jnp.float32)
            for near_y in range(4):
                at = 4 * (near_y % 2) + near_y // 2 + 1
                inner = row - ROW0 - shift_y - 3 * (near_y - shift_y)
                value = jnp.where((inner >= 0) & (inner < 3), plane[at : at + 1], value)
            start = (comp * 3 + near_x) * ROWS
            spread_y[start : start + ROWS] = value
    coarse = lax.broadcasted_iota(jnp.int32, (128, LANES), 0)
    fine = lax.broadcasted_iota(jnp.int32, (128, LANES), 1)
    inner = fine - 3 * coarse + 2 * shift_z - 10
    copies = jnp.where((inner >= 0) & (inner < 3), 1.0, 0.0)
    wide = jnp.dot(
        spread_y[...], copies, precision=lax.Precision.HIGHEST, preferred_element_type=jnp.float32
    )
    for which in range(18):
        spread_z[which] = wide[which * ROWS : (which + 1) * ROWS]

    row = lax.broadcasted_iota(jnp.int32, (ROWS, LANES), 0)
    fine = lax.broadcasted_iota(jnp.int32, (ROWS, LANES), 1)
    arm_y = (lax.rem(row + 4 - shift_y, 3) - 1).astype(jnp.float32)
    arm_z = (lax.rem(fine + 2 * shift_z + 2, 3) - 1).astype(jnp.float32)
    for plane in range(7):
        ahead = plane - 2 - shift_x + 6
        near_x = lax.div(ahead, 3) - 2 + shift_x
        arm_x = (lax.rem(ahead, 3) - 1).astype(jnp.float32)
        e = [spread_z[comp * 3 + near_x] for comp in range(6)]
        work[0, plane] = e[0] + e[4] * arm_z - e[5] * arm_y
        work[1, plane] = e[1] + e[5] * arm_x - e[3] * arm_z
        work[2, plane] = e[2] + e[3] * arm_y - e[4] * arm_x

    near[...] = jnp.zeros_like(near)
    near[:, :, SENT] = low[...]
    one = (shift_x == 1).astype(jnp.float32)
    two = 1.0 - one

    def remaining(at, comp):
        if at < 2:
            return near[at + 2 - shift_x, comp]
        if at == 2:
            return one * rest[0, comp] + two * near[2, comp]
        return rest[at - 1 - shift_x, comp]

    def first_step(plane, forces):
        at = plane - 1
        for comp in range(3):
            value = forces[comp] + nodes[1, at] * work[comp, plane]
            value = remaining(at, comp) - value
            resid[comp, at] = value
            step[comp, at] = nodes[0, at] * value * FINE_FIRST

    def last_step(plane, forces):
        for comp in range(3):
            old = step[comp, plane]
            value = resid[comp, plane] - (forces[comp] + nodes[1, plane] * old)
            update = FINE_STEPS[0][0] * old + FINE_STEPS[0][1] * (nodes[0, plane] * value)
            start = smoothed[plane - 1, comp]
            if plane == 1:
                start = one * start + two * near[3, comp]
            value = start + work[comp, plane + 1] + old + update
            displacement[comp, plane - 1] = value[
                ROW0 : ROW0 + OWN_Y, LANE0 : LANE0 + OWN_Z
            ]

    stencil(
        lambda comp, plane: work[comp, plane],
        lambda plane: (elements[0, plane], elements[1, plane]),
        0,
        6,
        first_step,
    )
    stencil(
        lambda comp, plane: step[comp, plane],
        lambda plane: (elements[0, plane + 1], elements[1, plane + 1]),
        0,
        4,
        last_step,
    )


def tables_kernel(blocks, tables):
    tables[0:36] = blocks[0:36]
    rows = []
    for i in range(6):
        row = [blocks[6 * i + j : 6 * i + j + 1] for j in range(6)]
        row[i] = row[i] + 6.0
        one = jnp.ones_like(row[0])
        rows.append(row + [one if i == j else jnp.zeros_like(one) for j in range(6)])
    for pivot in range(6):
        scaled = [value / rows[pivot][pivot] for value in rows[pivot]]
        for i in range(6):
            factor = rows[i][pivot]
            if i != pivot:
                rows[i] = [value - factor * line for value, line in zip(rows[i], scaled)]
        rows[pivot] = scaled
    for i in range(6):
        for j in range(6):
            entry = 36 + 6 * i + j
            tables[entry : entry + 1] = rows[i][6 + j]


def passed_along(value, axis, steps):
    count = lax.axis_size(axis)
    pairs = [(source, (source + steps) % count) for source in range(count)]
    return lax.ppermute(value, axis, pairs)


VMEM = pl.BlockSpec(memory_space=pltpu.VMEM)
SMEM = pl.BlockSpec(memory_space=pltpu.SMEM)
EDGES_VMEM = 64 * 1024 * 1024 - 64 * 1024


def call(kernel, scalars, vectors, shapes, scratch=(), work=1_000_000):
    return pl.pallas_call(
        kernel,
        out_shape=[jax.ShapeDtypeStruct(shape, jnp.float32) for shape in shapes],
        in_specs=[SMEM] * len(scalars) + [VMEM] * len(vectors),
        out_specs=[VMEM] * len(shapes),
        scratch_shapes=[pltpu.VMEM(shape, jnp.float32) for shape in scratch],
        compiler_params=pltpu.CompilerParams(vmem_limit_bytes=48 * 1024 * 1024),
        cost_estimate=pl.CostEstimate(flops=work, bytes_accessed=work, transcendentals=0),
    )(*scalars, *vectors)


def pack_edges(*arrays):
    return pl.pallas_call(
        edges_kernel,
        out_shape=[jax.ShapeDtypeStruct((OWN_X, FIELDS, 128), jnp.float32)] * 2,
        in_specs=[pl.BlockSpec(memory_space=pltpu.HBM)] * len(arrays),
        out_specs=[VMEM] * 2,
        scratch_shapes=[pltpu.VMEM(array.shape, array.dtype) for array in arrays]
        + [pltpu.SemaphoreType.DMA((len(arrays),))],
        compiler_params=pltpu.CompilerParams(vmem_limit_bytes=EDGES_VMEM),
    )(*arrays)


def pack(*arrays):
    shapes = [(OWN_X * OWN_Y * 2 * FIELDS, 128), (8, 128)]
    return call(pack_kernel, (), arrays, shapes, work=20_000_000)


def widen(block, low, high, class_ext):
    shapes = [(OWN_X * OWN_Y * 2 * FIELDS, 128), (8, 128)]
    return call(widen_kernel, (), (block, low, high, class_ext), shapes)


def pre_smooth(moduli, scalars, planes, left, right, class_wide):
    plane = (ROWS, LANES)
    return call(
        pre_kernel,
        (moduli.reshape(-1), scalars),
        (planes, left, right, class_wide),
        [(SIDE * SIDE, 8, 128), (3, 3) + plane, (4, 3, 8, LANES), (3, 3) + plane]
        + [(2, 6) + plane, (2, 5) + plane],
        [(FIELDS, PLANES) + plane] + [(PLANES,) + plane] * 3
        + [(3, 9) + plane, (3, 9) + plane, (3, 9) + plane, (5, 3) + plane],
    )


def coarse_and_post(scalars, tables, received, rest, low, smoothed, elements, nodes):
    plane = (ROWS, LANES)
    spots = (SIDE, 8, 128)
    return call(
        coarse_kernel,
        (scalars,),
        (tables, received, rest, low, smoothed, elements, nodes),
        [(3, OWN_X, OWN_Y, OWN_Z), (6, 1, 2, COARSE_OWN)],
        [(7,) + spots, (72,) + spots, (6,) + spots, (6,) + spots, (6,) + spots]
        + [(18 * ROWS, 128), (18,) + plane, (3, 7) + plane, (3, 5) + plane, (3, 5) + plane]
        + [(4, 3) + plane],
    )


def coarse_tables(class_blocks):
    entries = jnp.transpose(class_blocks.reshape(8, 36))
    entries = jnp.pad(entries, ((0, 4), (0, 120)))
    return call(tables_kernel, (), (entries,), [(72, 128)])[0]


def body(forcing, initial_guess, material, moduli, support, offsets, aggregate_class, class_blocks):
    tables = coarse_tables(class_blocks)
    place = jnp.stack([lax.axis_index("gx"), lax.axis_index("gy")]).astype(jnp.int32)
    scalars = jnp.concatenate([offsets, place])
    arrays = (initial_guess, forcing, support, material, aggregate_class)
    low, high = pack_edges(*arrays)
    from_low = passed_along(high, "gz", 1)
    from_high = passed_along(low, "gz", -1)
    block, class_ext = pack(*arrays)
    own, class_wide = widen(block, from_low, from_high, class_ext)
    own = own.reshape(OWN_X, OWN_Y, 2 * FIELDS, 128)
    before = passed_along(own[1:], "gx", 1)
    after = passed_along(own, "gx", -1)
    beyond = passed_along(own[:2], "gx", -2)
    planes = jnp.concatenate([before, own, after, beyond], axis=0)
    left = passed_along(planes[:, 1:], "gy", 1).reshape(-1, 128)
    right = passed_along(planes[:, :5], "gy", -1).reshape(-1, 128)
    chunk, rest, carry, smoothed, elements, nodes = pre_smooth(
        moduli, scalars, planes.reshape(-1, 128), left, right, class_wide
    )
    received = lax.all_to_all(chunk, ("gx", "gy"), 0, 0, tiled=True).reshape(-1, 128)
    from_before = passed_along(carry, "gx", 1)
    displacement, correction = coarse_and_post(
        scalars, tables, received, rest, from_before, smoothed, elements, nodes
    )
    return displacement, correction


def solution(mesh):
    placed = (
        P(None, "gx", "gy", "gz"),
        P(None, "gx", "gy", "gz"),
        P("gx", "gy", "gz"),
        P(),
        P("gx", "gy", "gz"),
        P(),
        P("gx", "gy", "gz"),
        P(),
    )
    return jax.shard_map(
        body,
        mesh=mesh,
        in_specs=placed,
        out_specs=(P(None, "gx", "gy", "gz"), P(None, "gx", "gy", "gz")),
        check_vma=False,
    )
```

```python
import jax
import jax.numpy as jnp
from jax import lax
from jax.experimental import pallas as pl
from jax.experimental.pallas import tpu as pltpu
from jax.sharding import PartitionSpec as P

FINE_LOW = 0.25
FINE_HIGH = 2.5
COARSE_LOW = 0.2
COARSE_HIGH = 1.9

ROWS = 16
LANES = 256
ROW0 = 5
LANE0 = 16
EDGE = 16
SENT = slice(4, 12)
PLANES = 10
OWN_X, OWN_Y, OWN_Z = 3, 6, 192
FIELDS = 8
SIDE = 8
COARSE_OWN = 64
COARSE_LANES = 70


def chebyshev(low, high, count):
    center = 0.5 * (high + low)
    spread = 0.5 * (high - low)
    ratio = center / spread
    weight = 1.0 / ratio
    steps = []
    for _ in range(1, count):
        following = 1.0 / (2.0 * ratio - weight)
        steps.append((following * weight, 2.0 * following / spread))
        weight = following
    return 1.0 / center, steps


FINE_FIRST, FINE_STEPS = chebyshev(FINE_LOW, FINE_HIGH, 2)
COARSE_FIRST, COARSE_STEPS = chebyshev(COARSE_LOW, COARSE_HIGH, 3)


def turned(value, shift, axis):
    shift = shift % value.shape[axis]
    return value if shift == 0 else pltpu.roll(value, shift, axis)


def following(value, axis):
    return turned(value, -1, axis)


def preceding(value, axis):
    return turned(value, 1, axis)


def plane_modes(value):
    ahead = following(value, 1)
    total, slope = value + ahead, ahead - value
    total_up, slope_up = following(total, 0), following(slope, 0)
    return {
        (0, 0): total + total_up,
        (1, 0): total_up - total,
        (0, 1): slope + slope_up,
        (1, 1): slope_up - slope,
    }


def element_modes(below, above, lame, shear):
    u = []
    for comp in range(3):
        modes = {}
        for key in ((0, 0), (1, 0), (0, 1), (1, 1)):
            first, second = below[comp][key], above[comp][key]
            if key != (0, 0):
                modes[(0,) + key] = first + second
            modes[(1,) + key] = second - first
        u.append(modes)
    x, y, z = u
    third = 1.0 / 3.0
    lame_b, shear_b = lame * third, shear * third
    shear_2 = shear + shear
    last = (lame + (shear_2 + shear_2)) * (1.0 / 9.0)
    f = [{}, {}, {}]
    divergence = lame * (x[1, 0, 0] + y[0, 1, 0] + z[0, 0, 1])
    f[0][1, 0, 0] = divergence + shear_2 * x[1, 0, 0]
    f[1][0, 1, 0] = divergence + shear_2 * y[0, 1, 0]
    f[2][0, 0, 1] = divergence + shear_2 * z[0, 0, 1]
    f[0][0, 1, 0] = f[1][1, 0, 0] = shear * (x[0, 1, 0] + y[1, 0, 0])
    f[0][0, 0, 1] = f[2][1, 0, 0] = shear * (x[0, 0, 1] + z[1, 0, 0])
    f[1][0, 0, 1] = f[2][0, 1, 0] = shear * (y[0, 0, 1] + z[0, 1, 0])
    for one, key_one, two, key_two in (
        (0, (1, 1, 0), 2, (0, 1, 1)),
        (0, (1, 0, 1), 1, (0, 1, 1)),
        (1, (1, 1, 0), 2, (1, 0, 1)),
    ):
        shared = lame_b * (u[one][key_one] + u[two][key_two])
        f[one][key_one] = shared + shear * u[one][key_one]
        f[two][key_two] = shared + shear * u[two][key_two]
    mixed = x[0, 1, 1] + y[1, 0, 1] + z[1, 1, 0]
    f[0][0, 1, 1] = shear_b * (mixed + x[0, 1, 1])
    f[1][1, 0, 1] = shear_b * (mixed + y[1, 0, 1])
    f[2][1, 1, 0] = shear_b * (mixed + z[1, 1, 0])
    for comp in range(3):
        f[comp][1, 1, 1] = last * u[comp][1, 1, 1]
    low, high = [], []
    for comp in range(3):
        down, up = {}, {}
        for key in ((0, 0), (1, 0), (0, 1), (1, 1)):
            slope = f[comp][(1,) + key]
            if key == (0, 0):
                down[key], up[key] = -slope, slope
            else:
                total = f[comp][(0,) + key]
                down[key], up[key] = total - slope, total + slope
        low.append(down)
        high.append(up)
    return low, high


def plane_forces(modes):
    parts = []
    for last in (0, 1):
        total, slope = modes[0, last], modes[1, last]
        parts.append((total - slope) + preceding(total + slope, 0))
    return (parts[0] - parts[1]) + preceding(parts[0] + parts[1], 1)


def stencil(read, elements, first, last, emit):
    below = [plane_modes(read(comp, first)) for comp in range(3)]
    carried = None
    for plane in range(first, last):
        above = [plane_modes(read(comp, plane + 1)) for comp in range(3)]
        low, high = element_modes(below, above, *elements(plane))
        if carried is not None:
            emit(
                plane,
                [
                    plane_forces({key: low[comp][key] + carried[comp][key] for key in low[comp]})
                    for comp in range(3)
                ],
            )
        below, carried = above, high


def picked_sums(values, weights):
    high = values.astype(jnp.bfloat16)
    left = values - high.astype(jnp.float32)
    middle = left.astype(jnp.bfloat16)
    low = (left - middle.astype(jnp.float32)).astype(jnp.bfloat16)
    weights = weights.astype(jnp.bfloat16)
    parts = [
        jnp.dot(part, weights, preferred_element_type=jnp.float32) for part in (low, middle, high)
    ]
    return (parts[0] + parts[1]) + parts[2]


def tile_row(plane, row, half):
    return ((plane * OWN_Y + row) * 2 + half) * FIELDS


def field_planes(guess, forcing, support, material, plane):
    for comp in range(3):
        yield comp, guess[comp, plane]
        yield 3 + comp, forcing[comp, plane]
    yield 6, support[plane]
    yield 7, material[plane].astype(jnp.float32)


def edges_kernel(
    guess_h, forcing_h, support_h, material_h, classes_h, low, high, guess, forcing, support, material,
    classes, done,
):
    pairs = (
        (guess_h, guess),
        (forcing_h, forcing),
        (support_h, support),
        (material_h, material),
        (classes_h, classes),
    )
    copies = [
        pltpu.make_async_copy(source, target, done.at[which])
        for which, (source, target) in enumerate(pairs)
    ]
    for copy in copies:
        copy.start()
    low[...] = jnp.zeros_like(low)
    high[...] = jnp.zeros_like(high)
    for copy in copies:
        copy.wait()
    kinds = classes[0].astype(jnp.float32)
    low[0, 0:2, 96:112] = kinds[:, 0:EDGE]
    high[0, 0:2, 96:112] = kinds[:, COARSE_OWN - EDGE :]
    for plane in range(OWN_X):
        for field, value in field_planes(guess, forcing, support, material, plane):
            for row in range(OWN_Y):
                line = value[row : row + 1]
                low[plane, field : field + 1, EDGE * row : EDGE * (row + 1)] = line[:, :EDGE]
                high[plane, field : field + 1, EDGE * row : EDGE * (row + 1)] = line[:, -EDGE:]


def pack_kernel(guess, forcing, support, material, classes, block, class_ext):
    first = 128 - LANE0
    block[...] = jnp.zeros_like(block)
    class_ext[...] = jnp.zeros_like(class_ext)
    class_ext[0:2, LANE0 : LANE0 + COARSE_OWN] = classes[0].astype(jnp.float32)
    for plane in range(OWN_X):
        for field, value in field_planes(guess, forcing, support, material, plane):
            for row in range(OWN_Y):
                line = value[row : row + 1]
                start = tile_row(plane, row, 0) + field
                block[start : start + 1, LANE0:128] = line[:, :first]
                start = tile_row(plane, row, 1) + field
                block[start : start + 1, 0 : OWN_Z - first] = line[:, first:]


def widen_kernel(block, low, high, class_ext, wide, class_wide):
    lane = lax.broadcasted_iota(jnp.int32, (8, 128), 1)
    end = LANE0 + OWN_Z - 128
    for plane in range(OWN_X):
        for row in range(OWN_Y):
            start = tile_row(plane, row, 0)
            wide[start : start + 8] = jnp.where(
                lane < LANE0, turned(low[plane], -EDGE * row, 1), block[start : start + 8]
            )
            start = tile_row(plane, row, 1)
            wide[start : start + 8] = jnp.where(
                (lane >= end) & (lane < end + EDGE),
                turned(high[plane], end - EDGE * row, 1),
                block[start : start + 8],
            )
    end = LANE0 + COARSE_OWN
    value = jnp.where(lane < LANE0, turned(low[0], -96, 1), class_ext[...])
    class_wide[...] = jnp.where(
        (lane >= end) & (lane < end + EDGE), turned(high[0], end - 96, 1), value
    )


def pre_kernel(
    moduli, scalars, planes, left, right, class_wide, chunk, remains, carry, smoothed, elements, nodes,
    fields, lame_s, shear_s, inverse_s, resid, step_one, step_two, sums_s,
):
    for plane in range(PLANES):
        for field in range(FIELDS):
            for half in range(2):
                lanes = slice(128 * half, 128 * half + 128)
                start = (plane * 5 * 2 + half) * FIELDS + field
                fields[field, plane, 0:5, lanes] = left[pl.ds(start, 5, stride=16), :]
                fields[field, plane, 11:16, lanes] = right[pl.ds(start, 5, stride=16), :]
                start = tile_row(plane, 0, half) + field
                fields[field, plane, 5:11, lanes] = planes[pl.ds(start, 6, stride=16), :]
    table = [
        [moduli[which : which + 1, kind : kind + 1] for kind in range(4)]
        for which in range(2)
    ]
    carried = None
    for plane in range(PLANES - 1):
        kind = fields[7, plane]
        picked = []
        for which in range(2):
            value = jnp.where(kind < 2.5, table[which][2], table[which][3])
            value = jnp.where(kind < 1.5, table[which][1], value)
            picked.append(jnp.where(kind < 0.5, table[which][0], value))
        lame_s[plane] = picked[0]
        shear_s[plane] = picked[1]
        weight = (picked[0] + 4.0 * picked[1]) * (16.0 / 9.0)
        weight = weight + preceding(weight, 1)
        weight = weight + preceding(weight, 0)
        if carried is not None:
            inverse_s[plane] = 1.0 / (fields[6, plane] + weight + carried)
        carried = weight
    for plane in range(6):
        elements[0, plane] = lame_s[plane]
        elements[1, plane] = shear_s[plane]
    for plane in range(5):
        nodes[0, plane] = inverse_s[plane + 1]
        nodes[1, plane] = fields[6, plane + 1]

    shift_x, shift_y, shift_z = scalars[0, 0], scalars[0, 1], scalars[0, 2]
    base = shift_x - 1

    def coefficients(plane):
        return lame_s[base + plane], shear_s[base + plane]

    def first_step(plane, forces):
        at = base + plane
        support, inverse = fields[6, at], inverse_s[at]
        for comp in range(3):
            value = forces[comp] + support * fields[comp, at]
            value = fields[3 + comp, at] - value
            resid[comp, plane] = value
            step_one[comp, plane] = inverse * value * FINE_FIRST

    def second_step(plane, forces):
        at = base + plane
        support, inverse = fields[6, at], inverse_s[at]
        for comp in range(3):
            step = step_one[comp, plane]
            value = resid[comp, plane] - (forces[comp] + support * step)
            resid[comp, plane] = value
            update = FINE_STEPS[0][0] * step + FINE_STEPS[0][1] * (inverse * value)
            step_two[comp, plane] = update
            sums_s[plane - 2, comp] = fields[comp, at] + step + update

    def last_step(plane, forces):
        support = fields[6, base + plane]
        for comp in range(3):
            value = forces[comp] + support * step_two[comp, plane]
            value = resid[comp, plane] - value
            remains[plane - 3, comp] = value
            carry[plane - 3, comp] = value[SENT]

    stencil(lambda comp, plane: fields[comp, base + plane], coefficients, 0, 8, first_step)
    stencil(lambda comp, plane: step_one[comp, plane], coefficients, 1, 7, second_step)
    stencil(lambda comp, plane: step_two[comp, plane], coefficients, 2, 6, last_step)
    for comp in range(3):
        smoothed[0, comp] = sums_s[0, comp]
        smoothed[1, comp] = sums_s[2 - shift_x, comp]
        smoothed[2, comp] = sums_s[3 - shift_x, comp]
        carry[3, comp] = sums_s[4 - shift_x, comp][SENT]

    total = [remains[0, comp] + remains[1, comp] + remains[2, comp] for comp in range(3)]
    moment = [remains[2, comp] - remains[0, comp] for comp in range(3)]
    row = lax.broadcasted_iota(jnp.int32, (ROWS, LANES), 0)
    plain = jnp.zeros((ROWS, LANES), jnp.float32)
    lever = jnp.zeros((ROWS, LANES), jnp.float32)
    for half in range(2):
        place = row - (ROW0 + 3 * half) - shift_y
        inside = (place >= 0) & (place < 3)
        arm = (place - 1).astype(jnp.float32)

        def summed(value):
            return jnp.sum(jnp.where(inside, value, 0.0), axis=0, keepdims=True)

        sums = [summed(total[comp]) for comp in range(3)]
        lines = sums + [
            summed(arm * total[2]),
            summed(-moment[2]),
            summed(moment[1] - arm * total[0]),
        ]
        for comp in range(6):
            plain = jnp.where(row == 8 * half + comp, lines[comp], plain)
        lever = jnp.where(row == 8 * half + 3, -sums[1], lever)
        lever = jnp.where(row == 8 * half + 4, sums[0], lever)
    fine = lax.broadcasted_iota(jnp.int32, (LANES, 128), 0)
    coarse = lax.broadcasted_iota(jnp.int32, (LANES, 128), 1)
    place = fine - 3 * coarse + 2 * shift_z - 10
    inside = (place >= 0) & (place < 3) & (coarse < COARSE_LANES)
    sums_z = jnp.where(inside, 1.0, 0.0)
    arms_z = jnp.where(inside, (place - 1).astype(jnp.float32), 0.0)
    result = picked_sums(plain, sums_z) + picked_sums(lever, arms_z)
    kinds = pltpu.roll(class_wide[...], shift_z + (128 - 14), 1)
    line = lax.broadcasted_iota(jnp.int32, (8, 128), 0)
    lane = lax.broadcasted_iota(jnp.int32, (8, 128), 1)
    low = jnp.where(line == 6, kinds[0:1], result[0:8])
    high = jnp.where(line == 6, kinds[1:2], result[8:16])
    packed = jnp.where(lane < 64, turned(low, -3, 1), turned(high, 61, 1))
    ends = jnp.zeros((1, 128), jnp.float32)
    lane_one = lane[0:1]
    for half in range(2):
        for comp in range(7):
            base = 12 * comp + 6 * half
            source = (low, high)[half][comp : comp + 1]
            ends = jnp.where(
                (lane_one >= base) & (lane_one < base + 3), turned(source, base, 1), ends
            )
            ends = jnp.where(
                (lane_one >= base + 3) & (lane_one < base + 6), turned(source, base - 64, 1), ends
            )
    packed = jnp.where(line == 7, ends, packed)
    for target in range(SIDE * SIDE):
        chunk[target] = packed


def coarse_kernel(
    scalars, tables, received, rest, low, smoothed, elements, nodes, displacement, correction, right,
    matrix, step_a, step_b, error, spread_y, spread_z, work, step, resid, near,
):
    shift_x, shift_y, shift_z = scalars[0, 0], scalars[0, 1], scalars[0, 2]
    mine_x, mine_y = scalars[0, 3], scalars[0, 4]
    lane = lax.broadcasted_iota(jnp.int32, (8, 128), 1)
    line = lax.broadcasted_iota(jnp.int32, (8, 128), 0)
    even = line < 4
    middle = (lane >= 3) & (lane < 67)
    odd_shift = lax.rem(shift_y, 2)
    turn_even = lax.rem(SIDE + 2 - mine_y, SIDE)
    turn_odd = lax.rem(SIDE + 6 - mine_y - odd_shift, SIDE)
    for at_x in range(SIDE):
        ends = received[pl.ds(64 * at_x + 7, 8, stride=8), :]
        ends = [pltpu.roll(ends, turn_even, 0), pltpu.roll(ends, turn_odd, 0)]
        for comp in range(7):
            main = received[pl.ds(64 * at_x + comp, 8, stride=8), :]
            main = [pltpu.roll(main, turn_even, 0), pltpu.roll(main, turn_odd, 0)]
            parts = []
            for which in range(2):
                half = odd_shift if which == 0 else 1 - odd_shift
                base = 12 * comp + 6 * half
                low_end = pltpu.roll(ends[which], lax.rem(128 - base, 128), 1)
                high_end = pltpu.roll(ends[which], lax.rem(192 - base, 128), 1)
                value = jnp.where(lane < 3, low_end, high_end)
                parts.append(jnp.where(middle, pltpu.roll(main[which], 3 + 64 * half, 1), value))
            value = jnp.where(even, parts[0], parts[1])
            right[comp, at_x] = jnp.where(lane < COARSE_LANES, value, 0.0)

    kinds = [right[6, spot].astype(jnp.int32) for spot in range(SIDE)]
    for entry in range(36):
        values = jnp.broadcast_to(tables[entry : entry + 1], (8, 128))
        for spot in range(SIDE):
            matrix[entry, spot] = jnp.take_along_axis(
                values, kinds[spot], axis=1, mode="promise_in_bounds"
            )

    def product(values, spot):
        result = []
        for i in range(6):
            total = matrix[6 * i, spot] * values[0]
            for j in range(1, 6):
                total = total + matrix[6 * i + j, spot] * values[j]
            result.append(total)
        return result

    def neighbours(source, spot, comp):
        value = source[comp, spot]
        faces = source[comp, (spot + 1) % SIDE] + source[comp, (spot - 1) % SIDE]
        faces = faces + turned(value, 4, 0)
        faces = faces + jnp.where(even, turned(value, -3, 0), turned(value, 3, 0))
        return faces + turned(value, 1, 1) + turned(value, -1, 1)

    for spot in range(SIDE):
        held = [right[comp, spot] for comp in range(6)]
        fresh = product(held, spot)
        for comp in range(6):
            step_a[comp, spot] = COARSE_FIRST * fresh[comp]
    scale_old, scale_new = COARSE_STEPS[0]
    for spot in range(SIDE):
        held = [right[comp, spot] for comp in range(6)]
        remains = []
        for comp in range(6):
            known = COARSE_FIRST * held[comp]
            value = held[comp] - (known - neighbours(step_a, spot, comp))
            remains.append(value)
            known = scale_old * known + scale_new * value
            right[comp, spot] = value - known
        fresh = product(remains, spot)
        for comp in range(6):
            step_b[comp, spot] = scale_old * step_a[comp, spot] + scale_new * fresh[comp]
    scale_old, scale_new = COARSE_STEPS[1]
    for spot in range(SIDE):
        remains = [right[comp, spot] + neighbours(step_b, spot, comp) for comp in range(6)]
        fresh = product(remains, spot)
        for comp in range(6):
            old = step_b[comp, spot]
            update = scale_old * old + scale_new * fresh[comp]
            error[comp, spot] = step_a[comp, spot] + old + update

    def window_row(inner):
        return 4 * lax.rem(inner, 2) + lax.div(inner, 2)

    for half in range(2):
        inner = window_row(half + shift_y + 2)
        for comp in range(6):
            value = error[comp, mine_x, pl.ds(inner, 1), :]
            value = pltpu.roll(jnp.broadcast_to(value, (8, 128)), 126 - shift_z, 1)
            correction[comp, 0, half : half + 1, :] = value[0:1, :COARSE_OWN]

    row = lax.broadcasted_iota(jnp.int32, (ROWS, 128), 0)
    for near_x in range(3):
        at_x = lax.rem(mine_x - shift_x + near_x + SIDE, SIDE)
        for comp in range(6):
            plane = error[comp, at_x]
            value = jnp.zeros((ROWS, 128), jnp.float32)
            for near_y in range(4):
                at = 4 * (near_y % 2) + near_y // 2 + 1
                inner = row - ROW0 - shift_y - 3 * (near_y - shift_y)
                value = jnp.where((inner >= 0) & (inner < 3), plane[at : at + 1], value)
            start = (comp * 3 + near_x) * ROWS
            spread_y[start : start + ROWS] = value
    coarse = lax.broadcasted_iota(jnp.int32, (128, LANES), 0)
    fine = lax.broadcasted_iota(jnp.int32, (128, LANES), 1)
    inner = fine - 3 * coarse + 2 * shift_z - 10
    copies = jnp.where((inner >= 0) & (inner < 3), 1.0, 0.0)
    wide = picked_sums(spread_y[...], copies)
    for which in range(18):
        spread_z[which] = wide[which * ROWS : (which + 1) * ROWS]

    row = lax.broadcasted_iota(jnp.int32, (ROWS, LANES), 0)
    fine = lax.broadcasted_iota(jnp.int32, (ROWS, LANES), 1)
    arm_y = (lax.rem(row + 4 - shift_y, 3) - 1).astype(jnp.float32)
    arm_z = (lax.rem(fine + 2 * shift_z + 2, 3) - 1).astype(jnp.float32)
    for plane in range(7):
        ahead = plane - 2 - shift_x + 6
        near_x = lax.div(ahead, 3) - 2 + shift_x
        arm_x = (lax.rem(ahead, 3) - 1).astype(jnp.float32)
        e = [spread_z[comp * 3 + near_x] for comp in range(6)]
        work[0, plane] = e[0] + e[4] * arm_z - e[5] * arm_y
        work[1, plane] = e[1] + e[5] * arm_x - e[3] * arm_z
        work[2, plane] = e[2] + e[3] * arm_y - e[4] * arm_x

    near[...] = jnp.zeros_like(near)
    near[:, :, SENT] = low[...]
    one = (shift_x == 1).astype(jnp.float32)
    two = 1.0 - one

    def remaining(at, comp):
        if at < 2:
            return near[at + 2 - shift_x, comp]
        if at == 2:
            return one * rest[0, comp] + two * near[2, comp]
        return rest[at - 1 - shift_x, comp]

    def first_step(plane, forces):
        at = plane - 1
        for comp in range(3):
            value = forces[comp] + nodes[1, at] * work[comp, plane]
            value = remaining(at, comp) - value
            resid[comp, at] = value
            step[comp, at] = nodes[0, at] * value * FINE_FIRST

    def last_step(plane, forces):
        for comp in range(3):
            old = step[comp, plane]
            value = resid[comp, plane] - (forces[comp] + nodes[1, plane] * old)
            update = FINE_STEPS[0][0] * old + FINE_STEPS[0][1] * (nodes[0, plane] * value)
            start = smoothed[plane - 1, comp]
            if plane == 1:
                start = one * start + two * near[3, comp]
            value = start + work[comp, plane + 1] + old + update
            displacement[comp, plane - 1] = value[
                ROW0 : ROW0 + OWN_Y, LANE0 : LANE0 + OWN_Z
            ]

    stencil(
        lambda comp, plane: work[comp, plane],
        lambda plane: (elements[0, plane], elements[1, plane]),
        0,
        6,
        first_step,
    )
    stencil(
        lambda comp, plane: step[comp, plane],
        lambda plane: (elements[0, plane + 1], elements[1, plane + 1]),
        0,
        4,
        last_step,
    )


def tables_kernel(blocks, tables):
    rows = []
    for i in range(6):
        row = [blocks[6 * i + j : 6 * i + j + 1] for j in range(6)]
        row[i] = row[i] + 6.0
        one = jnp.ones_like(row[0])
        rows.append(row + [one if i == j else jnp.zeros_like(one) for j in range(6)])
    for pivot in range(6):
        scaled = [value / rows[pivot][pivot] for value in rows[pivot]]
        for i in range(6):
            factor = rows[i][pivot]
            if i != pivot:
                rows[i] = [value - factor * line for value, line in zip(rows[i], scaled)]
        rows[pivot] = scaled
    tables[36:40] = jnp.zeros_like(tables[36:40])
    for i in range(6):
        for j in range(6):
            entry = 6 * i + j
            tables[entry : entry + 1] = rows[i][6 + j]


def passed_along(value, axis, steps):
    count = lax.axis_size(axis)
    pairs = [(source, (source + steps) % count) for source in range(count)]
    return lax.ppermute(value, axis, pairs)


VMEM = pl.BlockSpec(memory_space=pltpu.VMEM)
EDGES_VMEM = 64 * 1024 * 1024 - 64 * 1024


def call(kernel, arrays, shapes, scratch=(), work=1_000_000):
    return pl.pallas_call(
        kernel,
        out_shape=[jax.ShapeDtypeStruct(shape, jnp.float32) for shape in shapes],
        in_specs=[VMEM] * len(arrays),
        out_specs=[VMEM] * len(shapes),
        scratch_shapes=[pltpu.VMEM(shape, jnp.float32) for shape in scratch],
        compiler_params=pltpu.CompilerParams(vmem_limit_bytes=48 * 1024 * 1024),
        cost_estimate=pl.CostEstimate(flops=work, bytes_accessed=work, transcendentals=0),
    )(*arrays)


def pack_edges(*arrays):
    return pl.pallas_call(
        edges_kernel,
        out_shape=[jax.ShapeDtypeStruct((OWN_X, FIELDS, 128), jnp.float32)] * 2,
        in_specs=[pl.BlockSpec(memory_space=pltpu.HBM)] * len(arrays),
        out_specs=[VMEM] * 2,
        scratch_shapes=[pltpu.VMEM(array.shape, array.dtype) for array in arrays]
        + [pltpu.SemaphoreType.DMA((len(arrays),))],
        compiler_params=pltpu.CompilerParams(vmem_limit_bytes=EDGES_VMEM),
    )(*arrays)


def pack(*arrays):
    shapes = [(OWN_X * OWN_Y * 2 * FIELDS, 128), (8, 128)]
    return call(pack_kernel, arrays, shapes, work=20_000_000)


def widen(block, low, high, class_ext):
    shapes = [(OWN_X * OWN_Y * 2 * FIELDS, 128), (8, 128)]
    return call(widen_kernel, (block, low, high, class_ext), shapes)


def pre_smooth(moduli, scalars, planes, left, right, class_wide):
    plane = (ROWS, LANES)
    return call(
        pre_kernel,
        (moduli, scalars, planes, left, right, class_wide),
        [(SIDE * SIDE, 8, 128), (3, 3) + plane, (4, 3, 8, LANES), (3, 3) + plane]
        + [(2, 6) + plane, (2, 5) + plane],
        [(FIELDS, PLANES) + plane] + [(PLANES,) + plane] * 3
        + [(3, 9) + plane, (3, 9) + plane, (3, 9) + plane, (5, 3) + plane],
    )


def coarse_and_post(scalars, tables, received, rest, low, smoothed, elements, nodes):
    plane = (ROWS, LANES)
    spots = (SIDE, 8, 128)
    return call(
        coarse_kernel,
        (scalars, tables, received, rest, low, smoothed, elements, nodes),
        [(3, OWN_X, OWN_Y, OWN_Z), (6, 1, 2, COARSE_OWN)],
        [(7,) + spots, (36,) + spots, (6,) + spots, (6,) + spots, (6,) + spots]
        + [(18 * ROWS, 128), (18,) + plane, (3, 7) + plane, (3, 5) + plane, (3, 5) + plane]
        + [(4, 3) + plane],
    )


def coarse_tables(class_blocks):
    entries = jnp.transpose(class_blocks.reshape(8, 36))
    entries = jnp.pad(entries, ((0, 4), (0, 120)))
    return call(tables_kernel, (entries,), [(40, 128)])[0]


def body(forcing, initial_guess, material, moduli, support, offsets, aggregate_class, class_blocks):
    tables = coarse_tables(class_blocks)
    place = jnp.stack([lax.axis_index("gx"), lax.axis_index("gy")]).astype(jnp.int32)
    scalars = jnp.concatenate([offsets, place]).reshape(1, 5)
    arrays = (initial_guess, forcing, support, material, aggregate_class)
    low, high = pack_edges(*arrays)
    from_low = passed_along(high, "gz", 1)
    from_high = passed_along(low, "gz", -1)
    block, class_ext = pack(*arrays)
    own, class_wide = widen(block, from_low, from_high, class_ext)
    own = own.reshape(OWN_X, OWN_Y, 2 * FIELDS, 128)
    before = passed_along(own[1:], "gx", 1)
    after = passed_along(own, "gx", -1)
    beyond = passed_along(own[:2], "gx", -2)
    planes = jnp.concatenate([before, own, after, beyond], axis=0)
    left = passed_along(planes[:, 1:], "gy", 1).reshape(-1, 128)
    right = passed_along(planes[:, :5], "gy", -1).reshape(-1, 128)
    chunk, rest, carry, smoothed, elements, nodes = pre_smooth(
        moduli * (1.0 / 16.0), scalars, planes.reshape(-1, 128), left, right, class_wide
    )
    received = lax.all_to_all(chunk, ("gx", "gy"), 0, 0, tiled=True).reshape(-1, 128)
    from_before = passed_along(carry, "gx", 1)
    displacement, correction = coarse_and_post(
        scalars, tables, received, rest, from_before, smoothed, elements, nodes
    )
    return displacement, correction


def solution(mesh):
    placed = (
        P(None, "gx", "gy", "gz"),
        P(None, "gx", "gy", "gz"),
        P("gx", "gy", "gz"),
        P(),
        P("gx", "gy", "gz"),
        P(),
        P("gx", "gy", "gz"),
        P(),
    )
    return jax.shard_map(
        body,
        mesh=mesh,
        in_specs=placed,
        out_specs=(P(None, "gx", "gy", "gz"), P(None, "gx", "gy", "gz")),
        check_vma=False,
    )
```

```python
import jax
import jax.numpy as jnp
from jax import lax
from jax.experimental import pallas as pl
from jax.experimental.pallas import tpu as pltpu
from jax.sharding import PartitionSpec as P

FINE_LOW = 0.25
FINE_HIGH = 2.5
COARSE_LOW = 0.2
COARSE_HIGH = 1.9

ROWS = 16
LANES = 256
ROW0 = 5
LANE0 = 16
EDGE = 16
SENT = slice(4, 12)
PLANES = 10
OWN_X, OWN_Y, OWN_Z = 3, 6, 192
FIELDS = 8
SIDE = 8
COARSE_OWN = 64
COARSE_LANES = 70


def chebyshev(low, high, count):
    center = 0.5 * (high + low)
    spread = 0.5 * (high - low)
    ratio = center / spread
    weight = 1.0 / ratio
    steps = []
    for _ in range(1, count):
        following = 1.0 / (2.0 * ratio - weight)
        steps.append((following * weight, 2.0 * following / spread))
        weight = following
    return 1.0 / center, steps


FINE_FIRST, FINE_STEPS = chebyshev(FINE_LOW, FINE_HIGH, 2)
COARSE_FIRST, COARSE_STEPS = chebyshev(COARSE_LOW, COARSE_HIGH, 3)


def turned(value, shift, axis):
    shift = shift % value.shape[axis]
    return value if shift == 0 else pltpu.roll(value, shift, axis)


def following(value, axis):
    return turned(value, -1, axis)


def preceding(value, axis):
    return turned(value, 1, axis)


def plane_modes(value):
    ahead = following(value, 1)
    total, slope = value + ahead, ahead - value
    total_up, slope_up = following(total, 0), following(slope, 0)
    return {
        (0, 0): total + total_up,
        (1, 0): total_up - total,
        (0, 1): slope + slope_up,
        (1, 1): slope_up - slope,
    }


def element_modes(below, above, lame, shear):
    u = []
    for comp in range(3):
        modes = {}
        for key in ((0, 0), (1, 0), (0, 1), (1, 1)):
            first, second = below[comp][key], above[comp][key]
            if key != (0, 0):
                modes[(0,) + key] = first + second
            modes[(1,) + key] = second - first
        u.append(modes)
    x, y, z = u
    third = 1.0 / 3.0
    lame_b, shear_b = lame * third, shear * third
    shear_2 = shear + shear
    last = (lame + (shear_2 + shear_2)) * (1.0 / 9.0)
    f = [{}, {}, {}]
    divergence = lame * (x[1, 0, 0] + y[0, 1, 0] + z[0, 0, 1])
    f[0][1, 0, 0] = divergence + shear_2 * x[1, 0, 0]
    f[1][0, 1, 0] = divergence + shear_2 * y[0, 1, 0]
    f[2][0, 0, 1] = divergence + shear_2 * z[0, 0, 1]
    f[0][0, 1, 0] = f[1][1, 0, 0] = shear * (x[0, 1, 0] + y[1, 0, 0])
    f[0][0, 0, 1] = f[2][1, 0, 0] = shear * (x[0, 0, 1] + z[1, 0, 0])
    f[1][0, 0, 1] = f[2][0, 1, 0] = shear * (y[0, 0, 1] + z[0, 1, 0])
    for one, key_one, two, key_two in (
        (0, (1, 1, 0), 2, (0, 1, 1)),
        (0, (1, 0, 1), 1, (0, 1, 1)),
        (1, (1, 1, 0), 2, (1, 0, 1)),
    ):
        shared = lame_b * (u[one][key_one] + u[two][key_two])
        f[one][key_one] = shared + shear * u[one][key_one]
        f[two][key_two] = shared + shear * u[two][key_two]
    mixed = x[0, 1, 1] + y[1, 0, 1] + z[1, 1, 0]
    f[0][0, 1, 1] = shear_b * (mixed + x[0, 1, 1])
    f[1][1, 0, 1] = shear_b * (mixed + y[1, 0, 1])
    f[2][1, 1, 0] = shear_b * (mixed + z[1, 1, 0])
    for comp in range(3):
        f[comp][1, 1, 1] = last * u[comp][1, 1, 1]
    low, high = [], []
    for comp in range(3):
        down, up = {}, {}
        for key in ((0, 0), (1, 0), (0, 1), (1, 1)):
            slope = f[comp][(1,) + key]
            if key == (0, 0):
                down[key], up[key] = -slope, slope
            else:
                total = f[comp][(0,) + key]
                down[key], up[key] = total - slope, total + slope
        low.append(down)
        high.append(up)
    return low, high


def plane_forces(modes):
    parts = []
    for last in (0, 1):
        total, slope = modes[0, last], modes[1, last]
        parts.append((total - slope) + preceding(total + slope, 0))
    return (parts[0] - parts[1]) + preceding(parts[0] + parts[1], 1)


def stencil(read, elements, first, last, emit):
    below = [plane_modes(read(comp, first)) for comp in range(3)]
    carried = None
    for plane in range(first, last):
        above = [plane_modes(read(comp, plane + 1)) for comp in range(3)]
        low, high = element_modes(below, above, *elements(plane))
        if carried is not None:
            emit(
                plane,
                [
                    plane_forces({key: low[comp][key] + carried[comp][key] for key in low[comp]})
                    for comp in range(3)
                ],
            )
        below, carried = above, high


def picked_sums(values, weights):
    high = values.astype(jnp.bfloat16)
    left = values - high.astype(jnp.float32)
    middle = left.astype(jnp.bfloat16)
    low = (left - middle.astype(jnp.float32)).astype(jnp.bfloat16)
    weights = weights.astype(jnp.bfloat16)
    parts = [
        jnp.dot(part, weights, preferred_element_type=jnp.float32) for part in (low, middle, high)
    ]
    return (parts[0] + parts[1]) + parts[2]


def tile_row(plane, row, half):
    return ((plane * OWN_Y + row) * 2 + half) * FIELDS


def field_planes(guess, forcing, support, material, plane):
    for comp in range(3):
        yield comp, guess[comp, plane]
        yield 3 + comp, forcing[comp, plane]
    yield 6, support[plane]
    yield 7, material[plane].astype(jnp.float32)


def edges_kernel(
    guess_h, forcing_h, support_h, material_h, classes_h, low, high, guess, forcing, support, material,
    classes, done,
):
    pairs = (
        (guess_h, guess),
        (forcing_h, forcing),
        (support_h, support),
        (material_h, material),
        (classes_h, classes),
    )
    copies = [
        pltpu.make_async_copy(source, target, done.at[which])
        for which, (source, target) in enumerate(pairs)
    ]
    for copy in copies:
        copy.start()
    low[...] = jnp.zeros_like(low)
    high[...] = jnp.zeros_like(high)
    for copy in copies:
        copy.wait()
    kinds = classes[0].astype(jnp.float32)
    low[0, 0:2, 96:112] = kinds[:, 0:EDGE]
    high[0, 0:2, 96:112] = kinds[:, COARSE_OWN - EDGE :]
    for plane in range(OWN_X):
        for field, value in field_planes(guess, forcing, support, material, plane):
            for row in range(OWN_Y):
                line = value[row : row + 1]
                low[plane, field : field + 1, EDGE * row : EDGE * (row + 1)] = line[:, :EDGE]
                high[plane, field : field + 1, EDGE * row : EDGE * (row + 1)] = line[:, -EDGE:]


def pack_kernel(guess, forcing, support, material, classes, block, class_ext):
    first = 128 - LANE0
    block[...] = jnp.zeros_like(block)
    class_ext[...] = jnp.zeros_like(class_ext)
    class_ext[0:2, LANE0 : LANE0 + COARSE_OWN] = classes[0].astype(jnp.float32)
    for plane in range(OWN_X):
        for field, value in field_planes(guess, forcing, support, material, plane):
            for row in range(OWN_Y):
                line = value[row : row + 1]
                start = tile_row(plane, row, 0) + field
                block[start : start + 1, LANE0:128] = line[:, :first]
                start = tile_row(plane, row, 1) + field
                block[start : start + 1, 0 : OWN_Z - first] = line[:, first:]


def widen_kernel(block, low, high, class_ext, wide, class_wide):
    lane = lax.broadcasted_iota(jnp.int32, (8, 128), 1)
    end = LANE0 + OWN_Z - 128
    for plane in range(OWN_X):
        for row in range(OWN_Y):
            start = tile_row(plane, row, 0)
            wide[start : start + 8] = jnp.where(
                lane < LANE0, turned(low[plane], -EDGE * row, 1), block[start : start + 8]
            )
            start = tile_row(plane, row, 1)
            wide[start : start + 8] = jnp.where(
                (lane >= end) & (lane < end + EDGE),
                turned(high[plane], end - EDGE * row, 1),
                block[start : start + 8],
            )
    end = LANE0 + COARSE_OWN
    value = jnp.where(lane < LANE0, turned(low[0], -96, 1), class_ext[...])
    class_wide[...] = jnp.where(
        (lane >= end) & (lane < end + EDGE), turned(high[0], end - 96, 1), value
    )


def pre_kernel(
    moduli, scalars, planes, left, right, class_wide, chunk, remains, carry, smoothed, elements, nodes,
    fields, lame_s, shear_s, inverse_s, resid, step_one, step_two, sums_s,
):
    for plane in range(PLANES):
        for field in range(FIELDS):
            for half in range(2):
                lanes = slice(128 * half, 128 * half + 128)
                start = (plane * 5 * 2 + half) * FIELDS + field
                fields[field, plane, 0:5, lanes] = left[pl.ds(start, 5, stride=16), :]
                fields[field, plane, 11:16, lanes] = right[pl.ds(start, 5, stride=16), :]
                start = tile_row(plane, 0, half) + field
                fields[field, plane, 5:11, lanes] = planes[pl.ds(start, 6, stride=16), :]
    table = [
        [moduli[which : which + 1, kind : kind + 1] for kind in range(4)]
        for which in range(2)
    ]
    carried = None
    for plane in range(PLANES - 1):
        kind = fields[7, plane]
        picked = []
        for which in range(2):
            value = jnp.where(kind < 2.5, table[which][2], table[which][3])
            value = jnp.where(kind < 1.5, table[which][1], value)
            picked.append(jnp.where(kind < 0.5, table[which][0], value))
        lame_s[plane] = picked[0]
        shear_s[plane] = picked[1]
        weight = (picked[0] + 4.0 * picked[1]) * (16.0 / 9.0)
        weight = weight + preceding(weight, 1)
        weight = weight + preceding(weight, 0)
        if carried is not None:
            inverse_s[plane] = 1.0 / (fields[6, plane] + weight + carried)
        carried = weight
    for plane in range(6):
        elements[0, plane] = lame_s[plane]
        elements[1, plane] = shear_s[plane]
    for plane in range(5):
        nodes[0, plane] = inverse_s[plane + 1]
        nodes[1, plane] = fields[6, plane + 1]

    shift_x, shift_y, shift_z = scalars[0, 0], scalars[0, 1], scalars[0, 2]
    base = shift_x - 1

    def coefficients(plane):
        return lame_s[base + plane], shear_s[base + plane]

    def first_step(plane, forces):
        at = base + plane
        support, inverse = fields[6, at], inverse_s[at]
        for comp in range(3):
            value = forces[comp] + support * fields[comp, at]
            value = fields[3 + comp, at] - value
            resid[comp, plane] = value
            step_one[comp, plane] = inverse * value * FINE_FIRST

    def second_step(plane, forces):
        at = base + plane
        support, inverse = fields[6, at], inverse_s[at]
        for comp in range(3):
            step = step_one[comp, plane]
            value = resid[comp, plane] - (forces[comp] + support * step)
            resid[comp, plane] = value
            update = FINE_STEPS[0][0] * step + FINE_STEPS[0][1] * (inverse * value)
            step_two[comp, plane] = update
            sums_s[plane - 2, comp] = fields[comp, at] + step + update

    def last_step(plane, forces):
        support = fields[6, base + plane]
        for comp in range(3):
            value = forces[comp] + support * step_two[comp, plane]
            value = resid[comp, plane] - value
            remains[plane - 3, comp] = value
            carry[plane - 3, comp] = value[SENT]

    stencil(lambda comp, plane: fields[comp, base + plane], coefficients, 0, 8, first_step)
    stencil(lambda comp, plane: step_one[comp, plane], coefficients, 1, 7, second_step)
    stencil(lambda comp, plane: step_two[comp, plane], coefficients, 2, 6, last_step)
    for comp in range(3):
        smoothed[0, comp] = sums_s[0, comp]
        smoothed[1, comp] = sums_s[2 - shift_x, comp]
        smoothed[2, comp] = sums_s[3 - shift_x, comp]
        carry[3, comp] = sums_s[4 - shift_x, comp][SENT]

    total = [remains[0, comp] + remains[1, comp] + remains[2, comp] for comp in range(3)]
    moment = [remains[2, comp] - remains[0, comp] for comp in range(3)]
    row = lax.broadcasted_iota(jnp.int32, (ROWS, LANES), 0)
    plain = jnp.zeros((ROWS, LANES), jnp.float32)
    lever = jnp.zeros((ROWS, LANES), jnp.float32)
    for half in range(2):
        place = row - (ROW0 + 3 * half) - shift_y
        inside = (place >= 0) & (place < 3)
        arm = (place - 1).astype(jnp.float32)

        def summed(value):
            return jnp.sum(jnp.where(inside, value, 0.0), axis=0, keepdims=True)

        sums = [summed(total[comp]) for comp in range(3)]
        lines = sums + [
            summed(arm * total[2]),
            summed(-moment[2]),
            summed(moment[1] - arm * total[0]),
        ]
        for comp in range(6):
            plain = jnp.where(row == 8 * half + comp, lines[comp], plain)
        lever = jnp.where(row == 8 * half + 3, -sums[1], lever)
        lever = jnp.where(row == 8 * half + 4, sums[0], lever)
    fine = lax.broadcasted_iota(jnp.int32, (LANES, 128), 0)
    coarse = lax.broadcasted_iota(jnp.int32, (LANES, 128), 1)
    place = fine - 3 * coarse + 2 * shift_z - 10
    inside = (place >= 0) & (place < 3) & (coarse < COARSE_LANES)
    sums_z = jnp.where(inside, 1.0, 0.0)
    arms_z = jnp.where(inside, (place - 1).astype(jnp.float32), 0.0)
    result = picked_sums(plain, sums_z) + picked_sums(lever, arms_z)
    kinds = pltpu.roll(class_wide[...], shift_z + (128 - 14), 1)
    line = lax.broadcasted_iota(jnp.int32, (8, 128), 0)
    lane = lax.broadcasted_iota(jnp.int32, (8, 128), 1)
    low = jnp.where(line == 6, kinds[0:1], result[0:8])
    high = jnp.where(line == 6, kinds[1:2], result[8:16])
    packed = jnp.where(lane < 64, turned(low, -3, 1), turned(high, 61, 1))
    ends = jnp.zeros((1, 128), jnp.float32)
    lane_one = lane[0:1]
    for half in range(2):
        for comp in range(7):
            base = 12 * comp + 6 * half
            source = (low, high)[half][comp : comp + 1]
            ends = jnp.where(
                (lane_one >= base) & (lane_one < base + 3), turned(source, base, 1), ends
            )
            ends = jnp.where(
                (lane_one >= base + 3) & (lane_one < base + 6), turned(source, base - 64, 1), ends
            )
    packed = jnp.where(line == 7, ends, packed)
    for target in range(SIDE * SIDE):
        chunk[target] = packed


def coarse_kernel(
    scalars, tables, received, rest, low, smoothed, elements, nodes, displacement, correction, right,
    matrix, step_a, step_b, error, spread_y, spread_z, work, step, resid, near,
):
    shift_x, shift_y, shift_z = scalars[0, 0], scalars[0, 1], scalars[0, 2]
    mine_x, mine_y = scalars[0, 3], scalars[0, 4]
    lane = lax.broadcasted_iota(jnp.int32, (8, 128), 1)
    line = lax.broadcasted_iota(jnp.int32, (8, 128), 0)
    even = line < 4
    middle = (lane >= 3) & (lane < 67)
    odd_shift = lax.rem(shift_y, 2)
    turn_even = lax.rem(SIDE + 2 - mine_y, SIDE)
    turn_odd = lax.rem(SIDE + 6 - mine_y - odd_shift, SIDE)
    for at_x in range(SIDE):
        ends = received[pl.ds(64 * at_x + 7, 8, stride=8), :]
        ends = [pltpu.roll(ends, turn_even, 0), pltpu.roll(ends, turn_odd, 0)]
        for comp in range(7):
            main = received[pl.ds(64 * at_x + comp, 8, stride=8), :]
            main = [pltpu.roll(main, turn_even, 0), pltpu.roll(main, turn_odd, 0)]
            parts = []
            for which in range(2):
                half = odd_shift if which == 0 else 1 - odd_shift
                base = 12 * comp + 6 * half
                low_end = pltpu.roll(ends[which], lax.rem(128 - base, 128), 1)
                high_end = pltpu.roll(ends[which], lax.rem(192 - base, 128), 1)
                value = jnp.where(lane < 3, low_end, high_end)
                parts.append(jnp.where(middle, pltpu.roll(main[which], 3 + 64 * half, 1), value))
            value = jnp.where(even, parts[0], parts[1])
            right[comp, at_x] = jnp.where(lane < COARSE_LANES, value, 0.0)

    kinds = [right[6, spot].astype(jnp.int32) for spot in range(SIDE)]
    for entry in range(36):
        values = jnp.broadcast_to(tables[entry : entry + 1], (8, 128))
        for spot in range(SIDE):
            matrix[entry, spot] = jnp.take_along_axis(
                values, kinds[spot], axis=1, mode="promise_in_bounds"
            )

    def product(values, spot):
        result = []
        for i in range(6):
            total = matrix[6 * i, spot] * values[0]
            for j in range(1, 6):
                total = total + matrix[6 * i + j, spot] * values[j]
            result.append(total)
        return result

    def neighbours(source, spot, comp):
        value = source[comp, spot]
        faces = source[comp, (spot + 1) % SIDE] + source[comp, (spot - 1) % SIDE]
        faces = faces + turned(value, 4, 0)
        faces = faces + jnp.where(even, turned(value, -3, 0), turned(value, 3, 0))
        return faces + turned(value, 1, 1) + turned(value, -1, 1)

    for spot in range(SIDE):
        held = [right[comp, spot] for comp in range(6)]
        fresh = product(held, spot)
        for comp in range(6):
            step_a[comp, spot] = COARSE_FIRST * fresh[comp]
    scale_old, scale_new = COARSE_STEPS[0]
    for spot in range(SIDE):
        held = [right[comp, spot] for comp in range(6)]
        remains = []
        for comp in range(6):
            known = COARSE_FIRST * held[comp]
            value = held[comp] - (known - neighbours(step_a, spot, comp))
            remains.append(value)
            known = scale_old * known + scale_new * value
            right[comp, spot] = value - known
        fresh = product(remains, spot)
        for comp in range(6):
            step_b[comp, spot] = scale_old * step_a[comp, spot] + scale_new * fresh[comp]
    scale_old, scale_new = COARSE_STEPS[1]
    for spot in range(SIDE):
        remains = [right[comp, spot] + neighbours(step_b, spot, comp) for comp in range(6)]
        fresh = product(remains, spot)
        for comp in range(6):
            old = step_b[comp, spot]
            update = scale_old * old + scale_new * fresh[comp]
            error[comp, spot] = step_a[comp, spot] + old + update

    def window_row(inner):
        return 4 * lax.rem(inner, 2) + lax.div(inner, 2)

    for half in range(2):
        inner = window_row(half + shift_y + 2)
        for comp in range(6):
            value = error[comp, mine_x, pl.ds(inner, 1), :]
            value = pltpu.roll(jnp.broadcast_to(value, (8, 128)), 126 - shift_z, 1)
            correction[comp, 0, half : half + 1, :] = value[0:1, :COARSE_OWN]

    row = lax.broadcasted_iota(jnp.int32, (ROWS, 128), 0)
    for near_x in range(3):
        at_x = lax.rem(mine_x - shift_x + near_x + SIDE, SIDE)
        for comp in range(6):
            plane = error[comp, at_x]
            value = jnp.zeros((ROWS, 128), jnp.float32)
            for near_y in range(4):
                at = 4 * (near_y % 2) + near_y // 2 + 1
                inner = row - ROW0 - shift_y - 3 * (near_y - shift_y)
                value = jnp.where((inner >= 0) & (inner < 3), plane[at : at + 1], value)
            start = (comp * 3 + near_x) * ROWS
            spread_y[start : start + ROWS] = value
    coarse = lax.broadcasted_iota(jnp.int32, (128, LANES), 0)
    fine = lax.broadcasted_iota(jnp.int32, (128, LANES), 1)
    inner = fine - 3 * coarse + 2 * shift_z - 10
    copies = jnp.where((inner >= 0) & (inner < 3), 1.0, 0.0)
    wide = picked_sums(spread_y[...], copies)
    for which in range(18):
        spread_z[which] = wide[which * ROWS : (which + 1) * ROWS]

    row = lax.broadcasted_iota(jnp.int32, (ROWS, LANES), 0)
    fine = lax.broadcasted_iota(jnp.int32, (ROWS, LANES), 1)
    arm_y = (lax.rem(row + 4 - shift_y, 3) - 1).astype(jnp.float32)
    arm_z = (lax.rem(fine + 2 * shift_z + 2, 3) - 1).astype(jnp.float32)
    for plane in range(7):
        ahead = plane - 2 - shift_x + 6
        near_x = lax.div(ahead, 3) - 2 + shift_x
        arm_x = (lax.rem(ahead, 3) - 1).astype(jnp.float32)
        e = [spread_z[comp * 3 + near_x] for comp in range(6)]
        work[0, plane] = e[0] + e[4] * arm_z - e[5] * arm_y
        work[1, plane] = e[1] + e[5] * arm_x - e[3] * arm_z
        work[2, plane] = e[2] + e[3] * arm_y - e[4] * arm_x

    near[...] = jnp.zeros_like(near)
    near[:, :, SENT] = low[...]
    one = (shift_x == 1).astype(jnp.float32)
    two = 1.0 - one

    def remaining(at, comp):
        if at < 2:
            return near[at + 2 - shift_x, comp]
        if at == 2:
            return one * rest[0, comp] + two * near[2, comp]
        return rest[at - 1 - shift_x, comp]

    def first_step(plane, forces):
        at = plane - 1
        for comp in range(3):
            value = forces[comp] + nodes[1, at] * work[comp, plane]
            value = remaining(at, comp) - value
            resid[comp, at] = value
            step[comp, at] = nodes[0, at] * value * FINE_FIRST

    def last_step(plane, forces):
        for comp in range(3):
            old = step[comp, plane]
            value = resid[comp, plane] - (forces[comp] + nodes[1, plane] * old)
            update = FINE_STEPS[0][0] * old + FINE_STEPS[0][1] * (nodes[0, plane] * value)
            start = smoothed[plane - 1, comp]
            if plane == 1:
                start = one * start + two * near[3, comp]
            value = start + work[comp, plane + 1] + old + update
            displacement[comp, plane - 1] = value[
                ROW0 : ROW0 + OWN_Y, LANE0 : LANE0 + OWN_Z
            ]

    stencil(
        lambda comp, plane: work[comp, plane],
        lambda plane: (elements[0, plane], elements[1, plane]),
        0,
        6,
        first_step,
    )
    stencil(
        lambda comp, plane: step[comp, plane],
        lambda plane: (elements[0, plane + 1], elements[1, plane + 1]),
        0,
        4,
        last_step,
    )


def tables_kernel(blocks, tables):
    rows = []
    for i in range(6):
        row = [blocks[6 * i + j : 6 * i + j + 1] for j in range(6)]
        row[i] = row[i] + 6.0
        one = jnp.ones_like(row[0])
        rows.append(row + [one if i == j else jnp.zeros_like(one) for j in range(6)])
    for pivot in range(6):
        scaled = [value / rows[pivot][pivot] for value in rows[pivot]]
        for i in range(6):
            factor = rows[i][pivot]
            if i != pivot:
                rows[i] = [value - factor * line for value, line in zip(rows[i], scaled)]
        rows[pivot] = scaled
    tables[36:40] = jnp.zeros_like(tables[36:40])
    for i in range(6):
        for j in range(6):
            entry = 6 * i + j
            tables[entry : entry + 1] = rows[i][6 + j]


def passed_along(value, axis, steps):
    count = lax.axis_size(axis)
    pairs = [(source, (source + steps) % count) for source in range(count)]
    return lax.ppermute(value, axis, pairs)


VMEM = pl.BlockSpec(memory_space=pltpu.VMEM)
EDGES_VMEM = 64 * 1024 * 1024 - 512 * 1024


def call(kernel, arrays, shapes, scratch=(), work=1_000_000):
    return pl.pallas_call(
        kernel,
        out_shape=[jax.ShapeDtypeStruct(shape, jnp.float32) for shape in shapes],
        in_specs=[VMEM] * len(arrays),
        out_specs=[VMEM] * len(shapes),
        scratch_shapes=[pltpu.VMEM(shape, jnp.float32) for shape in scratch],
        compiler_params=pltpu.CompilerParams(vmem_limit_bytes=48 * 1024 * 1024),
        cost_estimate=pl.CostEstimate(flops=work, bytes_accessed=work, transcendentals=0),
    )(*arrays)


def pack_edges(*arrays):
    return pl.pallas_call(
        edges_kernel,
        out_shape=[jax.ShapeDtypeStruct((OWN_X, FIELDS, 128), jnp.float32)] * 2,
        in_specs=[pl.BlockSpec(memory_space=pltpu.HBM)] * len(arrays),
        out_specs=[VMEM] * 2,
        scratch_shapes=[pltpu.VMEM(array.shape, array.dtype) for array in arrays]
        + [pltpu.SemaphoreType.DMA((len(arrays),))],
        compiler_params=pltpu.CompilerParams(vmem_limit_bytes=EDGES_VMEM),
    )(*arrays)


def pack(*arrays):
    shapes = [(OWN_X * OWN_Y * 2 * FIELDS, 128), (8, 128)]
    return call(pack_kernel, arrays, shapes, work=20_000_000)


def widen(block, low, high, class_ext):
    shapes = [(OWN_X * OWN_Y * 2 * FIELDS, 128), (8, 128)]
    return call(widen_kernel, (block, low, high, class_ext), shapes)


def pre_smooth(moduli, scalars, planes, left, right, class_wide):
    plane = (ROWS, LANES)
    return call(
        pre_kernel,
        (moduli, scalars, planes, left, right, class_wide),
        [(SIDE * SIDE, 8, 128), (3, 3) + plane, (4, 3, 8, LANES), (3, 3) + plane]
        + [(2, 6) + plane, (2, 5) + plane],
        [(FIELDS, PLANES) + plane] + [(PLANES,) + plane] * 3
        + [(3, 9) + plane, (3, 9) + plane, (3, 9) + plane, (5, 3) + plane],
    )


def coarse_and_post(scalars, tables, received, rest, low, smoothed, elements, nodes):
    plane = (ROWS, LANES)
    spots = (SIDE, 8, 128)
    return call(
        coarse_kernel,
        (scalars, tables, received, rest, low, smoothed, elements, nodes),
        [(3, OWN_X, OWN_Y, OWN_Z), (6, 1, 2, COARSE_OWN)],
        [(7,) + spots, (36,) + spots, (6,) + spots, (6,) + spots, (6,) + spots]
        + [(18 * ROWS, 128), (18,) + plane, (3, 7) + plane, (3, 5) + plane, (3, 5) + plane]
        + [(4, 3) + plane],
    )


def coarse_tables(class_blocks):
    entries = jnp.transpose(class_blocks.reshape(8, 36))
    entries = jnp.pad(entries, ((0, 4), (0, 120)))
    return call(tables_kernel, (entries,), [(40, 128)])[0]


def body(forcing, initial_guess, material, moduli, support, offsets, aggregate_class, class_blocks):
    tables = coarse_tables(class_blocks)
    place = jnp.stack([lax.axis_index("gx"), lax.axis_index("gy")]).astype(jnp.int32)
    scalars = jnp.concatenate([offsets, place]).reshape(1, 5)
    arrays = (initial_guess, forcing, support, material, aggregate_class)
    low, high = pack_edges(*arrays)
    from_low = passed_along(high, "gz", 1)
    from_high = passed_along(low, "gz", -1)
    block, class_ext = pack(*arrays)
    own, class_wide = widen(block, from_low, from_high, class_ext)
    own = own.reshape(OWN_X, OWN_Y, 2 * FIELDS, 128)
    before = passed_along(own[1:], "gx", 1)
    after = passed_along(own, "gx", -1)
    beyond = own.reshape(-1, 2 * FIELDS, 128)[: 2 * OWN_Y + 1]
    beyond = passed_along(beyond, "gx", -2)[: 2 * OWN_Y].reshape(2, OWN_Y, 2 * FIELDS, 128)
    planes = jnp.concatenate([before, own, after, beyond], axis=0)
    left = passed_along(planes[:, 1:], "gy", 1).reshape(-1, 128)
    right = passed_along(planes[:, :5], "gy", -1).reshape(-1, 128)
    chunk, rest, carry, smoothed, elements, nodes = pre_smooth(
        moduli * (1.0 / 16.0), scalars, planes.reshape(-1, 128), left, right, class_wide
    )
    received = lax.all_to_all(chunk, ("gx", "gy"), 0, 0, tiled=True).reshape(-1, 128)
    from_before = passed_along(carry, "gx", 1)
    displacement, correction = coarse_and_post(
        scalars, tables, received, rest, from_before, smoothed, elements, nodes
    )
    return displacement, correction


def solution(mesh):
    placed = (
        P(None, "gx", "gy", "gz"),
        P(None, "gx", "gy", "gz"),
        P("gx", "gy", "gz"),
        P(),
        P("gx", "gy", "gz"),
        P(),
        P("gx", "gy", "gz"),
        P(),
    )
    return jax.shard_map(
        body,
        mesh=mesh,
        in_specs=placed,
        out_specs=(P(None, "gx", "gy", "gz"), P(None, "gx", "gy", "gz")),
        check_vma=False,
    )
```

```python
import jax
import jax.numpy as jnp
from jax import lax
from jax.experimental import pallas as pl
from jax.experimental.pallas import tpu as pltpu
from jax.sharding import PartitionSpec as P

FINE_LOW = 0.25
FINE_HIGH = 2.5
COARSE_LOW = 0.2
COARSE_HIGH = 1.9

ROWS = 16
LANES = 256
ROW0 = 5
LANE0 = 16
EDGE = 16
SENT = slice(4, 12)
PLANES = 10
OWN_X, OWN_Y, OWN_Z = 3, 6, 192
FIELDS = 8
SIDE = 8
COARSE_OWN = 64
COARSE_LANES = 70


def chebyshev(low, high, count):
    center = 0.5 * (high + low)
    spread = 0.5 * (high - low)
    ratio = center / spread
    weight = 1.0 / ratio
    steps = []
    for _ in range(1, count):
        following = 1.0 / (2.0 * ratio - weight)
        steps.append((following * weight, 2.0 * following / spread))
        weight = following
    return 1.0 / center, steps


FINE_FIRST, FINE_STEPS = chebyshev(FINE_LOW, FINE_HIGH, 2)
COARSE_FIRST, COARSE_STEPS = chebyshev(COARSE_LOW, COARSE_HIGH, 3)


def turned(value, shift, axis):
    shift = shift % value.shape[axis]
    return value if shift == 0 else pltpu.roll(value, shift, axis)


def following(value, axis):
    return turned(value, -1, axis)


def preceding(value, axis):
    return turned(value, 1, axis)


def plane_modes(value):
    ahead = following(value, 1)
    total, slope = value + ahead, ahead - value
    total_up, slope_up = following(total, 0), following(slope, 0)
    return {
        (0, 0): total + total_up,
        (1, 0): total_up - total,
        (0, 1): slope + slope_up,
        (1, 1): slope_up - slope,
    }


def element_modes(below, above, lame, shear):
    u = []
    for comp in range(3):
        modes = {}
        for key in ((0, 0), (1, 0), (0, 1), (1, 1)):
            first, second = below[comp][key], above[comp][key]
            if key != (0, 0):
                modes[(0,) + key] = first + second
            modes[(1,) + key] = second - first
        u.append(modes)
    x, y, z = u
    third = 1.0 / 3.0
    lame_b, shear_b = lame * third, shear * third
    shear_2 = shear + shear
    last = (lame + (shear_2 + shear_2)) * (1.0 / 9.0)
    f = [{}, {}, {}]
    divergence = lame * (x[1, 0, 0] + y[0, 1, 0] + z[0, 0, 1])
    f[0][1, 0, 0] = divergence + shear_2 * x[1, 0, 0]
    f[1][0, 1, 0] = divergence + shear_2 * y[0, 1, 0]
    f[2][0, 0, 1] = divergence + shear_2 * z[0, 0, 1]
    f[0][0, 1, 0] = f[1][1, 0, 0] = shear * (x[0, 1, 0] + y[1, 0, 0])
    f[0][0, 0, 1] = f[2][1, 0, 0] = shear * (x[0, 0, 1] + z[1, 0, 0])
    f[1][0, 0, 1] = f[2][0, 1, 0] = shear * (y[0, 0, 1] + z[0, 1, 0])
    for one, key_one, two, key_two in (
        (0, (1, 1, 0), 2, (0, 1, 1)),
        (0, (1, 0, 1), 1, (0, 1, 1)),
        (1, (1, 1, 0), 2, (1, 0, 1)),
    ):
        shared = lame_b * (u[one][key_one] + u[two][key_two])
        f[one][key_one] = shared + shear * u[one][key_one]
        f[two][key_two] = shared + shear * u[two][key_two]
    mixed = x[0, 1, 1] + y[1, 0, 1] + z[1, 1, 0]
    f[0][0, 1, 1] = shear_b * (mixed + x[0, 1, 1])
    f[1][1, 0, 1] = shear_b * (mixed + y[1, 0, 1])
    f[2][1, 1, 0] = shear_b * (mixed + z[1, 1, 0])
    for comp in range(3):
        f[comp][1, 1, 1] = last * u[comp][1, 1, 1]
    low, high = [], []
    for comp in range(3):
        down, up = {}, {}
        for key in ((0, 0), (1, 0), (0, 1), (1, 1)):
            slope = f[comp][(1,) + key]
            if key == (0, 0):
                down[key], up[key] = -slope, slope
            else:
                total = f[comp][(0,) + key]
                down[key], up[key] = total - slope, total + slope
        low.append(down)
        high.append(up)
    return low, high


def plane_forces(modes):
    parts = []
    for last in (0, 1):
        total, slope = modes[0, last], modes[1, last]
        parts.append((total - slope) + preceding(total + slope, 0))
    return (parts[0] - parts[1]) + preceding(parts[0] + parts[1], 1)


def stencil(read, elements, first, last, emit):
    below = [plane_modes(read(comp, first)) for comp in range(3)]
    carried = None
    for plane in range(first, last):
        above = [plane_modes(read(comp, plane + 1)) for comp in range(3)]
        low, high = element_modes(below, above, *elements(plane))
        if carried is not None:
            emit(
                plane,
                [
                    plane_forces({key: low[comp][key] + carried[comp][key] for key in low[comp]})
                    for comp in range(3)
                ],
            )
        below, carried = above, high


def picked_sums(values, weights):
    high = values.astype(jnp.bfloat16)
    left = values - high.astype(jnp.float32)
    middle = left.astype(jnp.bfloat16)
    low = (left - middle.astype(jnp.float32)).astype(jnp.bfloat16)
    weights = weights.astype(jnp.bfloat16)
    parts = [
        jnp.dot(part, weights, preferred_element_type=jnp.float32) for part in (low, middle, high)
    ]
    return (parts[0] + parts[1]) + parts[2]


def tile_row(plane, row, half):
    return ((plane * OWN_Y + row) * 2 + half) * FIELDS


def field_planes(guess, forcing, support, material, plane):
    for comp in range(3):
        yield comp, guess[comp, plane]
        yield 3 + comp, forcing[comp, plane]
    yield 6, support[plane]
    yield 7, material[plane].astype(jnp.float32)


def edges_kernel(
    guess_h, forcing_h, support_h, material_h, classes_h, low, high, guess, forcing, support, material,
    classes, done,
):
    pairs = (
        (guess_h, guess),
        (forcing_h, forcing),
        (support_h, support),
        (material_h, material),
        (classes_h, classes),
    )
    copies = [
        pltpu.make_async_copy(source, target, done.at[which])
        for which, (source, target) in enumerate(pairs)
    ]
    for copy in copies:
        copy.start()
    low[...] = jnp.zeros_like(low)
    high[...] = jnp.zeros_like(high)
    for copy in copies:
        copy.wait()
    kinds = classes[0].astype(jnp.float32)
    low[0, 0:2, 96:112] = kinds[:, 0:EDGE]
    high[0, 0:2, 96:112] = kinds[:, COARSE_OWN - EDGE :]
    for plane in range(OWN_X):
        for field, value in field_planes(guess, forcing, support, material, plane):
            for row in range(OWN_Y):
                line = value[row : row + 1]
                low[plane, field : field + 1, EDGE * row : EDGE * (row + 1)] = line[:, :EDGE]
                high[plane, field : field + 1, EDGE * row : EDGE * (row + 1)] = line[:, -EDGE:]


def pack_kernel(guess, forcing, support, material, classes, block, class_ext):
    first = 128 - LANE0
    block[...] = jnp.zeros_like(block)
    class_ext[...] = jnp.zeros_like(class_ext)
    class_ext[0:2, LANE0 : LANE0 + COARSE_OWN] = classes[0].astype(jnp.float32)
    for plane in range(OWN_X):
        for field, value in field_planes(guess, forcing, support, material, plane):
            for row in range(OWN_Y):
                line = value[row : row + 1]
                start = tile_row(plane, row, 0) + field
                block[start : start + 1, LANE0:128] = line[:, :first]
                start = tile_row(plane, row, 1) + field
                block[start : start + 1, 0 : OWN_Z - first] = line[:, first:]


def widen_kernel(block, low, high, class_ext, wide, class_wide, beyond):
    lane = lax.broadcasted_iota(jnp.int32, (8, 128), 1)
    end = LANE0 + OWN_Z - 128
    for plane in range(OWN_X):
        for row in range(OWN_Y):
            start = tile_row(plane, row, 0)
            wide[start : start + 8] = jnp.where(
                lane < LANE0, turned(low[plane], -EDGE * row, 1), block[start : start + 8]
            )
            start = tile_row(plane, row, 1)
            wide[start : start + 8] = jnp.where(
                (lane >= end) & (lane < end + EDGE),
                turned(high[plane], end - EDGE * row, 1),
                block[start : start + 8],
            )
    for row in range(OWN_Y):
        for half in range(2):
            start = tile_row(0, row, half)
            beyond[start : start + 8] = wide[start : start + 8]
            start = tile_row(1, row, half)
            beyond[start : start + 8] = turned(wide[start : start + 8], 3, 0)
    start = tile_row(2, 0, 0)
    beyond[start : start + 16] = jnp.zeros((16, 128), jnp.float32)
    end = LANE0 + COARSE_OWN
    value = jnp.where(lane < LANE0, turned(low[0], -96, 1), class_ext[...])
    class_wide[...] = jnp.where(
        (lane >= end) & (lane < end + EDGE), turned(high[0], end - 96, 1), value
    )


def pre_kernel(
    moduli, scalars, planes, left, right, class_wide, chunk, remains, carry, smoothed, elements, nodes,
    fields, lame_s, shear_s, inverse_s, resid, step_one, step_two, sums_s,
):
    for plane in range(PLANES):
        for field in range(FIELDS):
            if plane == 0 and 3 <= field < 7 or plane == PLANES - 1 and field >= 3:
                continue
            at, held = (0, field + 3) if plane == PLANES - 1 else (plane, field)
            for half in range(2):
                lanes = slice(128 * half, 128 * half + 128)
                fields[field, plane, 0:1, lanes] = jnp.zeros((1, 128), jnp.float32)
                start = (at * 4 * 2 + half) * FIELDS + held
                fields[field, plane, 1:5, lanes] = left[pl.ds(start, 4, stride=16), :]
                start = (at * 5 * 2 + half) * FIELDS + held
                fields[field, plane, 11:16, lanes] = right[pl.ds(start, 5, stride=16), :]
                start = tile_row(at, 0, half) + held
                fields[field, plane, 5:11, lanes] = planes[pl.ds(start, 6, stride=16), :]
    table = [
        [moduli[which : which + 1, kind : kind + 1] for kind in range(4)]
        for which in range(2)
    ]
    carried = None
    for plane in range(PLANES - 1):
        kind = fields[7, plane]
        picked = []
        for which in range(2):
            value = jnp.where(kind < 2.5, table[which][2], table[which][3])
            value = jnp.where(kind < 1.5, table[which][1], value)
            picked.append(jnp.where(kind < 0.5, table[which][0], value))
        lame_s[plane] = picked[0]
        shear_s[plane] = picked[1]
        weight = (picked[0] + 4.0 * picked[1]) * (16.0 / 9.0)
        weight = weight + preceding(weight, 1)
        weight = weight + preceding(weight, 0)
        if carried is not None:
            inverse_s[plane] = 1.0 / (fields[6, plane] + weight + carried)
        carried = weight
    for plane in range(6):
        elements[0, plane] = lame_s[plane]
        elements[1, plane] = shear_s[plane]
    for plane in range(5):
        nodes[0, plane] = inverse_s[plane + 1]
        nodes[1, plane] = fields[6, plane + 1]

    shift_x, shift_y, shift_z = scalars[0, 0], scalars[0, 1], scalars[0, 2]
    base = shift_x - 1

    def coefficients(plane):
        return lame_s[base + plane], shear_s[base + plane]

    def first_step(plane, forces):
        at = base + plane
        support, inverse = fields[6, at], inverse_s[at]
        for comp in range(3):
            value = forces[comp] + support * fields[comp, at]
            value = fields[3 + comp, at] - value
            resid[comp, plane] = value
            step_one[comp, plane] = inverse * value * FINE_FIRST

    def second_step(plane, forces):
        at = base + plane
        support, inverse = fields[6, at], inverse_s[at]
        for comp in range(3):
            step = step_one[comp, plane]
            value = resid[comp, plane] - (forces[comp] + support * step)
            resid[comp, plane] = value
            update = FINE_STEPS[0][0] * step + FINE_STEPS[0][1] * (inverse * value)
            step_two[comp, plane] = update
            sums_s[plane - 2, comp] = fields[comp, at] + step + update

    def last_step(plane, forces):
        support = fields[6, base + plane]
        for comp in range(3):
            value = forces[comp] + support * step_two[comp, plane]
            value = resid[comp, plane] - value
            remains[plane - 3, comp] = value
            carry[plane - 3, comp] = value[SENT]

    stencil(lambda comp, plane: fields[comp, base + plane], coefficients, 0, 8, first_step)
    stencil(lambda comp, plane: step_one[comp, plane], coefficients, 1, 7, second_step)
    stencil(lambda comp, plane: step_two[comp, plane], coefficients, 2, 6, last_step)
    for comp in range(3):
        smoothed[0, comp] = sums_s[0, comp]
        smoothed[1, comp] = sums_s[2 - shift_x, comp]
        smoothed[2, comp] = sums_s[3 - shift_x, comp]
        carry[3, comp] = sums_s[4 - shift_x, comp][SENT]

    total = [remains[0, comp] + remains[1, comp] + remains[2, comp] for comp in range(3)]
    moment = [remains[2, comp] - remains[0, comp] for comp in range(3)]
    row = lax.broadcasted_iota(jnp.int32, (ROWS, LANES), 0)
    plain = jnp.zeros((ROWS, LANES), jnp.float32)
    lever = jnp.zeros((ROWS, LANES), jnp.float32)
    for half in range(2):
        place = row - (ROW0 + 3 * half) - shift_y
        inside = (place >= 0) & (place < 3)
        arm = (place - 1).astype(jnp.float32)

        def summed(value):
            return jnp.sum(jnp.where(inside, value, 0.0), axis=0, keepdims=True)

        sums = [summed(total[comp]) for comp in range(3)]
        lines = sums + [
            summed(arm * total[2]),
            summed(-moment[2]),
            summed(moment[1] - arm * total[0]),
        ]
        for comp in range(6):
            plain = jnp.where(row == 8 * half + comp, lines[comp], plain)
        lever = jnp.where(row == 8 * half + 3, -sums[1], lever)
        lever = jnp.where(row == 8 * half + 4, sums[0], lever)
    fine = lax.broadcasted_iota(jnp.int32, (LANES, 128), 0)
    coarse = lax.broadcasted_iota(jnp.int32, (LANES, 128), 1)
    place = fine - 3 * coarse + 2 * shift_z - 10
    inside = (place >= 0) & (place < 3) & (coarse < COARSE_LANES)
    sums_z = jnp.where(inside, 1.0, 0.0)
    arms_z = jnp.where(inside, (place - 1).astype(jnp.float32), 0.0)
    result = picked_sums(plain, sums_z) + picked_sums(lever, arms_z)
    kinds = pltpu.roll(class_wide[...], shift_z + (128 - 14), 1)
    line = lax.broadcasted_iota(jnp.int32, (8, 128), 0)
    lane = lax.broadcasted_iota(jnp.int32, (8, 128), 1)
    low = jnp.where(line == 6, kinds[0:1], result[0:8])
    high = jnp.where(line == 6, kinds[1:2], result[8:16])
    packed = jnp.where(lane < 64, turned(low, -3, 1), turned(high, 61, 1))
    ends = jnp.zeros((1, 128), jnp.float32)
    lane_one = lane[0:1]
    for half in range(2):
        for comp in range(7):
            base = 12 * comp + 6 * half
            source = (low, high)[half][comp : comp + 1]
            ends = jnp.where(
                (lane_one >= base) & (lane_one < base + 3), turned(source, base, 1), ends
            )
            ends = jnp.where(
                (lane_one >= base + 3) & (lane_one < base + 6), turned(source, base - 64, 1), ends
            )
    packed = jnp.where(line == 7, ends, packed)
    for target in range(SIDE * SIDE):
        chunk[target] = packed


def coarse_kernel(
    scalars, tables, received, rest, low, smoothed, elements, nodes, displacement, correction, right,
    matrix, step_a, step_b, error, spread_y, spread_z, work, step, resid, near,
):
    shift_x, shift_y, shift_z = scalars[0, 0], scalars[0, 1], scalars[0, 2]
    mine_x, mine_y = scalars[0, 3], scalars[0, 4]
    lane = lax.broadcasted_iota(jnp.int32, (8, 128), 1)
    line = lax.broadcasted_iota(jnp.int32, (8, 128), 0)
    even = line < 4
    middle = (lane >= 3) & (lane < 67)
    odd_shift = lax.rem(shift_y, 2)
    turn_even = lax.rem(SIDE + 2 - mine_y, SIDE)
    turn_odd = lax.rem(SIDE + 6 - mine_y - odd_shift, SIDE)
    for at_x in range(SIDE):
        ends = received[pl.ds(64 * at_x + 7, 8, stride=8), :]
        ends = [pltpu.roll(ends, turn_even, 0), pltpu.roll(ends, turn_odd, 0)]
        for comp in range(7):
            main = received[pl.ds(64 * at_x + comp, 8, stride=8), :]
            main = [pltpu.roll(main, turn_even, 0), pltpu.roll(main, turn_odd, 0)]
            parts = []
            for which in range(2):
                half = odd_shift if which == 0 else 1 - odd_shift
                base = 12 * comp + 6 * half
                low_end = pltpu.roll(ends[which], lax.rem(128 - base, 128), 1)
                high_end = pltpu.roll(ends[which], lax.rem(192 - base, 128), 1)
                value = jnp.where(lane < 3, low_end, high_end)
                parts.append(jnp.where(middle, pltpu.roll(main[which], 3 + 64 * half, 1), value))
            value = jnp.where(even, parts[0], parts[1])
            right[comp, at_x] = jnp.where(lane < COARSE_LANES, value, 0.0)

    kinds = [right[6, spot].astype(jnp.int32) for spot in range(SIDE)]
    for entry in range(36):
        values = jnp.broadcast_to(tables[entry : entry + 1], (8, 128))
        for spot in range(SIDE):
            matrix[entry, spot] = jnp.take_along_axis(
                values, kinds[spot], axis=1, mode="promise_in_bounds"
            )

    def product(values, spot):
        result = []
        for i in range(6):
            total = matrix[6 * i, spot] * values[0]
            for j in range(1, 6):
                total = total + matrix[6 * i + j, spot] * values[j]
            result.append(total)
        return result

    def neighbours(source, spot, comp):
        value = source[comp, spot]
        faces = source[comp, (spot + 1) % SIDE] + source[comp, (spot - 1) % SIDE]
        faces = faces + turned(value, 4, 0)
        faces = faces + jnp.where(even, turned(value, -3, 0), turned(value, 3, 0))
        return faces + turned(value, 1, 1) + turned(value, -1, 1)

    for spot in range(SIDE):
        held = [right[comp, spot] for comp in range(6)]
        fresh = product(held, spot)
        for comp in range(6):
            step_a[comp, spot] = COARSE_FIRST * fresh[comp]
    scale_old, scale_new = COARSE_STEPS[0]
    for spot in range(SIDE):
        held = [right[comp, spot] for comp in range(6)]
        remains = []
        for comp in range(6):
            known = COARSE_FIRST * held[comp]
            value = held[comp] - (known - neighbours(step_a, spot, comp))
            remains.append(value)
            known = scale_old * known + scale_new * value
            right[comp, spot] = value - known
        fresh = product(remains, spot)
        for comp in range(6):
            step_b[comp, spot] = scale_old * step_a[comp, spot] + scale_new * fresh[comp]
    scale_old, scale_new = COARSE_STEPS[1]
    for spot in range(SIDE):
        remains = [right[comp, spot] + neighbours(step_b, spot, comp) for comp in range(6)]
        fresh = product(remains, spot)
        for comp in range(6):
            old = step_b[comp, spot]
            update = scale_old * old + scale_new * fresh[comp]
            error[comp, spot] = step_a[comp, spot] + old + update

    def window_row(inner):
        return 4 * lax.rem(inner, 2) + lax.div(inner, 2)

    for half in range(2):
        inner = window_row(half + shift_y + 2)
        for comp in range(6):
            value = error[comp, mine_x, pl.ds(inner, 1), :]
            value = pltpu.roll(jnp.broadcast_to(value, (8, 128)), 126 - shift_z, 1)
            correction[comp, 0, half : half + 1, :] = value[0:1, :COARSE_OWN]

    row = lax.broadcasted_iota(jnp.int32, (ROWS, 128), 0)
    for near_x in range(3):
        at_x = lax.rem(mine_x - shift_x + near_x + SIDE, SIDE)
        for comp in range(6):
            plane = error[comp, at_x]
            value = jnp.zeros((ROWS, 128), jnp.float32)
            for near_y in range(4):
                at = 4 * (near_y % 2) + near_y // 2 + 1
                inner = row - ROW0 - shift_y - 3 * (near_y - shift_y)
                value = jnp.where((inner >= 0) & (inner < 3), plane[at : at + 1], value)
            start = (comp * 3 + near_x) * ROWS
            spread_y[start : start + ROWS] = value
    coarse = lax.broadcasted_iota(jnp.int32, (128, LANES), 0)
    fine = lax.broadcasted_iota(jnp.int32, (128, LANES), 1)
    inner = fine - 3 * coarse + 2 * shift_z - 10
    copies = jnp.where((inner >= 0) & (inner < 3), 1.0, 0.0)
    wide = picked_sums(spread_y[...], copies)
    for which in range(18):
        spread_z[which] = wide[which * ROWS : (which + 1) * ROWS]

    row = lax.broadcasted_iota(jnp.int32, (ROWS, LANES), 0)
    fine = lax.broadcasted_iota(jnp.int32, (ROWS, LANES), 1)
    arm_y = (lax.rem(row + 4 - shift_y, 3) - 1).astype(jnp.float32)
    arm_z = (lax.rem(fine + 2 * shift_z + 2, 3) - 1).astype(jnp.float32)
    for plane in range(7):
        ahead = plane - 2 - shift_x + 6
        near_x = lax.div(ahead, 3) - 2 + shift_x
        arm_x = (lax.rem(ahead, 3) - 1).astype(jnp.float32)
        e = [spread_z[comp * 3 + near_x] for comp in range(6)]
        work[0, plane] = e[0] + e[4] * arm_z - e[5] * arm_y
        work[1, plane] = e[1] + e[5] * arm_x - e[3] * arm_z
        work[2, plane] = e[2] + e[3] * arm_y - e[4] * arm_x

    near[...] = jnp.zeros_like(near)
    near[:, :, SENT] = low[...]
    one = (shift_x == 1).astype(jnp.float32)
    two = 1.0 - one

    def remaining(at, comp):
        if at < 2:
            return near[at + 2 - shift_x, comp]
        if at == 2:
            return one * rest[0, comp] + two * near[2, comp]
        return rest[at - 1 - shift_x, comp]

    def first_step(plane, forces):
        at = plane - 1
        for comp in range(3):
            value = forces[comp] + nodes[1, at] * work[comp, plane]
            value = remaining(at, comp) - value
            resid[comp, at] = value
            step[comp, at] = nodes[0, at] * value * FINE_FIRST

    def last_step(plane, forces):
        for comp in range(3):
            old = step[comp, plane]
            value = resid[comp, plane] - (forces[comp] + nodes[1, plane] * old)
            update = FINE_STEPS[0][0] * old + FINE_STEPS[0][1] * (nodes[0, plane] * value)
            start = smoothed[plane - 1, comp]
            if plane == 1:
                start = one * start + two * near[3, comp]
            value = start + work[comp, plane + 1] + old + update
            displacement[comp, plane - 1] = value[
                ROW0 : ROW0 + OWN_Y, LANE0 : LANE0 + OWN_Z
            ]

    stencil(
        lambda comp, plane: work[comp, plane],
        lambda plane: (elements[0, plane], elements[1, plane]),
        0,
        6,
        first_step,
    )
    stencil(
        lambda comp, plane: step[comp, plane],
        lambda plane: (elements[0, plane + 1], elements[1, plane + 1]),
        0,
        4,
        last_step,
    )


def tables_kernel(blocks, tables):
    rows = []
    for i in range(6):
        row = [blocks[6 * i + j : 6 * i + j + 1] for j in range(6)]
        row[i] = row[i] + 6.0
        one = jnp.ones_like(row[0])
        rows.append(row + [one if i == j else jnp.zeros_like(one) for j in range(6)])
    for pivot in range(6):
        scaled = [value / rows[pivot][pivot] for value in rows[pivot]]
        for i in range(6):
            factor = rows[i][pivot]
            if i != pivot:
                rows[i] = [value - factor * line for value, line in zip(rows[i], scaled)]
        rows[pivot] = scaled
    tables[36:40] = jnp.zeros_like(tables[36:40])
    for i in range(6):
        for j in range(6):
            entry = 6 * i + j
            tables[entry : entry + 1] = rows[i][6 + j]


def passed_along(value, axis, steps):
    count = lax.axis_size(axis)
    pairs = [(source, (source + steps) % count) for source in range(count)]
    return lax.ppermute(value, axis, pairs)


VMEM = pl.BlockSpec(memory_space=pltpu.VMEM)
EDGES_VMEM = 64 * 1024 * 1024 - 512 * 1024


def call(kernel, arrays, shapes, scratch=(), work=1_000_000):
    return pl.pallas_call(
        kernel,
        out_shape=[jax.ShapeDtypeStruct(shape, jnp.float32) for shape in shapes],
        in_specs=[VMEM] * len(arrays),
        out_specs=[VMEM] * len(shapes),
        scratch_shapes=[pltpu.VMEM(shape, jnp.float32) for shape in scratch],
        compiler_params=pltpu.CompilerParams(vmem_limit_bytes=48 * 1024 * 1024),
        cost_estimate=pl.CostEstimate(flops=work, bytes_accessed=work, transcendentals=0),
    )(*arrays)


def pack_edges(*arrays):
    return pl.pallas_call(
        edges_kernel,
        out_shape=[jax.ShapeDtypeStruct((OWN_X, FIELDS, 128), jnp.float32)] * 2,
        in_specs=[pl.BlockSpec(memory_space=pltpu.HBM)] * len(arrays),
        out_specs=[VMEM] * 2,
        scratch_shapes=[pltpu.VMEM(array.shape, array.dtype) for array in arrays]
        + [pltpu.SemaphoreType.DMA((len(arrays),))],
        compiler_params=pltpu.CompilerParams(vmem_limit_bytes=EDGES_VMEM),
    )(*arrays)


def pack(*arrays):
    shapes = [(OWN_X * OWN_Y * 2 * FIELDS, 128), (8, 128)]
    return call(pack_kernel, arrays, shapes, work=20_000_000)


def widen(block, low, high, class_ext):
    shapes = [(OWN_X * OWN_Y * 2 * FIELDS, 128), (8, 128), ((2 * OWN_Y + 1) * 2 * FIELDS, 128)]
    return call(widen_kernel, (block, low, high, class_ext), shapes)


def pre_smooth(moduli, scalars, planes, left, right, class_wide):
    plane = (ROWS, LANES)
    return call(
        pre_kernel,
        (moduli, scalars, planes, left, right, class_wide),
        [(SIDE * SIDE, 8, 128), (3, 3) + plane, (4, 3, 8, LANES), (3, 3) + plane]
        + [(2, 6) + plane, (2, 5) + plane],
        [(FIELDS, PLANES) + plane] + [(PLANES,) + plane] * 3
        + [(3, 9) + plane, (3, 9) + plane, (3, 9) + plane, (5, 3) + plane],
    )


def coarse_and_post(scalars, tables, received, rest, low, smoothed, elements, nodes):
    plane = (ROWS, LANES)
    spots = (SIDE, 8, 128)
    return call(
        coarse_kernel,
        (scalars, tables, received, rest, low, smoothed, elements, nodes),
        [(3, OWN_X, OWN_Y, OWN_Z), (6, 1, 2, COARSE_OWN)],
        [(7,) + spots, (36,) + spots, (6,) + spots, (6,) + spots, (6,) + spots]
        + [(18 * ROWS, 128), (18,) + plane, (3, 7) + plane, (3, 5) + plane, (3, 5) + plane]
        + [(4, 3) + plane],
    )


def coarse_tables(class_blocks):
    entries = jnp.transpose(class_blocks.reshape(8, 36))
    entries = jnp.pad(entries, ((0, 4), (0, 120)))
    return call(tables_kernel, (entries,), [(40, 128)])[0]


def body(forcing, initial_guess, material, moduli, support, offsets, aggregate_class, class_blocks):
    tables = coarse_tables(class_blocks)
    place = jnp.stack([lax.axis_index("gx"), lax.axis_index("gy")]).astype(jnp.int32)
    scalars = jnp.concatenate([offsets, place]).reshape(1, 5)
    arrays = (initial_guess, forcing, support, material, aggregate_class)
    low, high = pack_edges(*arrays)
    from_low = passed_along(high, "gz", 1)
    from_high = passed_along(low, "gz", -1)
    block, class_ext = pack(*arrays)
    own, class_wide, beyond = widen(block, from_low, from_high, class_ext)
    own = own.reshape(OWN_X, OWN_Y, 2 * FIELDS, 128)
    before = passed_along(own[1:], "gx", 1)
    after = passed_along(own, "gx", -1)
    beyond = passed_along(beyond.reshape(-1, 2 * FIELDS, 128), "gx", -2)
    beyond = beyond[: 2 * OWN_Y].reshape(2, OWN_Y, 2 * FIELDS, 128)
    before, after = lax.optimization_barrier((before, after))
    field = lax.broadcasted_iota(jnp.int32, (OWN_Y, 2 * FIELDS, 128), 1) % FIELDS
    beyond = jnp.where(((field >= 3) & (field < 6))[None] | (jnp.arange(2) == 0)[:, None, None, None], beyond, 0.0)
    beyond = lax.optimization_barrier(beyond)
    mixed = jnp.where((field >= 3) & (field < 6), beyond[1], before[0])
    planes = jnp.concatenate([mixed[None], before[1:], own, after, beyond[:1]], axis=0)
    left = passed_along(planes[:, 2:], "gy", 1).reshape(-1, 128)
    right = passed_along(planes[:, :5], "gy", -1).reshape(-1, 128)
    chunk, rest, carry, smoothed, elements, nodes = pre_smooth(
        moduli * (1.0 / 16.0), scalars, planes.reshape(-1, 128), left, right, class_wide
    )
    received = lax.all_to_all(chunk, ("gx", "gy"), 0, 0, tiled=True).reshape(-1, 128)
    from_before = passed_along(carry, "gx", 1)
    displacement, correction = coarse_and_post(
        scalars, tables, received, rest, from_before, smoothed, elements, nodes
    )
    return displacement, correction


def solution(mesh):
    placed = (
        P(None, "gx", "gy", "gz"),
        P(None, "gx", "gy", "gz"),
        P("gx", "gy", "gz"),
        P(),
        P("gx", "gy", "gz"),
        P(),
        P("gx", "gy", "gz"),
        P(),
    )
    return jax.shard_map(
        body,
        mesh=mesh,
        in_specs=placed,
        out_specs=(P(None, "gx", "gy", "gz"), P(None, "gx", "gy", "gz")),
        check_vma=False,
    )
```

```python
import jax
import jax.numpy as jnp
from jax import lax
from jax.experimental import pallas as pl
from jax.experimental.pallas import tpu as pltpu
from jax.sharding import PartitionSpec as P

FINE_LOW = 0.25
FINE_HIGH = 2.5
COARSE_LOW = 0.2
COARSE_HIGH = 1.9

ROWS = 16
LANES = 256
ROW0 = 5
LANE0 = 16
EDGE = 16
SENT = slice(4, 12)
PLANES = 10
OWN_X, OWN_Y, OWN_Z = 3, 6, 192
FIELDS = 8
SIDE = 8
COARSE_OWN = 64
COARSE_LANES = 70


def chebyshev(low, high, count):
    center = 0.5 * (high + low)
    spread = 0.5 * (high - low)
    ratio = center / spread
    weight = 1.0 / ratio
    steps = []
    for _ in range(1, count):
        following = 1.0 / (2.0 * ratio - weight)
        steps.append((following * weight, 2.0 * following / spread))
        weight = following
    return 1.0 / center, steps


FINE_FIRST, FINE_STEPS = chebyshev(FINE_LOW, FINE_HIGH, 2)
COARSE_FIRST, COARSE_STEPS = chebyshev(COARSE_LOW, COARSE_HIGH, 3)


def turned(value, shift, axis):
    shift = shift % value.shape[axis]
    return value if shift == 0 else pltpu.roll(value, shift, axis)


def following(value, axis):
    return turned(value, -1, axis)


def preceding(value, axis):
    return turned(value, 1, axis)


def plane_modes(value):
    ahead = following(value, 1)
    total, slope = value + ahead, ahead - value
    total_up, slope_up = following(total, 0), following(slope, 0)
    return {
        (0, 0): total + total_up,
        (1, 0): total_up - total,
        (0, 1): slope + slope_up,
        (1, 1): slope_up - slope,
    }


def element_modes(below, above, lame, shear):
    u = []
    for comp in range(3):
        modes = {}
        for key in ((0, 0), (1, 0), (0, 1), (1, 1)):
            first, second = below[comp][key], above[comp][key]
            if key != (0, 0):
                modes[(0,) + key] = first + second
            modes[(1,) + key] = second - first
        u.append(modes)
    x, y, z = u
    third = 1.0 / 3.0
    lame_b, shear_b = lame * third, shear * third
    shear_2 = shear + shear
    last = (lame + (shear_2 + shear_2)) * (1.0 / 9.0)
    f = [{}, {}, {}]
    divergence = lame * (x[1, 0, 0] + y[0, 1, 0] + z[0, 0, 1])
    f[0][1, 0, 0] = divergence + shear_2 * x[1, 0, 0]
    f[1][0, 1, 0] = divergence + shear_2 * y[0, 1, 0]
    f[2][0, 0, 1] = divergence + shear_2 * z[0, 0, 1]
    f[0][0, 1, 0] = f[1][1, 0, 0] = shear * (x[0, 1, 0] + y[1, 0, 0])
    f[0][0, 0, 1] = f[2][1, 0, 0] = shear * (x[0, 0, 1] + z[1, 0, 0])
    f[1][0, 0, 1] = f[2][0, 1, 0] = shear * (y[0, 0, 1] + z[0, 1, 0])
    for one, key_one, two, key_two in (
        (0, (1, 1, 0), 2, (0, 1, 1)),
        (0, (1, 0, 1), 1, (0, 1, 1)),
        (1, (1, 1, 0), 2, (1, 0, 1)),
    ):
        shared = lame_b * (u[one][key_one] + u[two][key_two])
        f[one][key_one] = shared + shear * u[one][key_one]
        f[two][key_two] = shared + shear * u[two][key_two]
    mixed = x[0, 1, 1] + y[1, 0, 1] + z[1, 1, 0]
    f[0][0, 1, 1] = shear_b * (mixed + x[0, 1, 1])
    f[1][1, 0, 1] = shear_b * (mixed + y[1, 0, 1])
    f[2][1, 1, 0] = shear_b * (mixed + z[1, 1, 0])
    for comp in range(3):
        f[comp][1, 1, 1] = last * u[comp][1, 1, 1]
    low, high = [], []
    for comp in range(3):
        down, up = {}, {}
        for key in ((0, 0), (1, 0), (0, 1), (1, 1)):
            slope = f[comp][(1,) + key]
            if key == (0, 0):
                down[key], up[key] = -slope, slope
            else:
                total = f[comp][(0,) + key]
                down[key], up[key] = total - slope, total + slope
        low.append(down)
        high.append(up)
    return low, high


def plane_forces(modes):
    parts = []
    for last in (0, 1):
        total, slope = modes[0, last], modes[1, last]
        parts.append((total - slope) + preceding(total + slope, 0))
    return (parts[0] - parts[1]) + preceding(parts[0] + parts[1], 1)


def stencil(read, elements, first, last, emit):
    below = [plane_modes(read(comp, first)) for comp in range(3)]
    carried = None
    for plane in range(first, last):
        above = [plane_modes(read(comp, plane + 1)) for comp in range(3)]
        low, high = element_modes(below, above, *elements(plane))
        if carried is not None:
            emit(
                plane,
                [
                    plane_forces({key: low[comp][key] + carried[comp][key] for key in low[comp]})
                    for comp in range(3)
                ],
            )
        below, carried = above, high


def picked_sums(values, weights):
    high = values.astype(jnp.bfloat16)
    left = values - high.astype(jnp.float32)
    middle = left.astype(jnp.bfloat16)
    low = (left - middle.astype(jnp.float32)).astype(jnp.bfloat16)
    weights = weights.astype(jnp.bfloat16)
    parts = [
        jnp.dot(part, weights, preferred_element_type=jnp.float32) for part in (low, middle, high)
    ]
    return (parts[0] + parts[1]) + parts[2]


def tile_row(plane, row, half):
    return ((plane * OWN_Y + row) * 2 + half) * FIELDS


def field_planes(guess, forcing, support, material, plane):
    for comp in range(3):
        yield comp, guess[comp, plane]
        yield 3 + comp, forcing[comp, plane]
    yield 6, support[plane]
    yield 7, material[plane].astype(jnp.float32)


def edges_kernel(
    guess_h, forcing_h, support_h, material_h, classes_h, low, high, guess, forcing, support, material,
    classes, done,
):
    pairs = (
        (guess_h, guess),
        (forcing_h, forcing),
        (support_h, support),
        (material_h, material),
        (classes_h, classes),
    )
    copies = [
        pltpu.make_async_copy(source, target, done.at[which])
        for which, (source, target) in enumerate(pairs)
    ]
    for copy in copies:
        copy.start()
    low[...] = jnp.zeros_like(low)
    high[...] = jnp.zeros_like(high)
    for copy in copies:
        copy.wait()
    kinds = classes[0].astype(jnp.float32)
    low[0, 0:2, 96:112] = kinds[:, 0:EDGE]
    high[0, 0:2, 96:112] = kinds[:, COARSE_OWN - EDGE :]
    for plane in range(OWN_X):
        for field, value in field_planes(guess, forcing, support, material, plane):
            for row in range(OWN_Y):
                line = value[row : row + 1]
                low[plane, field : field + 1, EDGE * row : EDGE * (row + 1)] = line[:, :EDGE]
                high[plane, field : field + 1, EDGE * row : EDGE * (row + 1)] = line[:, -EDGE:]


def pack_kernel(guess, forcing, support, material, classes, block, class_ext):
    first = 128 - LANE0
    block[...] = jnp.zeros_like(block)
    class_ext[...] = jnp.zeros_like(class_ext)
    class_ext[0:2, LANE0 : LANE0 + COARSE_OWN] = classes[0].astype(jnp.float32)
    for plane in range(OWN_X):
        for field, value in field_planes(guess, forcing, support, material, plane):
            for row in range(OWN_Y):
                line = value[row : row + 1]
                start = tile_row(plane, row, 0) + field
                block[start : start + 1, LANE0:128] = line[:, :first]
                start = tile_row(plane, row, 1) + field
                block[start : start + 1, 0 : OWN_Z - first] = line[:, first:]


def widen_kernel(block, low, high, class_ext, wide, class_wide, beyond):
    lane = lax.broadcasted_iota(jnp.int32, (8, 128), 1)
    end = LANE0 + OWN_Z - 128
    for plane in range(OWN_X):
        for row in range(OWN_Y):
            start = tile_row(plane, row, 0)
            wide[start : start + 8] = jnp.where(
                lane < LANE0, turned(low[plane], -EDGE * row, 1), block[start : start + 8]
            )
            start = tile_row(plane, row, 1)
            wide[start : start + 8] = jnp.where(
                (lane >= end) & (lane < end + EDGE),
                turned(high[plane], end - EDGE * row, 1),
                block[start : start + 8],
            )
    for row in range(OWN_Y):
        for half in range(2):
            start = tile_row(0, row, half)
            beyond[start : start + 8] = wide[start : start + 8]
            start = tile_row(1, row, half)
            beyond[start : start + 8] = turned(wide[start : start + 8], 3, 0)
    end = LANE0 + COARSE_OWN
    value = jnp.where(lane < LANE0, turned(low[0], -96, 1), class_ext[...])
    class_wide[...] = jnp.where(
        (lane >= end) & (lane < end + EDGE), turned(high[0], end - 96, 1), value
    )


def pre_kernel(
    moduli, scalars, planes, left, right, class_wide, chunk, remains, carry, smoothed, elements, nodes,
    fields, lame_s, shear_s, inverse_s, resid, step_one, step_two, sums_s,
):
    for plane in range(PLANES):
        for field in range(FIELDS):
            if plane == 0 and 3 <= field < 7 or plane == PLANES - 1 and field >= 3:
                continue
            at, held = (0, field + 3) if plane == PLANES - 1 else (plane, field)
            for half in range(2):
                lanes = slice(128 * half, 128 * half + 128)
                fields[field, plane, 0:1, lanes] = jnp.zeros((1, 128), jnp.float32)
                start = (at * 4 * 2 + half) * FIELDS + held
                fields[field, plane, 1:5, lanes] = left[pl.ds(start, 4, stride=16), :]
                start = (at * 5 * 2 + half) * FIELDS + held
                fields[field, plane, 11:16, lanes] = right[pl.ds(start, 5, stride=16), :]
                start = tile_row(at, 0, half) + held
                fields[field, plane, 5:11, lanes] = planes[pl.ds(start, 6, stride=16), :]
    table = [
        [moduli[which : which + 1, kind : kind + 1] for kind in range(4)]
        for which in range(2)
    ]
    carried = None
    for plane in range(PLANES - 1):
        kind = fields[7, plane]
        picked = []
        for which in range(2):
            value = jnp.where(kind < 2.5, table[which][2], table[which][3])
            value = jnp.where(kind < 1.5, table[which][1], value)
            picked.append(jnp.where(kind < 0.5, table[which][0], value))
        lame_s[plane] = picked[0]
        shear_s[plane] = picked[1]
        weight = (picked[0] + 4.0 * picked[1]) * (16.0 / 9.0)
        weight = weight + preceding(weight, 1)
        weight = weight + preceding(weight, 0)
        if carried is not None:
            inverse_s[plane] = 1.0 / (fields[6, plane] + weight + carried)
        carried = weight
    for plane in range(6):
        elements[0, plane] = lame_s[plane]
        elements[1, plane] = shear_s[plane]
    for plane in range(5):
        nodes[0, plane] = inverse_s[plane + 1]
        nodes[1, plane] = fields[6, plane + 1]

    shift_x, shift_y, shift_z = scalars[0, 0], scalars[0, 1], scalars[0, 2]
    base = shift_x - 1

    def coefficients(plane):
        return lame_s[base + plane], shear_s[base + plane]

    def first_step(plane, forces):
        at = base + plane
        support, inverse = fields[6, at], inverse_s[at]
        for comp in range(3):
            value = forces[comp] + support * fields[comp, at]
            value = fields[3 + comp, at] - value
            resid[comp, plane] = value
            step_one[comp, plane] = inverse * value * FINE_FIRST

    def second_step(plane, forces):
        at = base + plane
        support, inverse = fields[6, at], inverse_s[at]
        for comp in range(3):
            step = step_one[comp, plane]
            value = resid[comp, plane] - (forces[comp] + support * step)
            resid[comp, plane] = value
            update = FINE_STEPS[0][0] * step + FINE_STEPS[0][1] * (inverse * value)
            step_two[comp, plane] = update
            sums_s[plane - 2, comp] = fields[comp, at] + step + update

    def last_step(plane, forces):
        support = fields[6, base + plane]
        for comp in range(3):
            value = forces[comp] + support * step_two[comp, plane]
            value = resid[comp, plane] - value
            remains[plane - 3, comp] = value
            carry[plane - 3, comp] = value[SENT]

    stencil(lambda comp, plane: fields[comp, base + plane], coefficients, 0, 8, first_step)
    stencil(lambda comp, plane: step_one[comp, plane], coefficients, 1, 7, second_step)
    stencil(lambda comp, plane: step_two[comp, plane], coefficients, 2, 6, last_step)
    for comp in range(3):
        smoothed[0, comp] = sums_s[0, comp]
        smoothed[1, comp] = sums_s[2 - shift_x, comp]
        smoothed[2, comp] = sums_s[3 - shift_x, comp]
        carry[3, comp] = sums_s[4 - shift_x, comp][SENT]

    total = [remains[0, comp] + remains[1, comp] + remains[2, comp] for comp in range(3)]
    moment = [remains[2, comp] - remains[0, comp] for comp in range(3)]
    row = lax.broadcasted_iota(jnp.int32, (ROWS, LANES), 0)
    plain = jnp.zeros((ROWS, LANES), jnp.float32)
    lever = jnp.zeros((ROWS, LANES), jnp.float32)
    for half in range(2):
        place = row - (ROW0 + 3 * half) - shift_y
        inside = (place >= 0) & (place < 3)
        arm = (place - 1).astype(jnp.float32)

        def summed(value):
            return jnp.sum(jnp.where(inside, value, 0.0), axis=0, keepdims=True)

        sums = [summed(total[comp]) for comp in range(3)]
        lines = sums + [
            summed(arm * total[2]),
            summed(-moment[2]),
            summed(moment[1] - arm * total[0]),
        ]
        for comp in range(6):
            plain = jnp.where(row == 8 * half + comp, lines[comp], plain)
        lever = jnp.where(row == 8 * half + 3, -sums[1], lever)
        lever = jnp.where(row == 8 * half + 4, sums[0], lever)
    fine = lax.broadcasted_iota(jnp.int32, (LANES, 128), 0)
    coarse = lax.broadcasted_iota(jnp.int32, (LANES, 128), 1)
    place = fine - 3 * coarse + 2 * shift_z - 10
    inside = (place >= 0) & (place < 3) & (coarse < COARSE_LANES)
    sums_z = jnp.where(inside, 1.0, 0.0)
    arms_z = jnp.where(inside, (place - 1).astype(jnp.float32), 0.0)
    result = picked_sums(plain, sums_z) + picked_sums(lever, arms_z)
    kinds = pltpu.roll(class_wide[...], shift_z + (128 - 14), 1)
    line = lax.broadcasted_iota(jnp.int32, (8, 128), 0)
    lane = lax.broadcasted_iota(jnp.int32, (8, 128), 1)
    low = jnp.where(line == 6, kinds[0:1], result[0:8])
    high = jnp.where(line == 6, kinds[1:2], result[8:16])
    packed = jnp.where(lane < 64, turned(low, -3, 1), turned(high, 61, 1))
    ends = jnp.zeros((1, 128), jnp.float32)
    lane_one = lane[0:1]
    for half in range(2):
        for comp in range(7):
            base = 6 * comp + 3 * half
            source = turned((low, high)[half][comp : comp + 1], base, 1)
            first = (lane_one >= base) & (lane_one < base + 3)
            last = (lane_one >= base + 67) & (lane_one < base + 70)
            ends = jnp.where(first | last, source, ends)
    packed = jnp.where(line == 7, ends, packed)
    for target in range(SIDE * SIDE):
        chunk[target] = packed


def coarse_kernel(
    scalars, tables, received, rest, low, smoothed, elements, nodes, displacement, correction, right,
    matrix, step_a, step_b, error, spread_y, spread_z, work, step, resid, near,
):
    shift_x, shift_y, shift_z = scalars[0, 0], scalars[0, 1], scalars[0, 2]
    mine_x, mine_y = scalars[0, 3], scalars[0, 4]
    lane = lax.broadcasted_iota(jnp.int32, (8, 128), 1)
    line = lax.broadcasted_iota(jnp.int32, (8, 128), 0)
    even = line < 4
    middle = (lane >= 3) & (lane < 67)
    odd_shift = lax.rem(shift_y, 2)
    turn_even = lax.rem(SIDE + 2 - mine_y, SIDE)
    turn_odd = lax.rem(SIDE + 6 - mine_y - odd_shift, SIDE)
    for at_x in range(SIDE):
        ends = received[pl.ds(64 * at_x + 7, 8, stride=8), :]
        ends = [pltpu.roll(ends, turn_even, 0), pltpu.roll(ends, turn_odd, 0)]
        for comp in range(7):
            main = received[pl.ds(64 * at_x + comp, 8, stride=8), :]
            main = [pltpu.roll(main, turn_even, 0), pltpu.roll(main, turn_odd, 0)]
            parts = []
            for which in range(2):
                half = odd_shift if which == 0 else 1 - odd_shift
                base = 6 * comp + 3 * half
                value = pltpu.roll(ends[which], lax.rem(128 - base, 128), 1)
                parts.append(jnp.where(middle, pltpu.roll(main[which], 3 + 64 * half, 1), value))
            value = jnp.where(even, parts[0], parts[1])
            right[comp, at_x] = jnp.where(lane < COARSE_LANES, value, 0.0)

    kinds = [right[6, spot].astype(jnp.int32) for spot in range(SIDE)]
    for entry in range(36):
        values = jnp.broadcast_to(tables[entry : entry + 1], (8, 128))
        for spot in range(SIDE):
            matrix[entry, spot] = jnp.take_along_axis(
                values, kinds[spot], axis=1, mode="promise_in_bounds"
            )

    def product(values, spot):
        result = []
        for i in range(6):
            total = matrix[6 * i, spot] * values[0]
            for j in range(1, 6):
                total = total + matrix[6 * i + j, spot] * values[j]
            result.append(total)
        return result

    def neighbours(source, spot, comp):
        value = source[comp, spot]
        faces = source[comp, (spot + 1) % SIDE] + source[comp, (spot - 1) % SIDE]
        faces = faces + turned(value, 4, 0)
        faces = faces + jnp.where(even, turned(value, -3, 0), turned(value, 3, 0))
        return faces + turned(value, 1, 1) + turned(value, -1, 1)

    for spot in range(SIDE):
        held = [right[comp, spot] for comp in range(6)]
        fresh = product(held, spot)
        for comp in range(6):
            step_a[comp, spot] = COARSE_FIRST * fresh[comp]
    scale_old, scale_new = COARSE_STEPS[0]
    for spot in range(SIDE):
        held = [right[comp, spot] for comp in range(6)]
        remains = []
        for comp in range(6):
            known = COARSE_FIRST * held[comp]
            value = held[comp] - (known - neighbours(step_a, spot, comp))
            remains.append(value)
            known = scale_old * known + scale_new * value
            right[comp, spot] = value - known
        fresh = product(remains, spot)
        for comp in range(6):
            step_b[comp, spot] = scale_old * step_a[comp, spot] + scale_new * fresh[comp]
    scale_old, scale_new = COARSE_STEPS[1]
    for spot in range(SIDE):
        remains = [right[comp, spot] + neighbours(step_b, spot, comp) for comp in range(6)]
        fresh = product(remains, spot)
        for comp in range(6):
            old = step_b[comp, spot]
            update = scale_old * old + scale_new * fresh[comp]
            error[comp, spot] = step_a[comp, spot] + old + update

    def window_row(inner):
        return 4 * lax.rem(inner, 2) + lax.div(inner, 2)

    for half in range(2):
        inner = window_row(half + shift_y + 2)
        for comp in range(6):
            value = error[comp, mine_x, pl.ds(inner, 1), :]
            value = pltpu.roll(jnp.broadcast_to(value, (8, 128)), 126 - shift_z, 1)
            correction[comp, 0, half : half + 1, :] = value[0:1, :COARSE_OWN]

    row = lax.broadcasted_iota(jnp.int32, (ROWS, 128), 0)
    for near_x in range(3):
        at_x = lax.rem(mine_x - shift_x + near_x + SIDE, SIDE)
        for comp in range(6):
            plane = error[comp, at_x]
            value = jnp.zeros((ROWS, 128), jnp.float32)
            for near_y in range(4):
                at = 4 * (near_y % 2) + near_y // 2 + 1
                inner = row - ROW0 - shift_y - 3 * (near_y - shift_y)
                value = jnp.where((inner >= 0) & (inner < 3), plane[at : at + 1], value)
            start = (comp * 3 + near_x) * ROWS
            spread_y[start : start + ROWS] = value
    coarse = lax.broadcasted_iota(jnp.int32, (128, LANES), 0)
    fine = lax.broadcasted_iota(jnp.int32, (128, LANES), 1)
    inner = fine - 3 * coarse + 2 * shift_z - 10
    copies = jnp.where((inner >= 0) & (inner < 3), 1.0, 0.0)
    wide = picked_sums(spread_y[...], copies)
    for which in range(18):
        spread_z[which] = wide[which * ROWS : (which + 1) * ROWS]

    row = lax.broadcasted_iota(jnp.int32, (ROWS, LANES), 0)
    fine = lax.broadcasted_iota(jnp.int32, (ROWS, LANES), 1)
    arm_y = (lax.rem(row + 4 - shift_y, 3) - 1).astype(jnp.float32)
    arm_z = (lax.rem(fine + 2 * shift_z + 2, 3) - 1).astype(jnp.float32)
    for plane in range(7):
        ahead = plane - 2 - shift_x + 6
        near_x = lax.div(ahead, 3) - 2 + shift_x
        arm_x = (lax.rem(ahead, 3) - 1).astype(jnp.float32)
        e = [spread_z[comp * 3 + near_x] for comp in range(6)]
        work[0, plane] = e[0] + e[4] * arm_z - e[5] * arm_y
        work[1, plane] = e[1] + e[5] * arm_x - e[3] * arm_z
        work[2, plane] = e[2] + e[3] * arm_y - e[4] * arm_x

    near[...] = jnp.zeros_like(near)
    near[:, :, SENT] = low[...]
    one = (shift_x == 1).astype(jnp.float32)
    two = 1.0 - one

    def remaining(at, comp):
        if at < 2:
            return near[at + 2 - shift_x, comp]
        if at == 2:
            return one * rest[0, comp] + two * near[2, comp]
        return rest[at - 1 - shift_x, comp]

    def first_step(plane, forces):
        at = plane - 1
        for comp in range(3):
            value = forces[comp] + nodes[1, at] * work[comp, plane]
            value = remaining(at, comp) - value
            resid[comp, at] = value
            step[comp, at] = nodes[0, at] * value * FINE_FIRST

    def last_step(plane, forces):
        for comp in range(3):
            old = step[comp, plane]
            value = resid[comp, plane] - (forces[comp] + nodes[1, plane] * old)
            update = FINE_STEPS[0][0] * old + FINE_STEPS[0][1] * (nodes[0, plane] * value)
            start = smoothed[plane - 1, comp]
            if plane == 1:
                start = one * start + two * near[3, comp]
            value = start + work[comp, plane + 1] + old + update
            displacement[comp, plane - 1] = value[
                ROW0 : ROW0 + OWN_Y, LANE0 : LANE0 + OWN_Z
            ]

    stencil(
        lambda comp, plane: work[comp, plane],
        lambda plane: (elements[0, plane], elements[1, plane]),
        0,
        6,
        first_step,
    )
    stencil(
        lambda comp, plane: step[comp, plane],
        lambda plane: (elements[0, plane + 1], elements[1, plane + 1]),
        0,
        4,
        last_step,
    )


def tables_kernel(blocks, tables):
    rows = []
    for i in range(6):
        row = [blocks[6 * i + j : 6 * i + j + 1] for j in range(6)]
        row[i] = row[i] + 6.0
        one = jnp.ones_like(row[0])
        rows.append(row + [one if i == j else jnp.zeros_like(one) for j in range(6)])
    for pivot in range(6):
        scaled = [value / rows[pivot][pivot] for value in rows[pivot]]
        for i in range(6):
            factor = rows[i][pivot]
            if i != pivot:
                rows[i] = [value - factor * line for value, line in zip(rows[i], scaled)]
        rows[pivot] = scaled
    tables[36:40] = jnp.zeros_like(tables[36:40])
    for i in range(6):
        for j in range(6):
            entry = 6 * i + j
            tables[entry : entry + 1] = rows[i][6 + j]


def passed_along(value, axis, steps):
    count = lax.axis_size(axis)
    pairs = [(source, (source + steps) % count) for source in range(count)]
    return lax.ppermute(value, axis, pairs)


VMEM = pl.BlockSpec(memory_space=pltpu.VMEM)
EDGES_VMEM = 64 * 1024 * 1024 - 512 * 1024


def call(kernel, arrays, shapes, scratch=(), work=1_000_000):
    return pl.pallas_call(
        kernel,
        out_shape=[jax.ShapeDtypeStruct(shape, jnp.float32) for shape in shapes],
        in_specs=[VMEM] * len(arrays),
        out_specs=[VMEM] * len(shapes),
        scratch_shapes=[pltpu.VMEM(shape, jnp.float32) for shape in scratch],
        compiler_params=pltpu.CompilerParams(vmem_limit_bytes=48 * 1024 * 1024),
        cost_estimate=pl.CostEstimate(flops=work, bytes_accessed=work, transcendentals=0),
    )(*arrays)


def pack_edges(*arrays):
    return pl.pallas_call(
        edges_kernel,
        out_shape=[jax.ShapeDtypeStruct((OWN_X, FIELDS, 128), jnp.float32)] * 2,
        in_specs=[pl.BlockSpec(memory_space=pltpu.HBM)] * len(arrays),
        out_specs=[VMEM] * 2,
        scratch_shapes=[pltpu.VMEM(array.shape, array.dtype) for array in arrays]
        + [pltpu.SemaphoreType.DMA((len(arrays),))],
        compiler_params=pltpu.CompilerParams(vmem_limit_bytes=EDGES_VMEM),
    )(*arrays)


def pack(*arrays):
    shapes = [(OWN_X * OWN_Y * 2 * FIELDS, 128), (8, 128)]
    return call(pack_kernel, arrays, shapes, work=20_000_000)


def widen(block, low, high, class_ext):
    shapes = [(OWN_X * OWN_Y * 2 * FIELDS, 128), (8, 128), (2 * OWN_Y * 2 * FIELDS, 128)]
    return call(widen_kernel, (block, low, high, class_ext), shapes)


def pre_smooth(moduli, scalars, planes, left, right, class_wide):
    plane = (ROWS, LANES)
    return call(
        pre_kernel,
        (moduli, scalars, planes, left, right, class_wide),
        [(SIDE * SIDE, 8, 128), (3, 3) + plane, (4, 3, 8, LANES), (3, 3) + plane]
        + [(2, 6) + plane, (2, 5) + plane],
        [(FIELDS, PLANES) + plane] + [(PLANES,) + plane] * 3
        + [(3, 9) + plane, (3, 9) + plane, (3, 9) + plane, (5, 3) + plane],
    )


def coarse_and_post(scalars, tables, received, rest, low, smoothed, elements, nodes):
    plane = (ROWS, LANES)
    spots = (SIDE, 8, 128)
    return call(
        coarse_kernel,
        (scalars, tables, received, rest, low, smoothed, elements, nodes),
        [(3, OWN_X, OWN_Y, OWN_Z), (6, 1, 2, COARSE_OWN)],
        [(7,) + spots, (36,) + spots, (6,) + spots, (6,) + spots, (6,) + spots]
        + [(18 * ROWS, 128), (18,) + plane, (3, 7) + plane, (3, 5) + plane, (3, 5) + plane]
        + [(4, 3) + plane],
    )


def coarse_tables(class_blocks):
    entries = jnp.transpose(class_blocks.reshape(8, 36))
    entries = jnp.pad(entries, ((0, 4), (0, 120)))
    return call(tables_kernel, (entries,), [(40, 128)])[0]


def body(forcing, initial_guess, material, moduli, support, offsets, aggregate_class, class_blocks):
    tables = coarse_tables(class_blocks)
    place = jnp.stack([lax.axis_index("gx"), lax.axis_index("gy")]).astype(jnp.int32)
    scalars = jnp.concatenate([offsets, place]).reshape(1, 5)
    arrays = (initial_guess, forcing, support, material, aggregate_class)
    low, high = pack_edges(*arrays)
    from_low = passed_along(high, "gz", 1)
    from_high = passed_along(low, "gz", -1)
    block, class_ext = pack(*arrays)
    own, class_wide, beyond = widen(block, from_low, from_high, class_ext)
    own = own.reshape(OWN_X, OWN_Y, 2 * FIELDS, 128)
    before = passed_along(own[1:], "gx", 1)
    after = passed_along(own, "gx", -1)
    beyond = passed_along(beyond.reshape(2, OWN_Y, 2 * FIELDS, 128), "gx", -2)
    before, after = lax.optimization_barrier((before, after))
    field = lax.broadcasted_iota(jnp.int32, (OWN_Y, 2 * FIELDS, 128), 1) % FIELDS
    beyond = jnp.where(((field >= 3) & (field < 6))[None] | (jnp.arange(2) == 0)[:, None, None, None], beyond, 0.0)
    beyond = lax.optimization_barrier(beyond)
    mixed = jnp.where((field >= 3) & (field < 6), beyond[1], before[0])
    planes = jnp.concatenate([mixed[None], before[1:], own, after, beyond[:1]], axis=0)
    left = passed_along(planes[:, 2:], "gy", 1).reshape(-1, 128)
    right = passed_along(planes[:, :5], "gy", -1).reshape(-1, 128)
    chunk, rest, carry, smoothed, elements, nodes = pre_smooth(
        moduli * (1.0 / 16.0), scalars, planes.reshape(-1, 128), left, right, class_wide
    )
    received = lax.all_to_all(chunk, ("gx", "gy"), 0, 0, tiled=True).reshape(-1, 128)
    from_before = passed_along(carry, "gx", 1)
    displacement, correction = coarse_and_post(
        scalars, tables, received, rest, from_before, smoothed, elements, nodes
    )
    return displacement, correction


def solution(mesh):
    placed = (
        P(None, "gx", "gy", "gz"),
        P(None, "gx", "gy", "gz"),
        P("gx", "gy", "gz"),
        P(),
        P("gx", "gy", "gz"),
        P(),
        P("gx", "gy", "gz"),
        P(),
    )
    return jax.shard_map(
        body,
        mesh=mesh,
        in_specs=placed,
        out_specs=(P(None, "gx", "gy", "gz"), P(None, "gx", "gy", "gz")),
        check_vma=False,
    )
```

```python
import jax
import jax.numpy as jnp
from jax import lax
from jax.experimental import pallas as pl
from jax.experimental.pallas import tpu as pltpu
from jax.sharding import PartitionSpec as P

FINE_LOW = 0.25
FINE_HIGH = 2.5
COARSE_LOW = 0.2
COARSE_HIGH = 1.9

ROWS = 16
LANES = 256
ROW0 = 5
LANE0 = 16
EDGE = 16
SENT = slice(4, 12)
PLANES = 10
OWN_X, OWN_Y, OWN_Z = 3, 6, 192
FIELDS = 8
SIDE = 8
SPOTS = 7
COARSE_OWN = 64
COARSE_LANES = 70


def chebyshev(low, high, count):
    center = 0.5 * (high + low)
    spread = 0.5 * (high - low)
    ratio = center / spread
    weight = 1.0 / ratio
    steps = []
    for _ in range(1, count):
        following = 1.0 / (2.0 * ratio - weight)
        steps.append((following * weight, 2.0 * following / spread))
        weight = following
    return 1.0 / center, steps


FINE_FIRST, FINE_STEPS = chebyshev(FINE_LOW, FINE_HIGH, 2)
COARSE_FIRST, COARSE_STEPS = chebyshev(COARSE_LOW, COARSE_HIGH, 3)


def turned(value, shift, axis):
    shift = shift % value.shape[axis]
    return value if shift == 0 else pltpu.roll(value, shift, axis)


def following(value, axis):
    return turned(value, -1, axis)


def preceding(value, axis):
    return turned(value, 1, axis)


def plane_modes(value):
    ahead = following(value, 1)
    total, slope = value + ahead, ahead - value
    total_up, slope_up = following(total, 0), following(slope, 0)
    return {
        (0, 0): total + total_up,
        (1, 0): total_up - total,
        (0, 1): slope + slope_up,
        (1, 1): slope_up - slope,
    }


def element_modes(below, above, lame, shear):
    u = []
    for comp in range(3):
        modes = {}
        for key in ((0, 0), (1, 0), (0, 1), (1, 1)):
            first, second = below[comp][key], above[comp][key]
            if key != (0, 0):
                modes[(0,) + key] = first + second
            modes[(1,) + key] = second - first
        u.append(modes)
    x, y, z = u
    third = 1.0 / 3.0
    lame_b, shear_b = lame * third, shear * third
    shear_2 = shear + shear
    last = (lame + (shear_2 + shear_2)) * (1.0 / 9.0)
    f = [{}, {}, {}]
    divergence = lame * (x[1, 0, 0] + y[0, 1, 0] + z[0, 0, 1])
    f[0][1, 0, 0] = divergence + shear_2 * x[1, 0, 0]
    f[1][0, 1, 0] = divergence + shear_2 * y[0, 1, 0]
    f[2][0, 0, 1] = divergence + shear_2 * z[0, 0, 1]
    f[0][0, 1, 0] = f[1][1, 0, 0] = shear * (x[0, 1, 0] + y[1, 0, 0])
    f[0][0, 0, 1] = f[2][1, 0, 0] = shear * (x[0, 0, 1] + z[1, 0, 0])
    f[1][0, 0, 1] = f[2][0, 1, 0] = shear * (y[0, 0, 1] + z[0, 1, 0])
    for one, key_one, two, key_two in (
        (0, (1, 1, 0), 2, (0, 1, 1)),
        (0, (1, 0, 1), 1, (0, 1, 1)),
        (1, (1, 1, 0), 2, (1, 0, 1)),
    ):
        shared = lame_b * (u[one][key_one] + u[two][key_two])
        f[one][key_one] = shared + shear * u[one][key_one]
        f[two][key_two] = shared + shear * u[two][key_two]
    mixed = x[0, 1, 1] + y[1, 0, 1] + z[1, 1, 0]
    f[0][0, 1, 1] = shear_b * (mixed + x[0, 1, 1])
    f[1][1, 0, 1] = shear_b * (mixed + y[1, 0, 1])
    f[2][1, 1, 0] = shear_b * (mixed + z[1, 1, 0])
    for comp in range(3):
        f[comp][1, 1, 1] = last * u[comp][1, 1, 1]
    low, high = [], []
    for comp in range(3):
        down, up = {}, {}
        for key in ((0, 0), (1, 0), (0, 1), (1, 1)):
            slope = f[comp][(1,) + key]
            if key == (0, 0):
                down[key], up[key] = -slope, slope
            else:
                total = f[comp][(0,) + key]
                down[key], up[key] = total - slope, total + slope
        low.append(down)
        high.append(up)
    return low, high


def plane_forces(modes):
    parts = []
    for last in (0, 1):
        total, slope = modes[0, last], modes[1, last]
        parts.append((total - slope) + preceding(total + slope, 0))
    return (parts[0] - parts[1]) + preceding(parts[0] + parts[1], 1)


def stencil(read, elements, first, last, emit):
    below = [plane_modes(read(comp, first)) for comp in range(3)]
    carried = None
    for plane in range(first, last):
        above = [plane_modes(read(comp, plane + 1)) for comp in range(3)]
        low, high = element_modes(below, above, *elements(plane))
        if carried is not None:
            emit(
                plane,
                [
                    plane_forces({key: low[comp][key] + carried[comp][key] for key in low[comp]})
                    for comp in range(3)
                ],
            )
        below, carried = above, high


def picked_sums(values, weights):
    high = values.astype(jnp.bfloat16)
    left = values - high.astype(jnp.float32)
    middle = left.astype(jnp.bfloat16)
    low = (left - middle.astype(jnp.float32)).astype(jnp.bfloat16)
    weights = weights.astype(jnp.bfloat16)
    parts = [
        jnp.dot(part, weights, preferred_element_type=jnp.float32) for part in (low, middle, high)
    ]
    return (parts[0] + parts[1]) + parts[2]


def tile_row(plane, row, half):
    return ((plane * OWN_Y + row) * 2 + half) * FIELDS


def field_planes(guess, forcing, support, material, plane):
    for comp in range(3):
        yield comp, guess[comp, plane]
        yield 3 + comp, forcing[comp, plane]
    yield 6, support[plane]
    yield 7, material[plane].astype(jnp.float32)


def edges_kernel(
    guess_h, forcing_h, support_h, material_h, classes_h, low, high, guess, forcing, support, material,
    classes, done,
):
    pairs = (
        (guess_h, guess),
        (forcing_h, forcing),
        (support_h, support),
        (material_h, material),
        (classes_h, classes),
    )
    copies = [
        pltpu.make_async_copy(source, target, done.at[which])
        for which, (source, target) in enumerate(pairs)
    ]
    for copy in copies:
        copy.start()
    low[...] = jnp.zeros_like(low)
    high[...] = jnp.zeros_like(high)
    for copy in copies:
        copy.wait()
    kinds = classes[0].astype(jnp.float32)
    low[0, 0:2, 96:112] = kinds[:, 0:EDGE]
    high[0, 0:2, 96:112] = kinds[:, COARSE_OWN - EDGE :]
    for plane in range(OWN_X):
        for field, value in field_planes(guess, forcing, support, material, plane):
            for row in range(OWN_Y):
                line = value[row : row + 1]
                low[plane, field : field + 1, EDGE * row : EDGE * (row + 1)] = line[:, :EDGE]
                high[plane, field : field + 1, EDGE * row : EDGE * (row + 1)] = line[:, -EDGE:]


def pack_kernel(guess, forcing, support, material, classes, block, class_ext):
    first = 128 - LANE0
    block[...] = jnp.zeros_like(block)
    class_ext[...] = jnp.zeros_like(class_ext)
    class_ext[0:2, LANE0 : LANE0 + COARSE_OWN] = classes[0].astype(jnp.float32)
    for plane in range(OWN_X):
        for field, value in field_planes(guess, forcing, support, material, plane):
            for row in range(OWN_Y):
                line = value[row : row + 1]
                start = tile_row(plane, row, 0) + field
                block[start : start + 1, LANE0:128] = line[:, :first]
                start = tile_row(plane, row, 1) + field
                block[start : start + 1, 0 : OWN_Z - first] = line[:, first:]


def widen_kernel(block, low, high, class_ext, wide, class_wide, beyond):
    lane = lax.broadcasted_iota(jnp.int32, (8, 128), 1)
    end = LANE0 + OWN_Z - 128
    for plane in range(OWN_X):
        for row in range(OWN_Y):
            start = tile_row(plane, row, 0)
            wide[start : start + 8] = jnp.where(
                lane < LANE0, turned(low[plane], -EDGE * row, 1), block[start : start + 8]
            )
            start = tile_row(plane, row, 1)
            wide[start : start + 8] = jnp.where(
                (lane >= end) & (lane < end + EDGE),
                turned(high[plane], end - EDGE * row, 1),
                block[start : start + 8],
            )
    for row in range(OWN_Y):
        for half in range(2):
            start = tile_row(0, row, half)
            beyond[start : start + 8] = wide[start : start + 8]
            start = tile_row(1, row, half)
            beyond[start : start + 8] = turned(wide[start : start + 8], 3, 0)
    end = LANE0 + COARSE_OWN
    value = jnp.where(lane < LANE0, turned(low[0], -96, 1), class_ext[...])
    class_wide[...] = jnp.where(
        (lane >= end) & (lane < end + EDGE), turned(high[0], end - 96, 1), value
    )


def pre_kernel(
    moduli, scalars, planes, left, right, class_wide, chunk, remains, carry, smoothed, elements, nodes,
    fields, lame_s, shear_s, inverse_s, resid, step_one, step_two, sums_s,
):
    for plane in range(PLANES):
        for field in range(FIELDS):
            if plane == 0 and 3 <= field < 7 or plane == PLANES - 1 and field >= 3:
                continue
            at, held = (0, field + 3) if plane == PLANES - 1 else (plane, field)
            for half in range(2):
                lanes = slice(128 * half, 128 * half + 128)
                fields[field, plane, 0:1, lanes] = jnp.zeros((1, 128), jnp.float32)
                start = (at * 4 * 2 + half) * FIELDS + held
                fields[field, plane, 1:5, lanes] = left[pl.ds(start, 4, stride=16), :]
                start = (at * 5 * 2 + half) * FIELDS + held
                fields[field, plane, 11:16, lanes] = right[pl.ds(start, 5, stride=16), :]
                start = tile_row(at, 0, half) + held
                fields[field, plane, 5:11, lanes] = planes[pl.ds(start, 6, stride=16), :]
    table = [
        [moduli[which : which + 1, kind : kind + 1] for kind in range(4)]
        for which in range(2)
    ]
    carried = None
    for plane in range(PLANES - 1):
        kind = fields[7, plane]
        picked = []
        for which in range(2):
            value = jnp.where(kind < 2.5, table[which][2], table[which][3])
            value = jnp.where(kind < 1.5, table[which][1], value)
            picked.append(jnp.where(kind < 0.5, table[which][0], value))
        lame_s[plane] = picked[0]
        shear_s[plane] = picked[1]
        weight = (picked[0] + 4.0 * picked[1]) * (16.0 / 9.0)
        weight = weight + preceding(weight, 1)
        weight = weight + preceding(weight, 0)
        if carried is not None:
            inverse_s[plane] = 1.0 / (fields[6, plane] + weight + carried)
        carried = weight
    for plane in range(6):
        elements[0, plane] = lame_s[plane]
        elements[1, plane] = shear_s[plane]
    for plane in range(5):
        nodes[0, plane] = inverse_s[plane + 1]
        nodes[1, plane] = fields[6, plane + 1]

    shift_x, shift_y, shift_z = scalars[0, 0], scalars[0, 1], scalars[0, 2]
    base = shift_x - 1

    def coefficients(plane):
        return lame_s[base + plane], shear_s[base + plane]

    def first_step(plane, forces):
        at = base + plane
        support, inverse = fields[6, at], inverse_s[at]
        for comp in range(3):
            value = forces[comp] + support * fields[comp, at]
            value = fields[3 + comp, at] - value
            resid[comp, plane] = value
            step_one[comp, plane] = inverse * value * FINE_FIRST

    def second_step(plane, forces):
        at = base + plane
        support, inverse = fields[6, at], inverse_s[at]
        for comp in range(3):
            step = step_one[comp, plane]
            value = resid[comp, plane] - (forces[comp] + support * step)
            resid[comp, plane] = value
            update = FINE_STEPS[0][0] * step + FINE_STEPS[0][1] * (inverse * value)
            step_two[comp, plane] = update
            sums_s[plane - 2, comp] = fields[comp, at] + step + update

    def last_step(plane, forces):
        support = fields[6, base + plane]
        for comp in range(3):
            value = forces[comp] + support * step_two[comp, plane]
            value = resid[comp, plane] - value
            remains[plane - 3, comp] = value
            carry[plane - 3, comp] = value[SENT]

    stencil(lambda comp, plane: fields[comp, base + plane], coefficients, 0, 8, first_step)
    stencil(lambda comp, plane: step_one[comp, plane], coefficients, 1, 7, second_step)
    stencil(lambda comp, plane: step_two[comp, plane], coefficients, 2, 6, last_step)
    for comp in range(3):
        smoothed[0, comp] = sums_s[0, comp]
        smoothed[1, comp] = sums_s[2 - shift_x, comp]
        smoothed[2, comp] = sums_s[3 - shift_x, comp]
        carry[3, comp] = sums_s[4 - shift_x, comp][SENT]

    total = [remains[0, comp] + remains[1, comp] + remains[2, comp] for comp in range(3)]
    moment = [remains[2, comp] - remains[0, comp] for comp in range(3)]
    row = lax.broadcasted_iota(jnp.int32, (ROWS, LANES), 0)
    plain = jnp.zeros((ROWS, LANES), jnp.float32)
    lever = jnp.zeros((ROWS, LANES), jnp.float32)
    for half in range(2):
        place = row - (ROW0 + 3 * half) - shift_y
        inside = (place >= 0) & (place < 3)
        arm = (place - 1).astype(jnp.float32)

        def summed(value):
            return jnp.sum(jnp.where(inside, value, 0.0), axis=0, keepdims=True)

        sums = [summed(total[comp]) for comp in range(3)]
        lines = sums + [
            summed(arm * total[2]),
            summed(-moment[2]),
            summed(moment[1] - arm * total[0]),
        ]
        for comp in range(6):
            plain = jnp.where(row == 8 * half + comp, lines[comp], plain)
        lever = jnp.where(row == 8 * half + 3, -sums[1], lever)
        lever = jnp.where(row == 8 * half + 4, sums[0], lever)
    fine = lax.broadcasted_iota(jnp.int32, (LANES, 128), 0)
    coarse = lax.broadcasted_iota(jnp.int32, (LANES, 128), 1)
    place = fine - 3 * coarse + 2 * shift_z - 10
    inside = (place >= 0) & (place < 3) & (coarse < COARSE_LANES)
    sums_z = jnp.where(inside, 1.0, 0.0)
    arms_z = jnp.where(inside, (place - 1).astype(jnp.float32), 0.0)
    result = picked_sums(plain, sums_z) + picked_sums(lever, arms_z)
    kinds = pltpu.roll(class_wide[...], shift_z + (128 - 14), 1)
    line = lax.broadcasted_iota(jnp.int32, (8, 128), 0)
    lane = lax.broadcasted_iota(jnp.int32, (8, 128), 1)
    low = jnp.where(line == 6, kinds[0:1], result[0:8])
    high = jnp.where(line == 6, kinds[1:2], result[8:16])
    packed = jnp.where(lane < 64, turned(low, -3, 1), turned(high, 61, 1))
    ends = jnp.zeros((1, 128), jnp.float32)
    lane_one = lane[0:1]
    for half in range(2):
        for comp in range(7):
            base = 6 * comp + 3 * half
            source = turned((low, high)[half][comp : comp + 1], base, 1)
            first = (lane_one >= base) & (lane_one < base + 3)
            last = (lane_one >= base + 67) & (lane_one < base + 70)
            ends = jnp.where(first | last, source, ends)
    packed = jnp.where(line == 7, ends, packed)
    for target in range(SIDE * SIDE):
        chunk[target] = packed


def coarse_kernel(
    scalars, tables, received, rest, low, smoothed, elements, nodes, displacement, correction, right,
    matrix, step_a, step_b, error, spread_y, spread_z, work, step, resid, near,
):
    shift_x, shift_y, shift_z = scalars[0, 0], scalars[0, 1], scalars[0, 2]
    mine_x, mine_y = scalars[0, 3], scalars[0, 4]
    lane = lax.broadcasted_iota(jnp.int32, (8, 128), 1)
    line = lax.broadcasted_iota(jnp.int32, (8, 128), 0)
    even = line < 4
    middle = (lane >= 3) & (lane < 67)
    odd_shift = lax.rem(shift_y, 2)
    turn_even = lax.rem(SIDE + 2 - mine_y, SIDE)
    turn_odd = lax.rem(SIDE + 6 - mine_y - odd_shift, SIDE)
    for spot in range(SPOTS):
        at_x = lax.rem(mine_x - shift_x + (SIDE - 2 + spot), SIDE)
        ends = received[at_x, pl.ds(7, 8, stride=8), :]
        ends = [pltpu.roll(ends, turn_even, 0), pltpu.roll(ends, turn_odd, 0)]
        for comp in range(7):
            main = received[at_x, pl.ds(comp, 8, stride=8), :]
            main = [pltpu.roll(main, turn_even, 0), pltpu.roll(main, turn_odd, 0)]
            parts = []
            for which in range(2):
                half = odd_shift if which == 0 else 1 - odd_shift
                base = 6 * comp + 3 * half
                value = pltpu.roll(ends[which], lax.rem(128 - base, 128), 1)
                parts.append(jnp.where(middle, pltpu.roll(main[which], 3 + 64 * half, 1), value))
            value = jnp.where(even, parts[0], parts[1])
            right[comp, spot] = jnp.where(lane < COARSE_LANES, value, 0.0)

    kinds = [right[6, spot].astype(jnp.int32) for spot in range(SPOTS)]
    for entry in range(36):
        values = jnp.broadcast_to(tables[entry : entry + 1], (8, 128))
        for spot in range(SPOTS):
            matrix[entry, spot] = jnp.take_along_axis(
                values, kinds[spot], axis=1, mode="promise_in_bounds"
            )

    def product(values, spot):
        result = []
        for i in range(6):
            total = matrix[6 * i, spot] * values[0]
            for j in range(1, 6):
                total = total + matrix[6 * i + j, spot] * values[j]
            result.append(total)
        return result

    def neighbours(source, spot, comp):
        value = source[comp, spot]
        faces = source[comp, spot + 1] + source[comp, spot - 1]
        faces = faces + turned(value, 4, 0)
        faces = faces + jnp.where(even, turned(value, -3, 0), turned(value, 3, 0))
        return faces + turned(value, 1, 1) + turned(value, -1, 1)

    for spot in range(SPOTS):
        held = [right[comp, spot] for comp in range(6)]
        fresh = product(held, spot)
        for comp in range(6):
            step_a[comp, spot] = COARSE_FIRST * fresh[comp]
    scale_old, scale_new = COARSE_STEPS[0]
    for spot in range(1, SPOTS - 1):
        held = [right[comp, spot] for comp in range(6)]
        remains = []
        for comp in range(6):
            known = COARSE_FIRST * held[comp]
            value = held[comp] - (known - neighbours(step_a, spot, comp))
            remains.append(value)
            known = scale_old * known + scale_new * value
            right[comp, spot] = value - known
        fresh = product(remains, spot)
        for comp in range(6):
            step_b[comp, spot] = scale_old * step_a[comp, spot] + scale_new * fresh[comp]
    scale_old, scale_new = COARSE_STEPS[1]
    for spot in range(2, SPOTS - 2):
        remains = [right[comp, spot] + neighbours(step_b, spot, comp) for comp in range(6)]
        fresh = product(remains, spot)
        for comp in range(6):
            old = step_b[comp, spot]
            update = scale_old * old + scale_new * fresh[comp]
            error[comp, spot] = step_a[comp, spot] + old + update

    def window_row(inner):
        return 4 * lax.rem(inner, 2) + lax.div(inner, 2)

    for half in range(2):
        inner = window_row(half + shift_y + 2)
        for comp in range(6):
            value = error[comp, shift_x + 2, pl.ds(inner, 1), :]
            value = pltpu.roll(jnp.broadcast_to(value, (8, 128)), 126 - shift_z, 1)
            correction[comp, 0, half : half + 1, :] = value[0:1, :COARSE_OWN]

    row = lax.broadcasted_iota(jnp.int32, (ROWS, 128), 0)
    for near_x in range(3):
        for comp in range(6):
            plane = error[comp, near_x + 2]
            value = jnp.zeros((ROWS, 128), jnp.float32)
            for near_y in range(4):
                at = 4 * (near_y % 2) + near_y // 2 + 1
                inner = row - ROW0 - shift_y - 3 * (near_y - shift_y)
                value = jnp.where((inner >= 0) & (inner < 3), plane[at : at + 1], value)
            start = (comp * 3 + near_x) * ROWS
            spread_y[start : start + ROWS] = value
    coarse = lax.broadcasted_iota(jnp.int32, (128, LANES), 0)
    fine = lax.broadcasted_iota(jnp.int32, (128, LANES), 1)
    inner = fine - 3 * coarse + 2 * shift_z - 10
    copies = jnp.where((inner >= 0) & (inner < 3), 1.0, 0.0)
    wide = picked_sums(spread_y[...], copies)
    for which in range(18):
        spread_z[which] = wide[which * ROWS : (which + 1) * ROWS]

    row = lax.broadcasted_iota(jnp.int32, (ROWS, LANES), 0)
    fine = lax.broadcasted_iota(jnp.int32, (ROWS, LANES), 1)
    arm_y = (lax.rem(row + 4 - shift_y, 3) - 1).astype(jnp.float32)
    arm_z = (lax.rem(fine + 2 * shift_z + 2, 3) - 1).astype(jnp.float32)
    for plane in range(7):
        ahead = plane - 2 - shift_x + 6
        near_x = lax.div(ahead, 3) - 2 + shift_x
        arm_x = (lax.rem(ahead, 3) - 1).astype(jnp.float32)
        e = [spread_z[comp * 3 + near_x] for comp in range(6)]
        work[0, plane] = e[0] + e[4] * arm_z - e[5] * arm_y
        work[1, plane] = e[1] + e[5] * arm_x - e[3] * arm_z
        work[2, plane] = e[2] + e[3] * arm_y - e[4] * arm_x

    near[...] = jnp.zeros_like(near)
    near[:, :, SENT] = low[...]
    one = (shift_x == 1).astype(jnp.float32)
    two = 1.0 - one

    def remaining(at, comp):
        if at < 2:
            return near[at + 2 - shift_x, comp]
        if at == 2:
            return one * rest[0, comp] + two * near[2, comp]
        return rest[at - 1 - shift_x, comp]

    def first_step(plane, forces):
        at = plane - 1
        for comp in range(3):
            value = forces[comp] + nodes[1, at] * work[comp, plane]
            value = remaining(at, comp) - value
            resid[comp, at] = value
            step[comp, at] = nodes[0, at] * value * FINE_FIRST

    def last_step(plane, forces):
        for comp in range(3):
            old = step[comp, plane]
            value = resid[comp, plane] - (forces[comp] + nodes[1, plane] * old)
            update = FINE_STEPS[0][0] * old + FINE_STEPS[0][1] * (nodes[0, plane] * value)
            start = smoothed[plane - 1, comp]
            if plane == 1:
                start = one * start + two * near[3, comp]
            value = start + work[comp, plane + 1] + old + update
            displacement[comp, plane - 1] = value[
                ROW0 : ROW0 + OWN_Y, LANE0 : LANE0 + OWN_Z
            ]

    stencil(
        lambda comp, plane: work[comp, plane],
        lambda plane: (elements[0, plane], elements[1, plane]),
        0,
        6,
        first_step,
    )
    stencil(
        lambda comp, plane: step[comp, plane],
        lambda plane: (elements[0, plane + 1], elements[1, plane + 1]),
        0,
        4,
        last_step,
    )


def tables_kernel(blocks, tables):
    rows = []
    for i in range(6):
        row = [blocks[6 * i + j : 6 * i + j + 1] for j in range(6)]
        row[i] = row[i] + 6.0
        one = jnp.ones_like(row[0])
        rows.append(row + [one if i == j else jnp.zeros_like(one) for j in range(6)])
    for pivot in range(6):
        scaled = [value / rows[pivot][pivot] for value in rows[pivot]]
        for i in range(6):
            factor = rows[i][pivot]
            if i != pivot:
                rows[i] = [value - factor * line for value, line in zip(rows[i], scaled)]
        rows[pivot] = scaled
    tables[36:40] = jnp.zeros_like(tables[36:40])
    for i in range(6):
        for j in range(6):
            entry = 6 * i + j
            tables[entry : entry + 1] = rows[i][6 + j]


def passed_along(value, axis, steps):
    count = lax.axis_size(axis)
    pairs = [(source, (source + steps) % count) for source in range(count)]
    return lax.ppermute(value, axis, pairs)


VMEM = pl.BlockSpec(memory_space=pltpu.VMEM)
EDGES_VMEM = 64 * 1024 * 1024 - 512 * 1024


def call(kernel, arrays, shapes, scratch=(), work=1_000_000):
    return pl.pallas_call(
        kernel,
        out_shape=[jax.ShapeDtypeStruct(shape, jnp.float32) for shape in shapes],
        in_specs=[VMEM] * len(arrays),
        out_specs=[VMEM] * len(shapes),
        scratch_shapes=[pltpu.VMEM(shape, jnp.float32) for shape in scratch],
        compiler_params=pltpu.CompilerParams(vmem_limit_bytes=48 * 1024 * 1024),
        cost_estimate=pl.CostEstimate(flops=work, bytes_accessed=work, transcendentals=0),
    )(*arrays)


def pack_edges(*arrays):
    return pl.pallas_call(
        edges_kernel,
        out_shape=[jax.ShapeDtypeStruct((OWN_X, FIELDS, 128), jnp.float32)] * 2,
        in_specs=[pl.BlockSpec(memory_space=pltpu.HBM)] * len(arrays),
        out_specs=[VMEM] * 2,
        scratch_shapes=[pltpu.VMEM(array.shape, array.dtype) for array in arrays]
        + [pltpu.SemaphoreType.DMA((len(arrays),))],
        compiler_params=pltpu.CompilerParams(vmem_limit_bytes=EDGES_VMEM),
    )(*arrays)


def pack(*arrays):
    shapes = [(OWN_X * OWN_Y * 2 * FIELDS, 128), (8, 128)]
    return call(pack_kernel, arrays, shapes, work=20_000_000)


def widen(block, low, high, class_ext):
    shapes = [(OWN_X * OWN_Y * 2 * FIELDS, 128), (8, 128), (2 * OWN_Y * 2 * FIELDS, 128)]
    return call(widen_kernel, (block, low, high, class_ext), shapes)


def pre_smooth(moduli, scalars, planes, left, right, class_wide):
    plane = (ROWS, LANES)
    return call(
        pre_kernel,
        (moduli, scalars, planes, left, right, class_wide),
        [(SIDE * SIDE, 8, 128), (3, 3) + plane, (4, 3, 8, LANES), (3, 3) + plane]
        + [(2, 6) + plane, (2, 5) + plane],
        [(FIELDS, PLANES) + plane] + [(PLANES,) + plane] * 3
        + [(3, 9) + plane, (3, 9) + plane, (3, 9) + plane, (5, 3) + plane],
    )


def coarse_and_post(scalars, tables, received, rest, low, smoothed, elements, nodes):
    plane = (ROWS, LANES)
    spots = (SPOTS, 8, 128)
    return call(
        coarse_kernel,
        (scalars, tables, received, rest, low, smoothed, elements, nodes),
        [(3, OWN_X, OWN_Y, OWN_Z), (6, 1, 2, COARSE_OWN)],
        [(7,) + spots, (36,) + spots, (6,) + spots, (6,) + spots, (6,) + spots]
        + [(18 * ROWS, 128), (18,) + plane, (3, 7) + plane, (3, 5) + plane, (3, 5) + plane]
        + [(4, 3) + plane],
    )


def coarse_tables(class_blocks):
    entries = jnp.transpose(class_blocks.reshape(8, 36))
    entries = jnp.pad(entries, ((0, 4), (0, 120)))
    return call(tables_kernel, (entries,), [(40, 128)])[0]


def body(forcing, initial_guess, material, moduli, support, offsets, aggregate_class, class_blocks):
    tables = coarse_tables(class_blocks)
    place = jnp.stack([lax.axis_index("gx"), lax.axis_index("gy")]).astype(jnp.int32)
    scalars = jnp.concatenate([offsets, place]).reshape(1, 5)
    arrays = (initial_guess, forcing, support, material, aggregate_class)
    low, high = pack_edges(*arrays)
    from_low = passed_along(high, "gz", 1)
    from_high = passed_along(low, "gz", -1)
    block, class_ext = pack(*arrays)
    own, class_wide, beyond = widen(block, from_low, from_high, class_ext)
    own = own.reshape(OWN_X, OWN_Y, 2 * FIELDS, 128)
    before = passed_along(own[1:], "gx", 1)
    after = passed_along(own, "gx", -1)
    beyond = passed_along(beyond.reshape(2, OWN_Y, 2 * FIELDS, 128), "gx", -2)
    before, after = lax.optimization_barrier((before, after))
    field = lax.broadcasted_iota(jnp.int32, (OWN_Y, 2 * FIELDS, 128), 1) % FIELDS
    beyond = jnp.where(((field >= 3) & (field < 6))[None] | (jnp.arange(2) == 0)[:, None, None, None], beyond, 0.0)
    beyond = lax.optimization_barrier(beyond)
    mixed = jnp.where((field >= 3) & (field < 6), beyond[1], before[0])
    planes = jnp.concatenate([mixed[None], before[1:], own, after, beyond[:1]], axis=0)
    left = passed_along(planes[:, 2:], "gy", 1).reshape(-1, 128)
    right = passed_along(planes[:, :5], "gy", -1).reshape(-1, 128)
    chunk, rest, carry, smoothed, elements, nodes = pre_smooth(
        moduli * (1.0 / 16.0), scalars, planes.reshape(-1, 128), left, right, class_wide
    )
    received = lax.all_to_all(chunk, ("gx", "gy"), 0, 0, tiled=True)
    received = received.reshape(SIDE, SIDE * 8, 128)
    from_before = passed_along(carry, "gx", 1)
    displacement, correction = coarse_and_post(
        scalars, tables, received, rest, from_before, smoothed, elements, nodes
    )
    return displacement, correction


def solution(mesh):
    placed = (
        P(None, "gx", "gy", "gz"),
        P(None, "gx", "gy", "gz"),
        P("gx", "gy", "gz"),
        P(),
        P("gx", "gy", "gz"),
        P(),
        P("gx", "gy", "gz"),
        P(),
    )
    return jax.shard_map(
        body,
        mesh=mesh,
        in_specs=placed,
        out_specs=(P(None, "gx", "gy", "gz"), P(None, "gx", "gy", "gz")),
        check_vma=False,
    )
```

```python
import jax
import jax.numpy as jnp
from jax import lax
from jax.experimental import pallas as pl
from jax.experimental.pallas import tpu as pltpu
from jax.sharding import PartitionSpec as P

FINE_LOW = 0.25
FINE_HIGH = 2.5
COARSE_LOW = 0.2
COARSE_HIGH = 1.9

ROWS = 16
LANES = 256
ROW0 = 8
LANE0 = 16
EDGE = 16
SENT = slice(7, 15)
PLANES = 10
OWN_X, OWN_Y, OWN_Z = 3, 6, 192
FIELDS = 8
SIDE = 8
SPOTS = 7
COARSE_OWN = 64
COARSE_LANES = 70


def chebyshev(low, high, count):
    center = 0.5 * (high + low)
    spread = 0.5 * (high - low)
    ratio = center / spread
    weight = 1.0 / ratio
    steps = []
    for _ in range(1, count):
        following = 1.0 / (2.0 * ratio - weight)
        steps.append((following * weight, 2.0 * following / spread))
        weight = following
    return 1.0 / center, steps


FINE_FIRST, FINE_STEPS = chebyshev(FINE_LOW, FINE_HIGH, 2)
COARSE_FIRST, COARSE_STEPS = chebyshev(COARSE_LOW, COARSE_HIGH, 3)


def turned(value, shift, axis):
    shift = shift % value.shape[axis]
    return value if shift == 0 else pltpu.roll(value, shift, axis)


def following(value, axis):
    return turned(value, -1, axis)


def preceding(value, axis):
    return turned(value, 1, axis)


def plane_modes(value):
    ahead = following(value, 1)
    total, slope = value + ahead, ahead - value
    total_up, slope_up = following(total, 0), following(slope, 0)
    return {
        (0, 0): total + total_up,
        (1, 0): total_up - total,
        (0, 1): slope + slope_up,
        (1, 1): slope_up - slope,
    }


def element_modes(below, above, lame, shear):
    u = []
    for comp in range(3):
        modes = {}
        for key in ((0, 0), (1, 0), (0, 1), (1, 1)):
            first, second = below[comp][key], above[comp][key]
            if key != (0, 0):
                modes[(0,) + key] = first + second
            modes[(1,) + key] = second - first
        u.append(modes)
    x, y, z = u
    third = 1.0 / 3.0
    lame_b, shear_b = lame * third, shear * third
    shear_2 = shear + shear
    last = (lame + (shear_2 + shear_2)) * (1.0 / 9.0)
    f = [{}, {}, {}]
    divergence = lame * (x[1, 0, 0] + y[0, 1, 0] + z[0, 0, 1])
    f[0][1, 0, 0] = divergence + shear_2 * x[1, 0, 0]
    f[1][0, 1, 0] = divergence + shear_2 * y[0, 1, 0]
    f[2][0, 0, 1] = divergence + shear_2 * z[0, 0, 1]
    f[0][0, 1, 0] = f[1][1, 0, 0] = shear * (x[0, 1, 0] + y[1, 0, 0])
    f[0][0, 0, 1] = f[2][1, 0, 0] = shear * (x[0, 0, 1] + z[1, 0, 0])
    f[1][0, 0, 1] = f[2][0, 1, 0] = shear * (y[0, 0, 1] + z[0, 1, 0])
    for one, key_one, two, key_two in (
        (0, (1, 1, 0), 2, (0, 1, 1)),
        (0, (1, 0, 1), 1, (0, 1, 1)),
        (1, (1, 1, 0), 2, (1, 0, 1)),
    ):
        shared = lame_b * (u[one][key_one] + u[two][key_two])
        f[one][key_one] = shared + shear * u[one][key_one]
        f[two][key_two] = shared + shear * u[two][key_two]
    mixed = x[0, 1, 1] + y[1, 0, 1] + z[1, 1, 0]
    f[0][0, 1, 1] = shear_b * (mixed + x[0, 1, 1])
    f[1][1, 0, 1] = shear_b * (mixed + y[1, 0, 1])
    f[2][1, 1, 0] = shear_b * (mixed + z[1, 1, 0])
    for comp in range(3):
        f[comp][1, 1, 1] = last * u[comp][1, 1, 1]
    low, high = [], []
    for comp in range(3):
        down, up = {}, {}
        for key in ((0, 0), (1, 0), (0, 1), (1, 1)):
            slope = f[comp][(1,) + key]
            if key == (0, 0):
                down[key], up[key] = -slope, slope
            else:
                total = f[comp][(0,) + key]
                down[key], up[key] = total - slope, total + slope
        low.append(down)
        high.append(up)
    return low, high


def plane_forces(modes):
    parts = []
    for last in (0, 1):
        total, slope = modes[0, last], modes[1, last]
        parts.append((total - slope) + preceding(total + slope, 0))
    return (parts[0] - parts[1]) + preceding(parts[0] + parts[1], 1)


def stencil(read, elements, first, last, emit):
    below = [plane_modes(read(comp, first)) for comp in range(3)]
    carried = None
    for plane in range(first, last):
        above = [plane_modes(read(comp, plane + 1)) for comp in range(3)]
        low, high = element_modes(below, above, *elements(plane))
        if carried is not None:
            emit(
                plane,
                [
                    plane_forces({key: low[comp][key] + carried[comp][key] for key in low[comp]})
                    for comp in range(3)
                ],
            )
        below, carried = above, high


def picked_sums(values, weights):
    high = values.astype(jnp.bfloat16)
    left = values - high.astype(jnp.float32)
    middle = left.astype(jnp.bfloat16)
    low = (left - middle.astype(jnp.float32)).astype(jnp.bfloat16)
    weights = weights.astype(jnp.bfloat16)
    parts = [
        jnp.dot(part, weights, preferred_element_type=jnp.float32) for part in (low, middle, high)
    ]
    return (parts[0] + parts[1]) + parts[2]


def tile_row(plane, row, half):
    return ((plane * OWN_Y + row) * 2 + half) * FIELDS


def field_planes(guess, forcing, support, material, plane):
    for comp in range(3):
        yield comp, guess[comp, plane]
        yield 3 + comp, forcing[comp, plane]
    yield 6, support[plane]
    yield 7, material[plane].astype(jnp.float32)


def edges_kernel(
    guess_h, forcing_h, support_h, material_h, classes_h, low, high, guess, forcing, support, material,
    classes, done,
):
    pairs = (
        (guess_h, guess),
        (forcing_h, forcing),
        (support_h, support),
        (material_h, material),
        (classes_h, classes),
    )
    copies = [
        pltpu.make_async_copy(source, target, done.at[which])
        for which, (source, target) in enumerate(pairs)
    ]
    for copy in copies:
        copy.start()
    low[...] = jnp.zeros_like(low)
    high[...] = jnp.zeros_like(high)
    for copy in copies:
        copy.wait()
    kinds = classes[0].astype(jnp.float32)
    low[0, 0:2, 96:112] = kinds[:, 0:EDGE]
    high[0, 0:2, 96:112] = kinds[:, COARSE_OWN - EDGE :]
    for plane in range(OWN_X):
        for field, value in field_planes(guess, forcing, support, material, plane):
            for row in range(OWN_Y):
                line = value[row : row + 1]
                low[plane, field : field + 1, EDGE * row : EDGE * (row + 1)] = line[:, :EDGE]
                high[plane, field : field + 1, EDGE * row : EDGE * (row + 1)] = line[:, -EDGE:]


def pack_kernel(guess, forcing, support, material, classes, block, class_ext):
    first = 128 - LANE0
    block[...] = jnp.zeros_like(block)
    class_ext[...] = jnp.zeros_like(class_ext)
    class_ext[0:2, LANE0 : LANE0 + COARSE_OWN] = classes[0].astype(jnp.float32)
    for plane in range(OWN_X):
        for field, value in field_planes(guess, forcing, support, material, plane):
            for row in range(OWN_Y):
                line = value[row : row + 1]
                start = tile_row(plane, row, 0) + field
                block[start : start + 1, LANE0:128] = line[:, :first]
                start = tile_row(plane, row, 1) + field
                block[start : start + 1, 0 : OWN_Z - first] = line[:, first:]


def widen_kernel(block, low, high, class_ext, wide, class_wide, beyond):
    lane = lax.broadcasted_iota(jnp.int32, (8, 128), 1)
    end = LANE0 + OWN_Z - 128
    for plane in range(OWN_X):
        for row in range(OWN_Y):
            start = tile_row(plane, row, 0)
            wide[start : start + 8] = jnp.where(
                lane < LANE0, turned(low[plane], -EDGE * row, 1), block[start : start + 8]
            )
            start = tile_row(plane, row, 1)
            wide[start : start + 8] = jnp.where(
                (lane >= end) & (lane < end + EDGE),
                turned(high[plane], end - EDGE * row, 1),
                block[start : start + 8],
            )
    for row in range(OWN_Y):
        for half in range(2):
            start = tile_row(0, row, half)
            beyond[start : start + 8] = wide[start : start + 8]
            start = tile_row(1, row, half)
            beyond[start : start + 8] = turned(wide[start : start + 8], 3, 0)
    end = LANE0 + COARSE_OWN
    value = jnp.where(lane < LANE0, turned(low[0], -96, 1), class_ext[...])
    class_wide[...] = jnp.where(
        (lane >= end) & (lane < end + EDGE), turned(high[0], end - 96, 1), value
    )


def pre_kernel(
    moduli, scalars, planes, left, right, class_wide, chunk, remains, carry, smoothed, elements, nodes,
    fields, lame_s, shear_s, inverse_s, resid, step_one, step_two, sums_s,
):
    for plane in range(PLANES):
        for field in range(FIELDS):
            if plane == 0 and 3 <= field < 7 or plane == PLANES - 1 and field >= 3:
                continue
            at, held = (0, field + 3) if plane == PLANES - 1 else (plane, field)
            for half in range(2):
                lanes = slice(128 * half, 128 * half + 128)
                fields[field, plane, 3:4, lanes] = jnp.zeros((1, 128), jnp.float32)
                start = (at * 4 * 2 + half) * FIELDS + held
                fields[field, plane, 4:8, lanes] = left[pl.ds(start, 4, stride=16), :]
                start = (at * 5 * 2 + half) * FIELDS + held
                fields[field, plane, 14:16, lanes] = right[pl.ds(start, 2, stride=16), :]
                fields[field, plane, 0:3, lanes] = right[pl.ds(start + 32, 3, stride=16), :]
                start = tile_row(at, 0, half) + held
                fields[field, plane, 8:14, lanes] = planes[pl.ds(start, 6, stride=16), :]
    table = [
        [moduli[which : which + 1, kind : kind + 1] for kind in range(4)]
        for which in range(2)
    ]
    carried = None
    for plane in range(PLANES - 1):
        kind = fields[7, plane]
        picked = []
        for which in range(2):
            value = jnp.where(kind < 2.5, table[which][2], table[which][3])
            value = jnp.where(kind < 1.5, table[which][1], value)
            picked.append(jnp.where(kind < 0.5, table[which][0], value))
        lame_s[plane] = picked[0]
        shear_s[plane] = picked[1]
        weight = (picked[0] + 4.0 * picked[1]) * (16.0 / 9.0)
        weight = weight + preceding(weight, 1)
        weight = weight + preceding(weight, 0)
        if carried is not None:
            inverse_s[plane] = 1.0 / (fields[6, plane] + weight + carried)
        carried = weight
    for plane in range(6):
        elements[0, plane] = lame_s[plane]
        elements[1, plane] = shear_s[plane]
    for plane in range(5):
        nodes[0, plane] = inverse_s[plane + 1]
        nodes[1, plane] = fields[6, plane + 1]

    shift_x, shift_y, shift_z = scalars[0, 0], scalars[0, 1], scalars[0, 2]
    base = shift_x - 1

    def coefficients(plane):
        return lame_s[base + plane], shear_s[base + plane]

    def first_step(plane, forces):
        at = base + plane
        support, inverse = fields[6, at], inverse_s[at]
        for comp in range(3):
            value = forces[comp] + support * fields[comp, at]
            value = fields[3 + comp, at] - value
            resid[comp, plane] = value
            step_one[comp, plane] = inverse * value * FINE_FIRST

    def second_step(plane, forces):
        at = base + plane
        support, inverse = fields[6, at], inverse_s[at]
        for comp in range(3):
            step = step_one[comp, plane]
            value = resid[comp, plane] - (forces[comp] + support * step)
            resid[comp, plane] = value
            update = FINE_STEPS[0][0] * step + FINE_STEPS[0][1] * (inverse * value)
            step_two[comp, plane] = update
            sums_s[plane - 2, comp] = fields[comp, at] + step + update

    def last_step(plane, forces):
        support = fields[6, base + plane]
        for comp in range(3):
            value = forces[comp] + support * step_two[comp, plane]
            value = resid[comp, plane] - value
            remains[plane - 3, comp] = value
            carry[plane - 3, comp] = value[SENT]

    stencil(lambda comp, plane: fields[comp, base + plane], coefficients, 0, 8, first_step)
    stencil(lambda comp, plane: step_one[comp, plane], coefficients, 1, 7, second_step)
    stencil(lambda comp, plane: step_two[comp, plane], coefficients, 2, 6, last_step)
    for comp in range(3):
        smoothed[0, comp] = sums_s[0, comp]
        smoothed[1, comp] = sums_s[2 - shift_x, comp]
        smoothed[2, comp] = sums_s[3 - shift_x, comp]
        carry[3, comp] = sums_s[4 - shift_x, comp][SENT]

    total = [remains[0, comp] + remains[1, comp] + remains[2, comp] for comp in range(3)]
    moment = [remains[2, comp] - remains[0, comp] for comp in range(3)]
    row = lax.broadcasted_iota(jnp.int32, (ROWS, LANES), 0)
    plain = jnp.zeros((ROWS, LANES), jnp.float32)
    lever = jnp.zeros((ROWS, LANES), jnp.float32)
    for half in range(2):
        place = row - (ROW0 + 3 * half) - shift_y
        inside = (place >= 0) & (place < 3)
        arm = (place - 1).astype(jnp.float32)

        def summed(value):
            return jnp.sum(jnp.where(inside, value, 0.0), axis=0, keepdims=True)

        sums = [summed(total[comp]) for comp in range(3)]
        lines = sums + [
            summed(arm * total[2]),
            summed(-moment[2]),
            summed(moment[1] - arm * total[0]),
        ]
        for comp in range(6):
            plain = jnp.where(row == 8 * half + comp, lines[comp], plain)
        lever = jnp.where(row == 8 * half + 3, -sums[1], lever)
        lever = jnp.where(row == 8 * half + 4, sums[0], lever)
    fine = lax.broadcasted_iota(jnp.int32, (LANES, 128), 0)
    coarse = lax.broadcasted_iota(jnp.int32, (LANES, 128), 1)
    place = fine - 3 * coarse + 2 * shift_z - 10
    inside = (place >= 0) & (place < 3) & (coarse < COARSE_LANES)
    sums_z = jnp.where(inside, 1.0, 0.0)
    arms_z = jnp.where(inside, (place - 1).astype(jnp.float32), 0.0)
    result = picked_sums(plain, sums_z) + picked_sums(lever, arms_z)
    kinds = pltpu.roll(class_wide[...], shift_z + (128 - 14), 1)
    line = lax.broadcasted_iota(jnp.int32, (8, 128), 0)
    lane = lax.broadcasted_iota(jnp.int32, (8, 128), 1)
    low = jnp.where(line == 6, kinds[0:1], result[0:8])
    high = jnp.where(line == 6, kinds[1:2], result[8:16])
    packed = jnp.where(lane < 64, turned(low, -3, 1), turned(high, 61, 1))
    ends = jnp.zeros((1, 128), jnp.float32)
    lane_one = lane[0:1]
    for half in range(2):
        for comp in range(7):
            base = 6 * comp + 3 * half
            source = turned((low, high)[half][comp : comp + 1], base, 1)
            first = (lane_one >= base) & (lane_one < base + 3)
            last = (lane_one >= base + 67) & (lane_one < base + 70)
            ends = jnp.where(first | last, source, ends)
    packed = jnp.where(line == 7, ends, packed)
    for target in range(SIDE * SIDE):
        chunk[target] = packed


def coarse_kernel(
    scalars, tables, received, rest, low, smoothed, elements, nodes, displacement, correction, right,
    matrix, step_a, step_b, error, spread_y, spread_z, work, step, resid, near,
):
    shift_x, shift_y, shift_z = scalars[0, 0], scalars[0, 1], scalars[0, 2]
    mine_x, mine_y = scalars[0, 3], scalars[0, 4]
    lane = lax.broadcasted_iota(jnp.int32, (8, 128), 1)
    line = lax.broadcasted_iota(jnp.int32, (8, 128), 0)
    even = line < 4
    middle = (lane >= 3) & (lane < 67)
    odd_shift = lax.rem(shift_y, 2)
    turn_even = lax.rem(SIDE + 2 - mine_y, SIDE)
    turn_odd = lax.rem(SIDE + 6 - mine_y - odd_shift, SIDE)
    for spot in range(SPOTS):
        at_x = lax.rem(mine_x - shift_x + (SIDE - 2 + spot), SIDE)
        ends = received[at_x, pl.ds(7, 8, stride=8), :]
        ends = [pltpu.roll(ends, turn_even, 0), pltpu.roll(ends, turn_odd, 0)]
        for comp in range(7):
            main = received[at_x, pl.ds(comp, 8, stride=8), :]
            main = [pltpu.roll(main, turn_even, 0), pltpu.roll(main, turn_odd, 0)]
            parts = []
            for which in range(2):
                half = odd_shift if which == 0 else 1 - odd_shift
                base = 6 * comp + 3 * half
                value = pltpu.roll(ends[which], lax.rem(128 - base, 128), 1)
                parts.append(jnp.where(middle, pltpu.roll(main[which], 3 + 64 * half, 1), value))
            value = jnp.where(even, parts[0], parts[1])
            right[comp, spot] = jnp.where(lane < COARSE_LANES, value, 0.0)

    kinds = [right[6, spot].astype(jnp.int32) for spot in range(SPOTS)]
    for entry in range(36):
        values = jnp.broadcast_to(tables[entry : entry + 1], (8, 128))
        for spot in range(SPOTS):
            matrix[entry, spot] = jnp.take_along_axis(
                values, kinds[spot], axis=1, mode="promise_in_bounds"
            )

    def product(values, spot):
        result = []
        for i in range(6):
            total = matrix[6 * i, spot] * values[0]
            for j in range(1, 6):
                total = total + matrix[6 * i + j, spot] * values[j]
            result.append(total)
        return result

    def neighbours(source, spot, comp):
        value = source[comp, spot]
        faces = source[comp, spot + 1] + source[comp, spot - 1]
        faces = faces + turned(value, 4, 0)
        faces = faces + jnp.where(even, turned(value, -3, 0), turned(value, 3, 0))
        return faces + turned(value, 1, 1) + turned(value, -1, 1)

    for spot in range(SPOTS):
        held = [right[comp, spot] for comp in range(6)]
        fresh = product(held, spot)
        for comp in range(6):
            step_a[comp, spot] = COARSE_FIRST * fresh[comp]
    scale_old, scale_new = COARSE_STEPS[0]
    for spot in range(1, SPOTS - 1):
        held = [right[comp, spot] for comp in range(6)]
        remains = []
        for comp in range(6):
            known = COARSE_FIRST * held[comp]
            value = held[comp] - (known - neighbours(step_a, spot, comp))
            remains.append(value)
            known = scale_old * known + scale_new * value
            right[comp, spot] = value - known
        fresh = product(remains, spot)
        for comp in range(6):
            step_b[comp, spot] = scale_old * step_a[comp, spot] + scale_new * fresh[comp]
    scale_old, scale_new = COARSE_STEPS[1]
    for spot in range(2, SPOTS - 2):
        remains = [right[comp, spot] + neighbours(step_b, spot, comp) for comp in range(6)]
        fresh = product(remains, spot)
        for comp in range(6):
            old = step_b[comp, spot]
            update = scale_old * old + scale_new * fresh[comp]
            error[comp, spot] = step_a[comp, spot] + old + update

    def window_row(inner):
        return 4 * lax.rem(inner, 2) + lax.div(inner, 2)

    for half in range(2):
        inner = window_row(half + shift_y + 2)
        for comp in range(6):
            value = error[comp, shift_x + 2, pl.ds(inner, 1), :]
            value = pltpu.roll(jnp.broadcast_to(value, (8, 128)), 126 - shift_z, 1)
            correction[comp, 0, half : half + 1, :] = value[0:1, :COARSE_OWN]

    row = lax.broadcasted_iota(jnp.int32, (ROWS, 128), 0)
    for near_x in range(3):
        for comp in range(6):
            plane = error[comp, near_x + 2]
            value = jnp.zeros((ROWS, 128), jnp.float32)
            for near_y in range(4):
                at = 4 * (near_y % 2) + near_y // 2 + 1
                inner = row - ROW0 - shift_y - 3 * (near_y - shift_y)
                value = jnp.where((inner >= 0) & (inner < 3), plane[at : at + 1], value)
            start = (comp * 3 + near_x) * ROWS
            spread_y[start : start + ROWS] = value
    coarse = lax.broadcasted_iota(jnp.int32, (128, LANES), 0)
    fine = lax.broadcasted_iota(jnp.int32, (128, LANES), 1)
    inner = fine - 3 * coarse + 2 * shift_z - 10
    copies = jnp.where((inner >= 0) & (inner < 3), 1.0, 0.0)
    wide = picked_sums(spread_y[...], copies)
    for which in range(18):
        spread_z[which] = wide[which * ROWS : (which + 1) * ROWS]

    row = lax.broadcasted_iota(jnp.int32, (ROWS, LANES), 0)
    fine = lax.broadcasted_iota(jnp.int32, (ROWS, LANES), 1)
    arm_y = (lax.rem(row + 4 - shift_y, 3) - 1).astype(jnp.float32)
    arm_z = (lax.rem(fine + 2 * shift_z + 2, 3) - 1).astype(jnp.float32)
    for plane in range(7):
        ahead = plane - 2 - shift_x + 6
        near_x = lax.div(ahead, 3) - 2 + shift_x
        arm_x = (lax.rem(ahead, 3) - 1).astype(jnp.float32)
        e = [spread_z[comp * 3 + near_x] for comp in range(6)]
        work[0, plane] = e[0] + e[4] * arm_z - e[5] * arm_y
        work[1, plane] = e[1] + e[5] * arm_x - e[3] * arm_z
        work[2, plane] = e[2] + e[3] * arm_y - e[4] * arm_x

    near[...] = jnp.zeros_like(near)
    near[:, :, SENT] = low[...]
    one = (shift_x == 1).astype(jnp.float32)
    two = 1.0 - one

    def remaining(at, comp):
        if at < 2:
            return near[at + 2 - shift_x, comp]
        if at == 2:
            return one * rest[0, comp] + two * near[2, comp]
        return rest[at - 1 - shift_x, comp]

    def first_step(plane, forces):
        at = plane - 1
        for comp in range(3):
            value = forces[comp] + nodes[1, at] * work[comp, plane]
            value = remaining(at, comp) - value
            resid[comp, at] = value
            step[comp, at] = nodes[0, at] * value * FINE_FIRST

    def last_step(plane, forces):
        for comp in range(3):
            old = step[comp, plane]
            value = resid[comp, plane] - (forces[comp] + nodes[1, plane] * old)
            update = FINE_STEPS[0][0] * old + FINE_STEPS[0][1] * (nodes[0, plane] * value)
            start = smoothed[plane - 1, comp]
            if plane == 1:
                start = one * start + two * near[3, comp]
            value = start + work[comp, plane + 1] + old + update
            displacement[comp, plane - 1] = value[
                ROW0 : ROW0 + OWN_Y, LANE0 : LANE0 + OWN_Z
            ]

    stencil(
        lambda comp, plane: work[comp, plane],
        lambda plane: (elements[0, plane], elements[1, plane]),
        0,
        6,
        first_step,
    )
    stencil(
        lambda comp, plane: step[comp, plane],
        lambda plane: (elements[0, plane + 1], elements[1, plane + 1]),
        0,
        4,
        last_step,
    )


def tables_kernel(blocks, tables):
    rows = []
    for i in range(6):
        row = [blocks[6 * i + j : 6 * i + j + 1] for j in range(6)]
        row[i] = row[i] + 6.0
        one = jnp.ones_like(row[0])
        rows.append(row + [one if i == j else jnp.zeros_like(one) for j in range(6)])
    for pivot in range(6):
        scaled = [value / rows[pivot][pivot] for value in rows[pivot]]
        for i in range(6):
            factor = rows[i][pivot]
            if i != pivot:
                rows[i] = [value - factor * line for value, line in zip(rows[i], scaled)]
        rows[pivot] = scaled
    tables[36:40] = jnp.zeros_like(tables[36:40])
    for i in range(6):
        for j in range(6):
            entry = 6 * i + j
            tables[entry : entry + 1] = rows[i][6 + j]


def passed_along(value, axis, steps):
    count = lax.axis_size(axis)
    pairs = [(source, (source + steps) % count) for source in range(count)]
    return lax.ppermute(value, axis, pairs)


VMEM = pl.BlockSpec(memory_space=pltpu.VMEM)
EDGES_VMEM = 64 * 1024 * 1024 - 512 * 1024


def call(kernel, arrays, shapes, scratch=(), work=1_000_000):
    return pl.pallas_call(
        kernel,
        out_shape=[jax.ShapeDtypeStruct(shape, jnp.float32) for shape in shapes],
        in_specs=[VMEM] * len(arrays),
        out_specs=[VMEM] * len(shapes),
        scratch_shapes=[pltpu.VMEM(shape, jnp.float32) for shape in scratch],
        compiler_params=pltpu.CompilerParams(vmem_limit_bytes=48 * 1024 * 1024),
        cost_estimate=pl.CostEstimate(flops=work, bytes_accessed=work, transcendentals=0),
    )(*arrays)


def pack_edges(*arrays):
    return pl.pallas_call(
        edges_kernel,
        out_shape=[jax.ShapeDtypeStruct((OWN_X, FIELDS, 128), jnp.float32)] * 2,
        in_specs=[pl.BlockSpec(memory_space=pltpu.HBM)] * len(arrays),
        out_specs=[VMEM] * 2,
        scratch_shapes=[pltpu.VMEM(array.shape, array.dtype) for array in arrays]
        + [pltpu.SemaphoreType.DMA((len(arrays),))],
        compiler_params=pltpu.CompilerParams(vmem_limit_bytes=EDGES_VMEM),
    )(*arrays)


def pack(*arrays):
    shapes = [(OWN_X * OWN_Y * 2 * FIELDS, 128), (8, 128)]
    return call(pack_kernel, arrays, shapes, work=20_000_000)


def widen(block, low, high, class_ext):
    shapes = [(OWN_X * OWN_Y * 2 * FIELDS, 128), (8, 128), (2 * OWN_Y * 2 * FIELDS, 128)]
    return call(widen_kernel, (block, low, high, class_ext), shapes)


def pre_smooth(moduli, scalars, planes, left, right, class_wide):
    plane = (ROWS, LANES)
    return call(
        pre_kernel,
        (moduli, scalars, planes, left, right, class_wide),
        [(SIDE * SIDE, 8, 128), (3, 3) + plane, (4, 3, 8, LANES), (3, 3) + plane]
        + [(2, 6) + plane, (2, 5) + plane],
        [(FIELDS, PLANES) + plane] + [(PLANES,) + plane] * 3
        + [(3, 9) + plane, (3, 9) + plane, (3, 9) + plane, (5, 3) + plane],
    )


def coarse_and_post(scalars, tables, received, rest, low, smoothed, elements, nodes):
    plane = (ROWS, LANES)
    spots = (SPOTS, 8, 128)
    return call(
        coarse_kernel,
        (scalars, tables, received, rest, low, smoothed, elements, nodes),
        [(3, OWN_X, OWN_Y, OWN_Z), (6, 1, 2, COARSE_OWN)],
        [(7,) + spots, (36,) + spots, (6,) + spots, (6,) + spots, (6,) + spots]
        + [(18 * ROWS, 128), (18,) + plane, (3, 7) + plane, (3, 5) + plane, (3, 5) + plane]
        + [(4, 3) + plane],
    )


def coarse_tables(class_blocks):
    entries = jnp.transpose(class_blocks.reshape(8, 36))
    entries = jnp.pad(entries, ((0, 4), (0, 120)))
    return call(tables_kernel, (entries,), [(40, 128)])[0]


def body(forcing, initial_guess, material, moduli, support, offsets, aggregate_class, class_blocks):
    tables = coarse_tables(class_blocks)
    place = jnp.stack([lax.axis_index("gx"), lax.axis_index("gy")]).astype(jnp.int32)
    scalars = jnp.concatenate([offsets, place]).reshape(1, 5)
    arrays = (initial_guess, forcing, support, material, aggregate_class)
    low, high = pack_edges(*arrays)
    from_low = passed_along(high, "gz", 1)
    from_high = passed_along(low, "gz", -1)
    block, class_ext = pack(*arrays)
    own, class_wide, beyond = widen(block, from_low, from_high, class_ext)
    own = own.reshape(OWN_X, OWN_Y, 2 * FIELDS, 128)
    before = passed_along(own[1:], "gx", 1)
    after = passed_along(own, "gx", -1)
    beyond = passed_along(beyond.reshape(2, OWN_Y, 2 * FIELDS, 128), "gx", -2)
    before, after = lax.optimization_barrier((before, after))
    field = lax.broadcasted_iota(jnp.int32, (OWN_Y, 2 * FIELDS, 128), 1) % FIELDS
    beyond = jnp.where(((field >= 3) & (field < 6))[None] | (jnp.arange(2) == 0)[:, None, None, None], beyond, 0.0)
    beyond = lax.optimization_barrier(beyond)
    mixed = jnp.where((field >= 3) & (field < 6), beyond[1], before[0])
    planes = jnp.concatenate([mixed[None], before[1:], own, after, beyond[:1]], axis=0)
    left = passed_along(planes[:, 2:], "gy", 1).reshape(-1, 128)
    right = passed_along(planes[:, :5], "gy", -1).reshape(-1, 128)
    chunk, rest, carry, smoothed, elements, nodes = pre_smooth(
        moduli * (1.0 / 16.0), scalars, planes.reshape(-1, 128), left, right, class_wide
    )
    received = lax.all_to_all(chunk, ("gx", "gy"), 0, 0, tiled=True)
    received = received.reshape(SIDE, SIDE * 8, 128)
    from_before = passed_along(carry, "gx", 1)
    displacement, correction = coarse_and_post(
        scalars, tables, received, rest, from_before, smoothed, elements, nodes
    )
    return displacement, correction


def solution(mesh):
    placed = (
        P(None, "gx", "gy", "gz"),
        P(None, "gx", "gy", "gz"),
        P("gx", "gy", "gz"),
        P(),
        P("gx", "gy", "gz"),
        P(),
        P("gx", "gy", "gz"),
        P(),
    )
    return jax.shard_map(
        body,
        mesh=mesh,
        in_specs=placed,
        out_specs=(P(None, "gx", "gy", "gz"), P(None, "gx", "gy", "gz")),
        check_vma=False,
    )
```

```python
import jax
import jax.numpy as jnp
from jax import lax
from jax.experimental import pallas as pl
from jax.experimental.pallas import tpu as pltpu
from jax.sharding import PartitionSpec as P

FINE_LOW = 0.25
FINE_HIGH = 2.5
COARSE_LOW = 0.2
COARSE_HIGH = 1.9

ROWS = 16
LANES = 256
ROW0 = 8
LANE0 = 16
EDGE = 16
SENT = slice(7, 15)
PLANES = 10
OWN_X, OWN_Y, OWN_Z = 3, 6, 192
FIELDS = 8
SIDE = 8
SPOTS = 7
COARSE_OWN = 64
COARSE_LANES = 70


def chebyshev(low, high, count):
    center = 0.5 * (high + low)
    spread = 0.5 * (high - low)
    ratio = center / spread
    weight = 1.0 / ratio
    steps = []
    for _ in range(1, count):
        following = 1.0 / (2.0 * ratio - weight)
        steps.append((following * weight, 2.0 * following / spread))
        weight = following
    return 1.0 / center, steps


FINE_FIRST, FINE_STEPS = chebyshev(FINE_LOW, FINE_HIGH, 2)
COARSE_FIRST, COARSE_STEPS = chebyshev(COARSE_LOW, COARSE_HIGH, 3)


def turned(value, shift, axis):
    shift = shift % value.shape[axis]
    return value if shift == 0 else pltpu.roll(value, shift, axis)


def following(value, axis):
    return turned(value, -1, axis)


def preceding(value, axis):
    return turned(value, 1, axis)


def plane_modes(value):
    ahead = following(value, 1)
    total, slope = value + ahead, ahead - value
    total_up, slope_up = following(total, 0), following(slope, 0)
    return {
        (0, 0): total + total_up,
        (1, 0): total_up - total,
        (0, 1): slope + slope_up,
        (1, 1): slope_up - slope,
    }


def element_modes(below, above, lame, shear):
    u = []
    for comp in range(3):
        modes = {}
        for key in ((0, 0), (1, 0), (0, 1), (1, 1)):
            first, second = below[comp][key], above[comp][key]
            if key != (0, 0):
                modes[(0,) + key] = first + second
            modes[(1,) + key] = second - first
        u.append(modes)
    x, y, z = u
    third = 1.0 / 3.0
    lame_b, shear_b = lame * third, shear * third
    shear_2 = shear + shear
    last = (lame + (shear_2 + shear_2)) * (1.0 / 9.0)
    f = [{}, {}, {}]
    divergence = lame * (x[1, 0, 0] + y[0, 1, 0] + z[0, 0, 1])
    f[0][1, 0, 0] = divergence + shear_2 * x[1, 0, 0]
    f[1][0, 1, 0] = divergence + shear_2 * y[0, 1, 0]
    f[2][0, 0, 1] = divergence + shear_2 * z[0, 0, 1]
    f[0][0, 1, 0] = f[1][1, 0, 0] = shear * (x[0, 1, 0] + y[1, 0, 0])
    f[0][0, 0, 1] = f[2][1, 0, 0] = shear * (x[0, 0, 1] + z[1, 0, 0])
    f[1][0, 0, 1] = f[2][0, 1, 0] = shear * (y[0, 0, 1] + z[0, 1, 0])
    for one, key_one, two, key_two in (
        (0, (1, 1, 0), 2, (0, 1, 1)),
        (0, (1, 0, 1), 1, (0, 1, 1)),
        (1, (1, 1, 0), 2, (1, 0, 1)),
    ):
        shared = lame_b * (u[one][key_one] + u[two][key_two])
        f[one][key_one] = shared + shear * u[one][key_one]
        f[two][key_two] = shared + shear * u[two][key_two]
    mixed = x[0, 1, 1] + y[1, 0, 1] + z[1, 1, 0]
    f[0][0, 1, 1] = shear_b * (mixed + x[0, 1, 1])
    f[1][1, 0, 1] = shear_b * (mixed + y[1, 0, 1])
    f[2][1, 1, 0] = shear_b * (mixed + z[1, 1, 0])
    for comp in range(3):
        f[comp][1, 1, 1] = last * u[comp][1, 1, 1]
    low, high = [], []
    for comp in range(3):
        down, up = {}, {}
        for key in ((0, 0), (1, 0), (0, 1), (1, 1)):
            slope = f[comp][(1,) + key]
            if key == (0, 0):
                down[key], up[key] = -slope, slope
            else:
                total = f[comp][(0,) + key]
                down[key], up[key] = total - slope, total + slope
        low.append(down)
        high.append(up)
    return low, high


def plane_forces(modes):
    parts = []
    for last in (0, 1):
        total, slope = modes[0, last], modes[1, last]
        parts.append((total - slope) + preceding(total + slope, 0))
    return (parts[0] - parts[1]) + preceding(parts[0] + parts[1], 1)


def stencil(read, elements, first, last, emit):
    below = [plane_modes(read(comp, first)) for comp in range(3)]
    carried = None
    for plane in range(first, last):
        above = [plane_modes(read(comp, plane + 1)) for comp in range(3)]
        low, high = element_modes(below, above, *elements(plane))
        if carried is not None:
            emit(
                plane,
                [
                    plane_forces({key: low[comp][key] + carried[comp][key] for key in low[comp]})
                    for comp in range(3)
                ],
            )
        below, carried = above, high


def picked_sums(values, weights):
    high = values.astype(jnp.bfloat16)
    left = values - high.astype(jnp.float32)
    middle = left.astype(jnp.bfloat16)
    low = (left - middle.astype(jnp.float32)).astype(jnp.bfloat16)
    weights = weights.astype(jnp.bfloat16)
    parts = [
        jnp.dot(part, weights, preferred_element_type=jnp.float32) for part in (low, middle, high)
    ]
    return (parts[0] + parts[1]) + parts[2]


def tile_row(plane, row, half):
    return ((plane * OWN_Y + row) * 2 + half) * FIELDS


def field_planes(guess, forcing, support, material, plane):
    for comp in range(3):
        yield comp, guess[comp, plane]
        yield 3 + comp, forcing[comp, plane]
    yield 6, support[plane]
    yield 7, material[plane].astype(jnp.float32)


def edges_kernel(
    guess_h, forcing_h, support_h, material_h, classes_h, low, high, guess, forcing, support, material,
    classes, done,
):
    pairs = (
        (guess_h, guess),
        (forcing_h, forcing),
        (support_h, support),
        (material_h, material),
        (classes_h, classes),
    )
    copies = [
        pltpu.make_async_copy(source, target, done.at[which])
        for which, (source, target) in enumerate(pairs)
    ]
    for copy in copies:
        copy.start()
    low[...] = jnp.zeros_like(low)
    high[...] = jnp.zeros_like(high)
    for copy in copies:
        copy.wait()
    kinds = classes[0].astype(jnp.float32)
    low[0, 0:2, 96:112] = kinds[:, 0:EDGE]
    high[0, 0:2, 96:112] = kinds[:, COARSE_OWN - EDGE :]
    for plane in range(OWN_X):
        for field, value in field_planes(guess, forcing, support, material, plane):
            for row in range(OWN_Y):
                line = value[row : row + 1]
                low[plane, field : field + 1, EDGE * row : EDGE * (row + 1)] = line[:, :EDGE]
                high[plane, field : field + 1, EDGE * row : EDGE * (row + 1)] = line[:, -EDGE:]


def pack_kernel(guess, forcing, support, material, classes, block, class_ext):
    first = 128 - LANE0
    block[...] = jnp.zeros_like(block)
    class_ext[...] = jnp.zeros_like(class_ext)
    class_ext[0:2, LANE0 : LANE0 + COARSE_OWN] = classes[0].astype(jnp.float32)
    for plane in range(OWN_X):
        for field, value in field_planes(guess, forcing, support, material, plane):
            for row in range(OWN_Y):
                line = value[row : row + 1]
                start = tile_row(plane, row, 0) + field
                block[start : start + 1, LANE0:128] = line[:, :first]
                start = tile_row(plane, row, 1) + field
                block[start : start + 1, 0 : OWN_Z - first] = line[:, first:]


def widen_kernel(block, low, high, class_ext, wide, class_wide, beyond):
    lane = lax.broadcasted_iota(jnp.int32, (8, 128), 1)
    end = LANE0 + OWN_Z - 128
    for plane in range(OWN_X):
        for row in range(OWN_Y):
            start = tile_row(plane, row, 0)
            wide[start : start + 8] = jnp.where(
                lane < LANE0, turned(low[plane], -EDGE * row, 1), block[start : start + 8]
            )
            start = tile_row(plane, row, 1)
            wide[start : start + 8] = jnp.where(
                (lane >= end) & (lane < end + EDGE),
                turned(high[plane], end - EDGE * row, 1),
                block[start : start + 8],
            )
    for row in range(OWN_Y):
        for half in range(2):
            start = tile_row(0, row, half)
            beyond[start : start + 8] = wide[start : start + 8]
            start = tile_row(1, row, half)
            beyond[start : start + 8] = turned(wide[start : start + 8], 3, 0)
    end = LANE0 + COARSE_OWN
    value = jnp.where(lane < LANE0, turned(low[0], -96, 1), class_ext[...])
    class_wide[...] = jnp.where(
        (lane >= end) & (lane < end + EDGE), turned(high[0], end - 96, 1), value
    )


def pre_kernel(
    moduli, scalars, planes, left, right, class_wide, chunk, remains, carry, smoothed, elements, nodes,
    fields, lame_s, shear_s, inverse_s, resid, step_one, step_two, sums_s,
):
    for plane in range(PLANES):
        for field in range(FIELDS):
            if plane == 0 and 3 <= field < 7 or plane == PLANES - 1 and field >= 3:
                continue
            at, held = (0, field + 3) if plane == PLANES - 1 else (plane, field)
            for half in range(2):
                lanes = slice(128 * half, 128 * half + 128)
                fields[field, plane, 3:4, lanes] = jnp.zeros((1, 128), jnp.float32)
                start = (at * 4 * 2 + half) * FIELDS + held
                fields[field, plane, 4:8, lanes] = left[pl.ds(start, 4, stride=16), :]
                start = (at * 5 * 2 + half) * FIELDS + held
                fields[field, plane, 14:16, lanes] = right[pl.ds(start, 2, stride=16), :]
                fields[field, plane, 0:3, lanes] = right[pl.ds(start + 32, 3, stride=16), :]
                start = tile_row(at, 0, half) + held
                fields[field, plane, 8:14, lanes] = planes[pl.ds(start, 6, stride=16), :]
    table = [
        [moduli[which : which + 1, kind : kind + 1] for kind in range(4)]
        for which in range(2)
    ]
    carried = None
    for plane in range(PLANES - 1):
        kind = fields[7, plane]
        picked = []
        for which in range(2):
            value = jnp.where(kind < 2.5, table[which][2], table[which][3])
            value = jnp.where(kind < 1.5, table[which][1], value)
            picked.append(jnp.where(kind < 0.5, table[which][0], value))
        lame_s[plane] = picked[0]
        shear_s[plane] = picked[1]
        weight = (picked[0] + 4.0 * picked[1]) * (16.0 / 9.0)
        weight = weight + preceding(weight, 1)
        weight = weight + preceding(weight, 0)
        if carried is not None:
            inverse_s[plane] = 1.0 / (fields[6, plane] + weight + carried)
        carried = weight
    for plane in range(6):
        elements[0, plane] = lame_s[plane]
        elements[1, plane] = shear_s[plane]
    for plane in range(5):
        nodes[0, plane] = inverse_s[plane + 1]
        nodes[1, plane] = fields[6, plane + 1]

    shift_x, shift_y, shift_z = scalars[0, 0], scalars[0, 1], scalars[0, 2]
    base = shift_x - 1

    def coefficients(plane):
        return lame_s[base + plane], shear_s[base + plane]

    def first_step(plane, forces):
        at = base + plane
        support, inverse = fields[6, at], inverse_s[at]
        for comp in range(3):
            value = forces[comp] + support * fields[comp, at]
            value = fields[3 + comp, at] - value
            resid[comp, plane] = value
            step_one[comp, plane] = inverse * value * FINE_FIRST

    def second_step(plane, forces):
        at = base + plane
        support, inverse = fields[6, at], inverse_s[at]
        for comp in range(3):
            step = step_one[comp, plane]
            value = resid[comp, plane] - (forces[comp] + support * step)
            resid[comp, plane] = value
            update = FINE_STEPS[0][0] * step + FINE_STEPS[0][1] * (inverse * value)
            step_two[comp, plane] = update
            sums_s[plane - 2, comp] = fields[comp, at] + step + update

    def last_step(plane, forces):
        support = fields[6, base + plane]
        for comp in range(3):
            value = forces[comp] + support * step_two[comp, plane]
            value = resid[comp, plane] - value
            remains[plane - 3, comp] = value
            carry[plane - 3, comp] = value[SENT]

    stencil(lambda comp, plane: fields[comp, base + plane], coefficients, 0, 8, first_step)
    stencil(lambda comp, plane: step_one[comp, plane], coefficients, 1, 7, second_step)
    stencil(lambda comp, plane: step_two[comp, plane], coefficients, 2, 6, last_step)
    for comp in range(3):
        smoothed[0, comp] = sums_s[0, comp]
        smoothed[1, comp] = sums_s[2 - shift_x, comp]
        smoothed[2, comp] = sums_s[3 - shift_x, comp]
        carry[3, comp] = sums_s[4 - shift_x, comp][SENT]

    total = [remains[0, comp] + remains[1, comp] + remains[2, comp] for comp in range(3)]
    moment = [remains[2, comp] - remains[0, comp] for comp in range(3)]
    row = lax.broadcasted_iota(jnp.int32, (ROWS, LANES), 0)
    plain = jnp.zeros((ROWS, LANES), jnp.float32)
    lever = jnp.zeros((ROWS, LANES), jnp.float32)
    for half in range(2):
        place = row - (ROW0 + 3 * half) - shift_y
        inside = (place >= 0) & (place < 3)
        arm = (place - 1).astype(jnp.float32)

        def summed(value):
            return jnp.sum(jnp.where(inside, value, 0.0), axis=0, keepdims=True)

        sums = [summed(total[comp]) for comp in range(3)]
        lines = sums + [
            summed(arm * total[2]),
            summed(-moment[2]),
            summed(moment[1] - arm * total[0]),
        ]
        for comp in range(6):
            plain = jnp.where(row == 8 * half + comp, lines[comp], plain)
        lever = jnp.where(row == 8 * half + 3, -sums[1], lever)
        lever = jnp.where(row == 8 * half + 4, sums[0], lever)
    fine = lax.broadcasted_iota(jnp.int32, (LANES, 128), 0)
    coarse = lax.broadcasted_iota(jnp.int32, (LANES, 128), 1)
    place = fine - 3 * coarse + 2 * shift_z - 10
    inside = (place >= 0) & (place < 3) & (coarse < COARSE_LANES)
    sums_z = jnp.where(inside, 1.0, 0.0)
    arms_z = jnp.where(inside, (place - 1).astype(jnp.float32), 0.0)
    result = picked_sums(
        jnp.concatenate([plain, lever], axis=1), jnp.concatenate([sums_z, arms_z], axis=0)
    )
    kinds = pltpu.roll(class_wide[...], shift_z + (128 - 14), 1)
    line = lax.broadcasted_iota(jnp.int32, (8, 128), 0)
    lane = lax.broadcasted_iota(jnp.int32, (8, 128), 1)
    low = jnp.where(line == 6, kinds[0:1], result[0:8])
    high = jnp.where(line == 6, kinds[1:2], result[8:16])
    packed = jnp.where(lane < 64, turned(low, -3, 1), turned(high, 61, 1))
    ends = jnp.zeros((1, 128), jnp.float32)
    lane_one = lane[0:1]
    for half in range(2):
        for comp in range(7):
            base = 6 * comp + 3 * half
            source = turned((low, high)[half][comp : comp + 1], base, 1)
            first = (lane_one >= base) & (lane_one < base + 3)
            last = (lane_one >= base + 67) & (lane_one < base + 70)
            ends = jnp.where(first | last, source, ends)
    packed = jnp.where(line == 7, ends, packed)
    for target in range(SIDE * SIDE):
        chunk[target] = packed


def coarse_kernel(
    scalars, tables, received, rest, low, smoothed, elements, nodes, displacement, correction, right,
    matrix, step_a, step_b, error, spread_y, spread_z, work, step, resid, near,
):
    shift_x, shift_y, shift_z = scalars[0, 0], scalars[0, 1], scalars[0, 2]
    mine_x, mine_y = scalars[0, 3], scalars[0, 4]
    lane = lax.broadcasted_iota(jnp.int32, (8, 128), 1)
    line = lax.broadcasted_iota(jnp.int32, (8, 128), 0)
    even = line < 4
    middle = (lane >= 3) & (lane < 67)
    odd_shift = lax.rem(shift_y, 2)
    turn_even = lax.rem(SIDE + 2 - mine_y, SIDE)
    turn_odd = lax.rem(SIDE + 6 - mine_y - odd_shift, SIDE)
    for spot in range(SPOTS):
        at_x = lax.rem(mine_x - shift_x + (SIDE - 2 + spot), SIDE)
        ends = received[at_x, pl.ds(7, 8, stride=8), :]
        ends = [pltpu.roll(ends, turn_even, 0), pltpu.roll(ends, turn_odd, 0)]
        for comp in range(7):
            main = received[at_x, pl.ds(comp, 8, stride=8), :]
            main = [pltpu.roll(main, turn_even, 0), pltpu.roll(main, turn_odd, 0)]
            parts = []
            for which in range(2):
                half = odd_shift if which == 0 else 1 - odd_shift
                base = 6 * comp + 3 * half
                value = pltpu.roll(ends[which], lax.rem(128 - base, 128), 1)
                parts.append(jnp.where(middle, pltpu.roll(main[which], 3 + 64 * half, 1), value))
            value = jnp.where(even, parts[0], parts[1])
            right[comp, spot] = jnp.where(lane < COARSE_LANES, value, 0.0)

    kinds = [right[6, spot].astype(jnp.int32) for spot in range(SPOTS)]
    for entry in range(36):
        values = jnp.broadcast_to(tables[entry : entry + 1], (8, 128))
        for spot in range(SPOTS):
            matrix[entry, spot] = jnp.take_along_axis(
                values, kinds[spot], axis=1, mode="promise_in_bounds"
            )

    def product(values, spot):
        result = []
        for i in range(6):
            total = matrix[6 * i, spot] * values[0]
            for j in range(1, 6):
                total = total + matrix[6 * i + j, spot] * values[j]
            result.append(total)
        return result

    def neighbours(source, spot, comp):
        value = source[comp, spot]
        faces = source[comp, spot + 1] + source[comp, spot - 1]
        faces = faces + turned(value, 4, 0)
        faces = faces + jnp.where(even, turned(value, -3, 0), turned(value, 3, 0))
        return faces + turned(value, 1, 1) + turned(value, -1, 1)

    for spot in range(SPOTS):
        held = [right[comp, spot] for comp in range(6)]
        fresh = product(held, spot)
        for comp in range(6):
            step_a[comp, spot] = COARSE_FIRST * fresh[comp]
    scale_old, scale_new = COARSE_STEPS[0]
    for spot in range(1, SPOTS - 1):
        held = [right[comp, spot] for comp in range(6)]
        remains = []
        for comp in range(6):
            known = COARSE_FIRST * held[comp]
            value = held[comp] - (known - neighbours(step_a, spot, comp))
            remains.append(value)
            known = scale_old * known + scale_new * value
            right[comp, spot] = value - known
        fresh = product(remains, spot)
        for comp in range(6):
            step_b[comp, spot] = scale_old * step_a[comp, spot] + scale_new * fresh[comp]
    scale_old, scale_new = COARSE_STEPS[1]
    for spot in range(2, SPOTS - 2):
        remains = [right[comp, spot] + neighbours(step_b, spot, comp) for comp in range(6)]
        fresh = product(remains, spot)
        for comp in range(6):
            old = step_b[comp, spot]
            update = scale_old * old + scale_new * fresh[comp]
            error[comp, spot] = step_a[comp, spot] + old + update

    def window_row(inner):
        return 4 * lax.rem(inner, 2) + lax.div(inner, 2)

    for half in range(2):
        inner = window_row(half + shift_y + 2)
        for comp in range(6):
            value = error[comp, shift_x + 2, pl.ds(inner, 1), :]
            value = pltpu.roll(jnp.broadcast_to(value, (8, 128)), 126 - shift_z, 1)
            correction[comp, 0, half : half + 1, :] = value[0:1, :COARSE_OWN]

    row = lax.broadcasted_iota(jnp.int32, (ROWS, 128), 0)
    for near_x in range(3):
        for comp in range(6):
            plane = error[comp, near_x + 2]
            value = jnp.zeros((ROWS, 128), jnp.float32)
            for near_y in range(4):
                at = 4 * (near_y % 2) + near_y // 2 + 1
                inner = row - ROW0 - shift_y - 3 * (near_y - shift_y)
                value = jnp.where((inner >= 0) & (inner < 3), plane[at : at + 1], value)
            start = (comp * 3 + near_x) * ROWS
            spread_y[start : start + ROWS] = value
    coarse = lax.broadcasted_iota(jnp.int32, (128, LANES), 0)
    fine = lax.broadcasted_iota(jnp.int32, (128, LANES), 1)
    inner = fine - 3 * coarse + 2 * shift_z - 10
    copies = jnp.where((inner >= 0) & (inner < 3), 1.0, 0.0)
    wide = picked_sums(spread_y[...], copies)
    for which in range(18):
        spread_z[which] = wide[which * ROWS : (which + 1) * ROWS]

    row = lax.broadcasted_iota(jnp.int32, (ROWS, LANES), 0)
    fine = lax.broadcasted_iota(jnp.int32, (ROWS, LANES), 1)
    arm_y = (lax.rem(row + 4 - shift_y, 3) - 1).astype(jnp.float32)
    arm_z = (lax.rem(fine + 2 * shift_z + 2, 3) - 1).astype(jnp.float32)
    for plane in range(7):
        ahead = plane - 2 - shift_x + 6
        near_x = lax.div(ahead, 3) - 2 + shift_x
        arm_x = (lax.rem(ahead, 3) - 1).astype(jnp.float32)
        e = [spread_z[comp * 3 + near_x] for comp in range(6)]
        work[0, plane] = e[0] + e[4] * arm_z - e[5] * arm_y
        work[1, plane] = e[1] + e[5] * arm_x - e[3] * arm_z
        work[2, plane] = e[2] + e[3] * arm_y - e[4] * arm_x

    near[...] = jnp.zeros_like(near)
    near[:, :, SENT] = low[...]
    one = (shift_x == 1).astype(jnp.float32)
    two = 1.0 - one

    def remaining(at, comp):
        if at < 2:
            return near[at + 2 - shift_x, comp]
        if at == 2:
            return one * rest[0, comp] + two * near[2, comp]
        return rest[at - 1 - shift_x, comp]

    def first_step(plane, forces):
        at = plane - 1
        for comp in range(3):
            value = forces[comp] + nodes[1, at] * work[comp, plane]
            value = remaining(at, comp) - value
            resid[comp, at] = value
            step[comp, at] = nodes[0, at] * value * FINE_FIRST

    def last_step(plane, forces):
        for comp in range(3):
            old = step[comp, plane]
            value = resid[comp, plane] - (forces[comp] + nodes[1, plane] * old)
            update = FINE_STEPS[0][0] * old + FINE_STEPS[0][1] * (nodes[0, plane] * value)
            start = smoothed[plane - 1, comp]
            if plane == 1:
                start = one * start + two * near[3, comp]
            value = start + work[comp, plane + 1] + old + update
            displacement[comp, plane - 1] = value[
                ROW0 : ROW0 + OWN_Y, LANE0 : LANE0 + OWN_Z
            ]

    stencil(
        lambda comp, plane: work[comp, plane],
        lambda plane: (elements[0, plane], elements[1, plane]),
        0,
        6,
        first_step,
    )
    stencil(
        lambda comp, plane: step[comp, plane],
        lambda plane: (elements[0, plane + 1], elements[1, plane + 1]),
        0,
        4,
        last_step,
    )


def tables_kernel(blocks, tables):
    rows = []
    for i in range(6):
        row = [blocks[6 * i + j : 6 * i + j + 1] for j in range(6)]
        row[i] = row[i] + 6.0
        one = jnp.ones_like(row[0])
        rows.append(row + [one if i == j else jnp.zeros_like(one) for j in range(6)])
    for pivot in range(6):
        scaled = [value / rows[pivot][pivot] for value in rows[pivot]]
        for i in range(6):
            factor = rows[i][pivot]
            if i != pivot:
                rows[i] = [value - factor * line for value, line in zip(rows[i], scaled)]
        rows[pivot] = scaled
    tables[36:40] = jnp.zeros_like(tables[36:40])
    for i in range(6):
        for j in range(6):
            entry = 6 * i + j
            tables[entry : entry + 1] = rows[i][6 + j]


def passed_along(value, axis, steps):
    count = lax.axis_size(axis)
    pairs = [(source, (source + steps) % count) for source in range(count)]
    return lax.ppermute(value, axis, pairs)


VMEM = pl.BlockSpec(memory_space=pltpu.VMEM)
EDGES_VMEM = 64 * 1024 * 1024 - 512 * 1024


def call(kernel, arrays, shapes, scratch=(), work=1_000_000):
    return pl.pallas_call(
        kernel,
        out_shape=[jax.ShapeDtypeStruct(shape, jnp.float32) for shape in shapes],
        in_specs=[VMEM] * len(arrays),
        out_specs=[VMEM] * len(shapes),
        scratch_shapes=[pltpu.VMEM(shape, jnp.float32) for shape in scratch],
        compiler_params=pltpu.CompilerParams(vmem_limit_bytes=48 * 1024 * 1024),
        cost_estimate=pl.CostEstimate(flops=work, bytes_accessed=work, transcendentals=0),
    )(*arrays)


def pack_edges(*arrays):
    return pl.pallas_call(
        edges_kernel,
        out_shape=[jax.ShapeDtypeStruct((OWN_X, FIELDS, 128), jnp.float32)] * 2,
        in_specs=[pl.BlockSpec(memory_space=pltpu.HBM)] * len(arrays),
        out_specs=[VMEM] * 2,
        scratch_shapes=[pltpu.VMEM(array.shape, array.dtype) for array in arrays]
        + [pltpu.SemaphoreType.DMA((len(arrays),))],
        compiler_params=pltpu.CompilerParams(vmem_limit_bytes=EDGES_VMEM),
    )(*arrays)


def pack(*arrays):
    shapes = [(OWN_X * OWN_Y * 2 * FIELDS, 128), (8, 128)]
    return call(pack_kernel, arrays, shapes, work=20_000_000)


def widen(block, low, high, class_ext):
    shapes = [(OWN_X * OWN_Y * 2 * FIELDS, 128), (8, 128), (2 * OWN_Y * 2 * FIELDS, 128)]
    return call(widen_kernel, (block, low, high, class_ext), shapes)


def pre_smooth(moduli, scalars, planes, left, right, class_wide):
    plane = (ROWS, LANES)
    return call(
        pre_kernel,
        (moduli, scalars, planes, left, right, class_wide),
        [(SIDE * SIDE, 8, 128), (3, 3) + plane, (4, 3, 8, LANES), (3, 3) + plane]
        + [(2, 6) + plane, (2, 5) + plane],
        [(FIELDS, PLANES) + plane] + [(PLANES,) + plane] * 3
        + [(3, 9) + plane, (3, 9) + plane, (3, 9) + plane, (5, 3) + plane],
    )


def coarse_and_post(scalars, tables, received, rest, low, smoothed, elements, nodes):
    plane = (ROWS, LANES)
    spots = (SPOTS, 8, 128)
    return call(
        coarse_kernel,
        (scalars, tables, received, rest, low, smoothed, elements, nodes),
        [(3, OWN_X, OWN_Y, OWN_Z), (6, 1, 2, COARSE_OWN)],
        [(7,) + spots, (36,) + spots, (6,) + spots, (6,) + spots, (6,) + spots]
        + [(18 * ROWS, 128), (18,) + plane, (3, 7) + plane, (3, 5) + plane, (3, 5) + plane]
        + [(4, 3) + plane],
    )


def coarse_tables(class_blocks):
    entries = jnp.transpose(class_blocks.reshape(8, 36))
    entries = jnp.pad(entries, ((0, 4), (0, 120)))
    return call(tables_kernel, (entries,), [(40, 128)])[0]


def body(forcing, initial_guess, material, moduli, support, offsets, aggregate_class, class_blocks):
    tables = coarse_tables(class_blocks)
    place = jnp.stack([lax.axis_index("gx"), lax.axis_index("gy")]).astype(jnp.int32)
    scalars = jnp.concatenate([offsets, place]).reshape(1, 5)
    arrays = (initial_guess, forcing, support, material, aggregate_class)
    low, high = pack_edges(*arrays)
    from_low = passed_along(high, "gz", 1)
    from_high = passed_along(low, "gz", -1)
    block, class_ext = pack(*arrays)
    own, class_wide, beyond = widen(block, from_low, from_high, class_ext)
    own = own.reshape(OWN_X, OWN_Y, 2 * FIELDS, 128)
    before = passed_along(own[1:], "gx", 1)
    after = passed_along(own, "gx", -1)
    beyond = passed_along(beyond.reshape(2, OWN_Y, 2 * FIELDS, 128), "gx", -2)
    before, after = lax.optimization_barrier((before, after))
    field = lax.broadcasted_iota(jnp.int32, (OWN_Y, 2 * FIELDS, 128), 1) % FIELDS
    beyond = jnp.where(((field >= 3) & (field < 6))[None] | (jnp.arange(2) == 0)[:, None, None, None], beyond, 0.0)
    beyond = lax.optimization_barrier(beyond)
    mixed = jnp.where((field >= 3) & (field < 6), beyond[1], before[0])
    planes = jnp.concatenate([mixed[None], before[1:], own, after, beyond[:1]], axis=0)
    left = passed_along(planes[:, 2:], "gy", 1).reshape(-1, 128)
    right = passed_along(planes[:, :5], "gy", -1).reshape(-1, 128)
    chunk, rest, carry, smoothed, elements, nodes = pre_smooth(
        moduli * (1.0 / 16.0), scalars, planes.reshape(-1, 128), left, right, class_wide
    )
    received = lax.all_to_all(chunk, ("gx", "gy"), 0, 0, tiled=True)
    received = received.reshape(SIDE, SIDE * 8, 128)
    from_before = passed_along(carry, "gx", 1)
    displacement, correction = coarse_and_post(
        scalars, tables, received, rest, from_before, smoothed, elements, nodes
    )
    return displacement, correction


def solution(mesh):
    placed = (
        P(None, "gx", "gy", "gz"),
        P(None, "gx", "gy", "gz"),
        P("gx", "gy", "gz"),
        P(),
        P("gx", "gy", "gz"),
        P(),
        P("gx", "gy", "gz"),
        P(),
    )
    return jax.shard_map(
        body,
        mesh=mesh,
        in_specs=placed,
        out_specs=(P(None, "gx", "gy", "gz"), P(None, "gx", "gy", "gz")),
        check_vma=False,
    )
```
